128 devices in a mesh: morton: 32 (over y, x, core), chan: 4 (over z).
Axes of the slice: x: 4, y: 4, z: 4, core: 2. Of those that a mesh axis runs over, the one named last changes fastest.
Arguments:
- features: bfloat16 [256, 65536], P('chan', 'morton'), may hold values from -6 to 6
- conv_weight: bfloat16 [27, 256, 256], P(None, 'chan'), may hold values from -0.078125 to 0.078125
- coarse_weight: bfloat16 [256, 256], P('chan'), may hold values from -0.375 to 0.375
- out_grad: bfloat16 [256, 65536], P('chan', 'morton'), may hold values from -6 to 6
- send_block: int32 [32, 32], P('morton'), may hold values from 0 to 15
- send_count: int32 [32, 32], P('morton'), may hold values from 0 to 1, as said below
- neighbour: int32 [27, 512], P(None, 'morton'), may hold values from -1 to 47, as said below
Outputs:
- output: bfloat16 [256, 65536], P('chan', 'morton')
- input_grad: float32 [256, 65536], P('chan', 'morton')
- conv_grad: float32 [27, 256, 256], P(None, 'chan')
- coarse_grad: float32 [256, 256], P('chan')
The draws below stay inside these ranges and needn't reach their ends.
Inputs may be any that keep to these rules, and one draw needn't show every extreme that they name: send_count[s, d] is 0 where d = s, 1 where d = s - 1 or s + 1, else 0 or 1. neighbour[13, g] = g % 16 (the block itself). A value 16 + s in a column of owner m appears only where send_count[s, m] = 1, and every such pair (s, m) appears in some column of owner m.
All inputs are finite; a program needn't handle non-finite values.
Results may differ from the reference program's by a relative error of at most 0.0065.
Values may be sent and summed in bfloat16 or wider, within the bound.
No kernel may reach another device: no remote copies, remote signals or barrier semaphores. Data moves between devices by JAX's collectives and lax.ppermute only.
A program may use at most 128 MiB of HBM per device.

```python
import jax
import jax.numpy as jnp
from jax import lax

C = 256
NB = 16
OFFSETS = 27
VOXELS = 65536
N_MORTON = 32


def live_links(key):
    first = jax.random.fold_in(key, 101)
    second = jax.random.fold_in(key, 102)
    coin = jax.random.randint(first, (N_MORTON, N_MORTON), 0, 5)
    level = jax.random.randint(second, (1, N_MORTON), 1, 6)
    senders = jnp.arange(N_MORTON)[:, None]
    targets = jnp.arange(N_MORTON)[None, :]
    linked = (coin < level) | (jnp.abs(senders - targets) == 1)
    linked = linked & (senders != targets)
    return linked.astype(jnp.int32)


def draw_send_count(key, part):
    linked = live_links(key)
    return linked.astype(jnp.int32)


def draw_neighbour(key, part):
    linked = live_links(key)
    key = jax.random.fold_in(key, 5)
    keys = jax.random.split(key, 3)
    total = N_MORTON * NB
    owner = jnp.arange(total) // NB
    kind = jax.random.randint(keys[0], (OFFSETS, total), 0, 20)
    local_pick = jax.random.randint(keys[1], (OFFSETS, total), 0, NB)
    sender_pick = jax.random.randint(keys[2], (OFFSETS, total), 0, N_MORTON)
    usable = linked[sender_pick, jnp.broadcast_to(owner[None, :], (OFFSETS, total))] == 1
    entry = jnp.where(kind < 3, -1, jnp.where((kind >= 12) & usable, NB + sender_pick, local_pick))
    entry = entry.at[13].set(jnp.arange(total) % NB)
    senders = jnp.broadcast_to(jnp.arange(N_MORTON)[:, None], (N_MORTON, N_MORTON))
    owners = jnp.broadcast_to(jnp.arange(N_MORTON)[None, :], (N_MORTON, N_MORTON))
    row_index = senders % 13
    col_index = owners * NB + senders // 13
    forced = jnp.where(linked == 1, NB + senders, entry[row_index, col_index])
    entry = entry.at[row_index, col_index].set(forced)
    return entry.astype(jnp.int32)


def touch_ends(values, own_key, low, high):
    index_at = [jax.random.randint(jax.random.fold_in(own_key, axis), (), 0, length) for axis, length in enumerate(values.shape)]
    widest = values.shape.index(max(values.shape))
    beside = index_at[:widest] + [(index_at[widest] + 1) % values.shape[widest]] + index_at[widest + 1:]
    return values.at[tuple(index_at)].set(low).at[tuple(beside)].set(high)


def block_levels(rng, extent, pieces, smallest, top_value):
    loudness = 1.0
    for position, blocks in pieces:
        steps = jax.random.uniform(jax.random.fold_in(jax.random.fold_in(rng, 6), position), (blocks,), jnp.float32, smallest / len(pieces), top_value / len(pieces))
        loudness = loudness * jnp.repeat(jnp.exp(steps), extent[position] // blocks).reshape((-1,) + (1,) * (len(extent) - 1 - position))
    return loudness


def bell_draw(stream_key, shape, scale, reach, cuts=(), held_as=jnp.bfloat16):
    entries = scale * jax.random.normal(stream_key, shape, jnp.float32)
    if cuts:
        entries = entries * block_levels(stream_key, shape, cuts, -0.22, 0.18)
    return jnp.clip(entries, -reach, reach).astype(held_as)


def setup_inputs(seed: int = 0) -> dict:
    seeds = jax.random.split(jax.random.key(seed), 8)
    features = bell_draw(seeds[0], (C, VOXELS), 1.0, 6.0, ((0, 4), (1, 32)))
    conv_weight = bell_draw(seeds[1], (OFFSETS, C, C), (OFFSETS * C) ** -0.5, 0.078125, ((1, 4),))
    coarse_weight = bell_draw(seeds[2], (C, C), C ** -0.5, 0.375, ((0, 4),))
    out_grad = bell_draw(seeds[3], (C, VOXELS), 1.0, 6.0, ((0, 4), (1, 32)))
    send_block = touch_ends(jax.random.randint(seeds[4], (N_MORTON, N_MORTON), 0, NB), jax.random.fold_in(seeds[4], 1), 0, NB - 1).astype(jnp.int32)
    send_count = draw_send_count(jax.random.fold_in(seeds[7], 71), 0)
    neighbour = draw_neighbour(jax.random.fold_in(seeds[7], 71), 0)
    return dict(features=features, conv_weight=conv_weight, coarse_weight=coarse_weight, out_grad=out_grad, send_block=send_block, send_count=send_count, neighbour=neighbour)


def source_blocks(neighbour, send_block, send_count):
    block_ids = jnp.arange(N_MORTON * NB, dtype=jnp.int32)
    owner = jnp.broadcast_to(block_ids // NB, neighbour.shape)
    sender = jnp.clip(neighbour - NB, 0, N_MORTON - 1)
    local_source = owner * NB + jnp.clip(neighbour, 0, NB - 1)
    halo_source = sender * NB + send_block[sender, owner]
    source = jnp.where(neighbour >= NB, halo_source, local_source)
    keep_flag = jnp.where(neighbour < 0, 0, jnp.where(neighbour >= NB, send_count[sender, owner], 1))
    return source.astype(jnp.int32), keep_flag.astype(jnp.int32)


def reference(features, conv_weight, coarse_weight, out_grad, send_block, send_count, neighbour):
    channels, voxels = features.shape
    nblocks = voxels // 128
    source, keep_flag = source_blocks(neighbour, send_block, send_count)
    grid = features.reshape(channels, nblocks, 128)

    def gather_offset(offset):
        picked = jnp.take(grid, source[offset], axis=1)
        factor = keep_flag[offset].astype(features.dtype)[None, :, None]
        return (picked * factor).reshape(channels, voxels)

    def forward_step(offset, total):
        return total + jnp.dot(conv_weight[offset], gather_offset(offset), preferred_element_type=jnp.float32)

    conv_out = lax.fori_loop(0, OFFSETS, forward_step, jnp.zeros((channels, voxels), jnp.float32))
    pooled = jnp.mean(features.astype(jnp.float32).reshape(channels, voxels // 8, 8), axis=2).astype(jnp.bfloat16)
    coarse = jnp.dot(coarse_weight, pooled, preferred_element_type=jnp.float32)
    pre = conv_out + jnp.repeat(coarse, 8, axis=1)
    output = jax.nn.silu(pre).astype(jnp.bfloat16)
    sigma = jax.nn.sigmoid(pre)
    grad_pre = out_grad.astype(jnp.float32) * sigma * (1.0 + pre * (1.0 - sigma))
    grad_pre_bf = grad_pre.astype(jnp.bfloat16)
    grad_parent = jnp.sum(grad_pre.reshape(channels, voxels // 8, 8), axis=2)
    scale = float(voxels) ** -0.5
    coarse_grad = jnp.dot(grad_parent, pooled.astype(jnp.float32).T, precision=lax.Precision.HIGHEST) * scale
    coarse_input = jnp.dot(coarse_weight.astype(jnp.float32).T, grad_parent, precision=lax.Precision.HIGHEST)
    start_grad = (jnp.repeat(coarse_input, 8, axis=1) / 8.0).reshape(channels, nblocks, 128)

    def backward_step(offset, carry):
        input_grad, weight_grad = carry
        spread = jnp.dot(conv_weight[offset].T, grad_pre_bf, preferred_element_type=jnp.float32)
        spread = spread.reshape(channels, nblocks, 128) * keep_flag[offset].astype(jnp.float32)[None, :, None]
        input_grad = input_grad.at[:, source[offset], :].add(spread)
        single = jnp.dot(grad_pre_bf, gather_offset(offset).T, preferred_element_type=jnp.float32)
        weight_grad = weight_grad.at[offset].set(single)
        return input_grad, weight_grad

    input_grad, weight_grad = lax.fori_loop(0, OFFSETS, backward_step, (start_grad, jnp.zeros((OFFSETS, channels, channels), jnp.float32)))
    return output, input_grad.reshape(channels, voxels), weight_grad * scale, coarse_grad
```

```python
import functools

import jax
import jax.numpy as jnp
from jax import lax
from jax.experimental import pallas as pl
from jax.experimental.pallas import tpu as pltpu
from jax.sharding import PartitionSpec as P

OFFSETS = 27
TERMS = 28
PAIRS = TERMS // 2
BLOCK = 128
BF = jnp.bfloat16
F32 = jnp.float32


def call(kernel, name, outs, kinds, scratch=(), flops=0, size=0, limit=48 << 20):
    space = {"s": pltpu.SMEM, "v": pltpu.VMEM}
    many = isinstance(outs, (list, tuple))
    spec = pl.BlockSpec(memory_space=pltpu.VMEM)
    return pl.pallas_call(
        kernel,
        name=name,
        out_shape=outs,
        in_specs=[pl.BlockSpec(memory_space=space[k]) for k in kinds],
        out_specs=[spec] * len(outs) if many else spec,
        scratch_shapes=list(scratch),
        compiler_params=pltpu.CompilerParams(vmem_limit_bytes=limit),
        cost_estimate=pl.CostEstimate(flops=flops, bytes_accessed=size, transcendentals=0),
    )


def mean_matrix():
    row = lax.broadcasted_iota(jnp.int32, (BLOCK, BLOCK), 0) // 8
    column = lax.broadcasted_iota(jnp.int32, (BLOCK, BLOCK), 1) // 8
    return jnp.where(row == column, 0.125, 0.0).astype(BF)


def columns(index):
    return pl.ds(pl.multiple_of(index * BLOCK, BLOCK), BLOCK)


def pack_kernel(send_block, send_count, features, outgoing):
    for peer in range(outgoing.shape[0]):
        block = features[:, columns(send_block[0, peer])]
        outgoing[peer] = block * send_count[0, peer].astype(F32).astype(BF)


def split_kernel(place, conv_weight, coarse_weight, pieces):
    quarter = conv_weight.shape[1]
    for pair in range(PAIRS):
        first = conv_weight[2 * pair]
        second = conv_weight[2 * pair + 1] if 2 * pair + 1 < OFFSETS else coarse_weight[...]
        cuts = [slice(t * quarter, (t + 1) * quarter) for t in range(4)]
        tiles = [jnp.concatenate([first[:, c], second[:, c]], axis=1) for c in cuts]
        for step in range(4):
            target = lax.rem(place[0] + step, 4)
            low = jnp.where(target == 0, tiles[0], tiles[1])
            high = jnp.where(target == 2, tiles[2], tiles[3])
            pieces[step * PAIRS + pair] = jnp.where(target < 2, low, high)


def join_kernel(piece0, piece1, piece2, piece3, weight, flipped):
    for pair in range(PAIRS):
        tile = jnp.concatenate([p[pair] for p in (piece0, piece1, piece2, piece3)], axis=0)
        weight[:, pair * BLOCK : (pair + 1) * BLOCK] = tile
        flipped[pair * BLOCK : (pair + 1) * BLOCK, :] = tile.T


def fill_table(features, incoming, table, nblocks):
    for block in range(nblocks):
        table[block] = features[:, block * BLOCK : (block + 1) * BLOCK]
    table[nblocks : nblocks + incoming.shape[0]] = incoming[...]
    table[nblocks + incoming.shape[0]] = jnp.zeros(table.shape[1:], BF)


def slot(neighbour, offset, block, extent):
    named = neighbour[offset, block]
    return jnp.where(named < 0, extent, named)


def fill_gathered(neighbour, table, gathered, nblocks, extent):
    quarter = table.shape[1]

    def step(offset, carry):
        rows = pl.ds(pl.multiple_of(offset * quarter, quarter), quarter)
        for block in range(nblocks):
            picked = table[slot(neighbour, offset, block, extent)]
            gathered[rows, block * BLOCK : (block + 1) * BLOCK] = picked
        return carry

    lax.fori_loop(0, OFFSETS, step, 0)
    mean = mean_matrix()
    for block in range(nblocks):
        pooled = jnp.dot(table[block], mean, preferred_element_type=F32).astype(BF)
        gathered[OFFSETS * quarter :, block * BLOCK : (block + 1) * BLOCK] = pooled


def forward_kernel(
    neighbour, features, incoming, weight, out0, out1, out2, out3, table, gathered
):
    quarter, row_count = features.shape
    nblocks = row_count // BLOCK
    extent = nblocks + incoming.shape[0]
    fill_table(features, incoming, table, nblocks)
    fill_gathered(neighbour, table, gathered, nblocks, extent)
    for tile in range(row_count // 256):
        cut = slice(tile * 256, (tile + 1) * 256)
        total = jnp.dot(weight[...], gathered[:, cut], preferred_element_type=F32)
        for step, out in enumerate((out0, out1, out2, out3)):
            out[:, cut] = total[step * quarter : (step + 1) * quarter].astype(out.dtype)


def activation_kernel(own, part1, part2, part3, out_grad, output, grad):
    pre = (own[...] + part1[...].astype(F32)) + (part2[...].astype(F32) + part3[...].astype(F32))
    sigma = 1.0 / (1.0 + jnp.exp(-pre))
    output[...] = (pre * sigma).astype(BF)
    grad[...] = (out_grad[...].astype(F32) * sigma * (1.0 + pre * (1.0 - sigma))).astype(BF)


def weight_kernel(
    place, neighbour, features, incoming, grad0, grad1, grad2, grad3, parts, table, gathered, flipped
):
    quarter, row_count = features.shape
    nblocks = row_count // BLOCK
    extent = nblocks + incoming.shape[0]
    fill_table(features, incoming, table, nblocks)
    fill_gathered(neighbour, table, gathered, nblocks, extent)
    for block in range(nblocks):
        cut = slice(block * BLOCK, (block + 1) * BLOCK)
        tall = jnp.concatenate([g[:, cut] for g in (grad0, grad1, grad2, grad3)], axis=0)
        flipped[cut, :] = tall.T
    half = quarter // 2
    for pair in range(PAIRS):
        rows = slice(pair * BLOCK, (pair + 1) * BLOCK)
        product = jnp.dot(gathered[rows, :], flipped[...], preferred_element_type=F32)
        upright = product.T.astype(BF)
        for step in range(4):
            target = lax.rem(place[0] - step + 4, 4)
            for side in range(2):
                start = step * quarter + side * half
                parts[2 * pair + side, target] = upright[start : start + half]
    for spare in range(2 * PAIRS, parts.shape[0]):
        parts[spare] = jnp.zeros(parts.shape[1:], BF)


def table_kernel(neighbour, weight_t, grad0, grad1, grad2, grad3, local, returned, total):
    quarter, row_count = grad0.shape
    nblocks = row_count // BLOCK
    extent = nblocks + returned.shape[0]
    total[...] = jnp.zeros_like(total)
    mean = mean_matrix()
    for tile in range(nblocks // 2):
        cut = slice(tile * 256, (tile + 1) * 256)
        tall = jnp.concatenate([g[:, cut] for g in (grad0, grad1, grad2, grad3)], axis=0)

        def step(offset, carry, tall=tall, tile=tile):
            rows = pl.ds(pl.multiple_of(offset * quarter, quarter), quarter)
            product = jnp.dot(weight_t[rows, :], tall, preferred_element_type=F32)
            for side in range(2):
                place = slot(neighbour, offset, 2 * tile + side, extent)
                total[place] += product[:, side * BLOCK : (side + 1) * BLOCK]
            return carry

        lax.fori_loop(0, OFFSETS, step, 0)
        coarse = jnp.dot(weight_t[OFFSETS * quarter :, :], tall, preferred_element_type=F32)
        for side in range(2):
            value = coarse[:, side * BLOCK : (side + 1) * BLOCK]
            high = value.astype(BF)
            low = (value - high.astype(F32)).astype(BF)
            total[2 * tile + side] += jnp.dot(high, mean, preferred_element_type=F32) + jnp.dot(
                low, mean, preferred_element_type=F32
            )
    for block in range(nblocks):
        local[:, block * BLOCK : (block + 1) * BLOCK] = total[block]
    returned[...] = total[nblocks:extent].astype(BF)


def return_kernel(send_block, send_count, local, returned, input_grad):
    input_grad[...] = local[...]
    for peer in range(returned.shape[0]):
        factor = send_count[0, peer].astype(F32)
        input_grad[:, columns(send_block[0, peer])] += returned[peer].astype(F32) * factor


def sum_kernel(scale, parts, chunk):
    quarter = 64
    total = parts[0].astype(F32)
    for source in range(1, parts.shape[0]):
        total = total + parts[source].astype(F32)
    total = total * scale
    for side in range(2):
        cut = slice(side * quarter, (side + 1) * quarter)
        chunk[side] = jnp.concatenate([total[c, :, cut] for c in range(4)], axis=1).astype(BF)


def unpack_kernel(chunks, conv_grad, coarse_grad):
    half = chunks.shape[2]
    for piece in range(2 * PAIRS):
        rows = slice((piece % 2) * half, (piece % 2 + 1) * half)
        for side in range(2):
            offset = 2 * (piece // 2) + side
            value = chunks[piece, side].astype(F32)
            if offset < OFFSETS:
                conv_grad[offset, rows, :] = value
            else:
                coarse_grad[rows, :] = value


def shift(value, axis, step):
    size = lax.axis_size(axis)
    return lax.ppermute(value, axis, [(i, (i + step) % size) for i in range(size)])


def local_step(features, conv_weight, coarse_weight, out_grad, send_block, send_count, neighbour):
    n_morton = lax.axis_size("morton")
    quarter, row_count = features.shape
    channels = conv_weight.shape[2]
    nblocks = row_count // BLOCK
    extent = nblocks + n_morton
    depth = TERMS * quarter
    flops = 2 * depth * channels * row_count
    place = lax.axis_index("chan").astype(jnp.int32).reshape(1)
    shape = jax.ShapeDtypeStruct

    outgoing = call(
        pack_kernel, "pack", shape((n_morton, quarter, BLOCK), BF), "ssv", size=1 << 20
    )(send_block, send_count, features)
    incoming = lax.all_to_all(outgoing, "morton", 0, 0, tiled=True)

    pieces = call(
        split_kernel, "split", shape((4 * PAIRS, quarter, BLOCK), BF), "svv", size=2 << 20
    )(place, conv_weight, coarse_weight)
    pieces = pieces.reshape(4, PAIRS, quarter, BLOCK)
    weights = [pieces[0]] + [shift(pieces[s], "chan", s) for s in (1, 2, 3)]
    weight, weight_t = call(
        join_kernel,
        "join",
        [shape((channels, depth), BF), shape((depth, channels), BF)],
        "vvvv",
        size=3 << 20,
    )(*weights)

    big = [pltpu.VMEM((extent + 1, quarter, BLOCK), BF), pltpu.VMEM((depth, row_count), BF)]
    wide = (quarter, row_count)
    partial = call(
        forward_kernel,
        "forward",
        [shape(wide, F32)] + [shape(wide, BF)] * 3,
        "svvv",
        big,
        flops,
        4 << 20,
    )(neighbour, features, incoming, weight)
    arrived = [shift(partial[s], "chan", -s) for s in (1, 2, 3)]
    output, grad = call(
        activation_kernel, "activation", [shape(wide, BF)] * 2, "vvvvv", size=2 << 20
    )(partial[0], *arrived, out_grad)
    grads = [grad] + [shift(grad, "chan", s) for s in (1, 2, 3)]

    parts = call(
        weight_kernel,
        "weight_grad",
        shape((n_morton, 4, quarter // 2, BLOCK), BF),
        "ssvvvvvv",
        big + [pltpu.VMEM((row_count, channels), BF)],
        flops,
        4 << 20,
    )(place, neighbour, features, incoming, *grads)
    received = lax.all_to_all(
        parts.reshape(n_morton * 4, quarter // 2, BLOCK), ("morton", "chan"), 0, 0, tiled=True
    ).reshape(parts.shape)

    local, outward = call(
        table_kernel,
        "table_grad",
        [shape(wide, F32), shape((n_morton, quarter, BLOCK), BF)],
        "svvvvv",
        [pltpu.VMEM((extent + 1, quarter, BLOCK), F32)],
        flops,
        4 << 20,
    )(neighbour, weight_t, *grads)
    returned = lax.all_to_all(outward, "morton", 0, 0, tiled=True)
    input_grad = call(return_kernel, "return_add", shape(wide, F32), "ssvv", size=2 << 20)(
        send_block, send_count, local, returned
    )

    scale = float(row_count * n_morton) ** (-0.5)
    chunk = call(
        functools.partial(sum_kernel, scale),
        "sum_parts",
        shape((2, quarter // 2, channels), BF),
        "v",
        size=1 << 20,
    )(received)
    chunks = lax.all_to_all(
        jnp.broadcast_to(chunk, (n_morton,) + chunk.shape), "morton", 0, 0, tiled=True
    )
    conv_grad, coarse_grad = call(
        unpack_kernel,
        "unpack",
        [shape((OFFSETS, quarter, channels), F32), shape((quarter, channels), F32)],
        "v",
        size=3 << 20,
    )(chunks)
    return output, input_grad, conv_grad, coarse_grad


def solution(mesh):
    placed = (
        P("chan", "morton"),
        P(None, "chan", None),
        P("chan", None),
        P("chan", "morton"),
        P("morton", None),
        P("morton", None),
        P(None, "morton"),
    )
    return jax.shard_map(
        local_step,
        mesh=mesh,
        in_specs=placed,
        out_specs=(
            P("chan", "morton"),
            P("chan", "morton"),
            P(None, "chan", None),
            P("chan", None),
        ),
        check_vma=False,
    )
```

```python
import functools

import jax
import jax.numpy as jnp
from jax import lax
from jax.experimental import pallas as pl
from jax.experimental.pallas import tpu as pltpu
from jax.sharding import PartitionSpec as P

OFFSETS = 27
TERMS = 28
PAIRS = TERMS // 2
BLOCK = 128
BF = jnp.bfloat16
F32 = jnp.float32


def call(kernel, name, outs, kinds, scratch=(), flops=0, size=0, limit=48 << 20):
    space = {"s": pltpu.SMEM, "v": pltpu.VMEM}
    many = isinstance(outs, (list, tuple))
    spec = pl.BlockSpec(memory_space=pltpu.VMEM)
    return pl.pallas_call(
        kernel,
        name=name,
        out_shape=outs,
        in_specs=[pl.BlockSpec(memory_space=space[k]) for k in kinds],
        out_specs=[spec] * len(outs) if many else spec,
        scratch_shapes=list(scratch),
        compiler_params=pltpu.CompilerParams(vmem_limit_bytes=limit),
        cost_estimate=pl.CostEstimate(flops=flops, bytes_accessed=size, transcendentals=0),
    )


def mean_matrix():
    row = lax.broadcasted_iota(jnp.int32, (BLOCK, BLOCK), 0) // 8
    column = lax.broadcasted_iota(jnp.int32, (BLOCK, BLOCK), 1) // 8
    return jnp.where(row == column, 0.125, 0.0).astype(BF)


def columns(index):
    return pl.ds(pl.multiple_of(index * BLOCK, BLOCK), BLOCK)


def pack_kernel(send_block, send_count, features, outgoing):
    for peer in range(outgoing.shape[0]):
        block = features[:, columns(send_block[0, peer])]
        outgoing[peer] = block * send_count[0, peer].astype(F32).astype(BF)


def split_kernel(place, conv_weight, coarse_weight, pieces):
    quarter = conv_weight.shape[1]
    for pair in range(PAIRS):
        first = conv_weight[2 * pair]
        second = conv_weight[2 * pair + 1] if 2 * pair + 1 < OFFSETS else coarse_weight[...]
        cuts = [slice(t * quarter, (t + 1) * quarter) for t in range(4)]
        tiles = [jnp.concatenate([first[:, c], second[:, c]], axis=1) for c in cuts]
        for step in range(4):
            target = lax.rem(place[0] + step, 4)
            low = jnp.where(target == 0, tiles[0], tiles[1])
            high = jnp.where(target == 2, tiles[2], tiles[3])
            pieces[step * PAIRS + pair] = jnp.where(target < 2, low, high)


def join_kernel(piece0, piece1, piece2, piece3, weight, flipped):
    for pair in range(PAIRS):
        tile = jnp.concatenate([p[pair] for p in (piece0, piece1, piece2, piece3)], axis=0)
        weight[:, pair * BLOCK : (pair + 1) * BLOCK] = tile
        flipped[pair * BLOCK : (pair + 1) * BLOCK, :] = tile.T


def fill_table(features, incoming, table, nblocks):
    for block in range(nblocks):
        table[block] = features[:, block * BLOCK : (block + 1) * BLOCK]
    table[nblocks : nblocks + incoming.shape[0]] = incoming[...]
    table[nblocks + incoming.shape[0]] = jnp.zeros(table.shape[1:], BF)


def slot(neighbour, offset, block, extent):
    named = neighbour[offset, block]
    return jnp.where(named < 0, extent, named)


def fill_gathered(neighbour, table, gathered, nblocks, extent):
    quarter = table.shape[1]

    def step(offset, carry):
        rows = pl.ds(pl.multiple_of(offset * quarter, quarter), quarter)
        for block in range(nblocks):
            picked = table[slot(neighbour, offset, block, extent)]
            gathered[rows, block * BLOCK : (block + 1) * BLOCK] = picked
        return carry

    lax.fori_loop(0, OFFSETS, step, 0, unroll=27)
    mean = mean_matrix()
    for block in range(nblocks):
        pooled = jnp.dot(table[block], mean, preferred_element_type=F32).astype(BF)
        gathered[OFFSETS * quarter :, block * BLOCK : (block + 1) * BLOCK] = pooled


def forward_kernel(
    neighbour, features, incoming, weight, out0, out1, out2, out3, table, gathered
):
    quarter, row_count = features.shape
    nblocks = row_count // BLOCK
    extent = nblocks + incoming.shape[0]
    fill_table(features, incoming, table, nblocks)
    fill_gathered(neighbour, table, gathered, nblocks, extent)
    for tile in range(row_count // 256):
        cut = slice(tile * 256, (tile + 1) * 256)
        total = jnp.dot(weight[...], gathered[:, cut], preferred_element_type=F32)
        for step, out in enumerate((out0, out1, out2, out3)):
            out[:, cut] = total[step * quarter : (step + 1) * quarter].astype(out.dtype)


def activation_kernel(own, part1, part2, part3, out_grad, output, grad):
    pre = (own[...] + part1[...].astype(F32)) + (part2[...].astype(F32) + part3[...].astype(F32))
    sigma = 1.0 / (1.0 + jnp.exp(-pre))
    output[...] = (pre * sigma).astype(BF)
    grad[...] = (out_grad[...].astype(F32) * sigma * (1.0 + pre * (1.0 - sigma))).astype(BF)


def weight_kernel(
    place, neighbour, features, incoming, grad0, grad1, grad2, grad3, parts, table, gathered, flipped
):
    quarter, row_count = features.shape
    nblocks = row_count // BLOCK
    extent = nblocks + incoming.shape[0]
    fill_table(features, incoming, table, nblocks)
    fill_gathered(neighbour, table, gathered, nblocks, extent)
    for block in range(nblocks):
        cut = slice(block * BLOCK, (block + 1) * BLOCK)
        tall = jnp.concatenate([g[:, cut] for g in (grad0, grad1, grad2, grad3)], axis=0)
        flipped[cut, :] = tall.T
    half = quarter // 2
    for pair in range(PAIRS):
        rows = slice(pair * BLOCK, (pair + 1) * BLOCK)
        product = jnp.dot(gathered[rows, :], flipped[...], preferred_element_type=F32)
        upright = product.T.astype(BF)
        for step in range(4):
            target = lax.rem(place[0] - step + 4, 4)
            for side in range(2):
                start = step * quarter + side * half
                parts[2 * pair + side, target] = upright[start : start + half]
    for spare in range(2 * PAIRS, parts.shape[0]):
        parts[spare] = jnp.zeros(parts.shape[1:], BF)


def table_kernel(neighbour, weight_t, grad0, grad1, grad2, grad3, local, returned, total, spread):
    quarter, row_count = grad0.shape
    nblocks = row_count // BLOCK
    extent = nblocks + returned.shape[0]
    total[...] = jnp.zeros_like(total)
    mean = mean_matrix()
    for tile in range(nblocks // 2):
        cut = slice(tile * 256, (tile + 1) * 256)
        tall = jnp.concatenate([g[:, cut] for g in (grad0, grad1, grad2, grad3)], axis=0)
        product = jnp.dot(weight_t[...], tall, preferred_element_type=F32)
        spread[...] = product[: OFFSETS * quarter]

        def step(offset, carry, tile=tile):
            rows = pl.ds(pl.multiple_of(offset * quarter, quarter), quarter)
            for side in range(2):
                place = slot(neighbour, offset, 2 * tile + side, extent)
                total[place] += spread[rows, side * BLOCK : (side + 1) * BLOCK]
            return carry

        lax.fori_loop(0, OFFSETS, step, 0, unroll=27)
        coarse = product[OFFSETS * quarter :]
        for side in range(2):
            value = coarse[:, side * BLOCK : (side + 1) * BLOCK]
            high = value.astype(BF)
            low = (value - high.astype(F32)).astype(BF)
            total[2 * tile + side] += jnp.dot(high, mean, preferred_element_type=F32) + jnp.dot(
                low, mean, preferred_element_type=F32
            )
    for block in range(nblocks):
        local[:, block * BLOCK : (block + 1) * BLOCK] = total[block]
    returned[...] = total[nblocks:extent].astype(BF)


def return_kernel(send_block, send_count, local, returned, input_grad):
    input_grad[...] = local[...]
    for peer in range(returned.shape[0]):
        factor = send_count[0, peer].astype(F32)
        input_grad[:, columns(send_block[0, peer])] += returned[peer].astype(F32) * factor


def sum_kernel(scale, parts, chunk):
    quarter = 64
    total = parts[0].astype(F32)
    for source in range(1, parts.shape[0]):
        total = total + parts[source].astype(F32)
    total = total * scale
    for side in range(2):
        cut = slice(side * quarter, (side + 1) * quarter)
        chunk[side] = jnp.concatenate([total[c, :, cut] for c in range(4)], axis=1).astype(BF)


def unpack_kernel(core, mine, other, conv_grad, coarse_grad):
    half = mine.shape[2]
    for chunks, side in ((mine, core[0]), (other, 1 - core[0])):
        rows = pl.ds(pl.multiple_of(side * half, half), half)
        for offset in range(TERMS):
            value = chunks[offset // 2, offset % 2].astype(F32)
            if offset < OFFSETS:
                conv_grad[offset, rows, :] = value
            else:
                coarse_grad[rows, :] = value


def shift(value, axis, step):
    size = lax.axis_size(axis)
    return lax.ppermute(value, axis, [(i, (i + step) % size) for i in range(size)])


def local_step(features, conv_weight, coarse_weight, out_grad, send_block, send_count, neighbour):
    n_morton = lax.axis_size("morton")
    quarter, row_count = features.shape
    channels = conv_weight.shape[2]
    nblocks = row_count // BLOCK
    extent = nblocks + n_morton
    depth = TERMS * quarter
    flops = 2 * depth * channels * row_count
    place = lax.axis_index("chan").astype(jnp.int32).reshape(1)
    shape = jax.ShapeDtypeStruct

    outgoing = call(
        pack_kernel, "pack", shape((n_morton, quarter, BLOCK), BF), "ssv", size=1 << 20
    )(send_block, send_count, features)
    incoming = lax.all_to_all(outgoing, "morton", 0, 0, tiled=True)

    pieces = call(
        split_kernel, "split", shape((4 * PAIRS, quarter, BLOCK), BF), "svv", size=2 << 20
    )(place, conv_weight, coarse_weight)
    pieces = pieces.reshape(4, PAIRS, quarter, BLOCK)
    weights = [pieces[0]] + [shift(pieces[s], "chan", s) for s in (1, 2, 3)]
    weight, weight_t = call(
        join_kernel,
        "join",
        [shape((channels, depth), BF), shape((depth, channels), BF)],
        "vvvv",
        size=3 << 20,
    )(*weights)

    big = [pltpu.VMEM((extent + 1, quarter, BLOCK), BF), pltpu.VMEM((depth, row_count), BF)]
    wide = (quarter, row_count)
    partial = call(
        forward_kernel,
        "forward",
        [shape(wide, F32)] + [shape(wide, BF)] * 3,
        "svvv",
        big,
        flops,
        4 << 20,
    )(neighbour, features, incoming, weight)
    arrived = [shift(partial[s], "chan", -s) for s in (1, 2, 3)]
    output, grad = call(
        activation_kernel, "activation", [shape(wide, BF)] * 2, "vvvvv", size=2 << 20
    )(partial[0], *arrived, out_grad)
    grads = [grad] + [shift(grad, "chan", s) for s in (1, 2, 3)]

    parts = call(
        weight_kernel,
        "weight_grad",
        shape((n_morton, 4, quarter // 2, BLOCK), BF),
        "ssvvvvvv",
        big + [pltpu.VMEM((row_count, channels), BF)],
        flops,
        4 << 20,
    )(place, neighbour, features, incoming, *grads)
    received = lax.all_to_all(
        parts.reshape(n_morton * 4, quarter // 2, BLOCK), ("morton", "chan"), 0, 0, tiled=True
    ).reshape(parts.shape)

    local, outward = call(
        table_kernel,
        "table_grad",
        [shape(wide, F32), shape((n_morton, quarter, BLOCK), BF)],
        "svvvvv",
        [pltpu.VMEM((extent + 1, quarter, BLOCK), F32), pltpu.VMEM((OFFSETS * quarter, 256), F32)],
        flops,
        4 << 20,
    )(neighbour, weight_t, *grads)
    returned = lax.all_to_all(outward, "morton", 0, 0, tiled=True)
    input_grad = call(return_kernel, "return_add", shape(wide, F32), "ssvv", size=2 << 20)(
        send_block, send_count, local, returned
    )

    scale = float(row_count * n_morton) ** (-0.5)
    chunk = call(
        functools.partial(sum_kernel, scale),
        "sum_parts",
        shape((2, quarter // 2, channels), BF),
        "v",
        size=1 << 20,
    )(received)
    chips = n_morton // 2
    same_core = [[2 * chip + core for chip in range(chips)] for core in range(2)]
    mine = lax.all_to_all(
        jnp.broadcast_to(chunk, (chips,) + chunk.shape),
        "morton",
        0,
        0,
        axis_index_groups=same_core,
        tiled=True,
    )
    other = lax.ppermute(mine, "morton", [(i, i ^ 1) for i in range(n_morton)])
    core = lax.rem(lax.axis_index("morton"), 2).astype(jnp.int32).reshape(1)
    conv_grad, coarse_grad = call(
        unpack_kernel,
        "unpack",
        [shape((OFFSETS, quarter, channels), F32), shape((quarter, channels), F32)],
        "svv",
        size=3 << 20,
    )(core, mine, other)
    return output, input_grad, conv_grad, coarse_grad


def solution(mesh):
    placed = (
        P("chan", "morton"),
        P(None, "chan", None),
        P("chan", None),
        P("chan", "morton"),
        P("morton", None),
        P("morton", None),
        P(None, "morton"),
    )
    return jax.shard_map(
        local_step,
        mesh=mesh,
        in_specs=placed,
        out_specs=(
            P("chan", "morton"),
            P("chan", "morton"),
            P(None, "chan", None),
            P("chan", None),
        ),
        check_vma=False,
    )
```

```python
import functools

import jax
import jax.numpy as jnp
from jax import lax
from jax.experimental import pallas as pl
from jax.experimental.pallas import tpu as pltpu
from jax.sharding import PartitionSpec as P

OFFSETS = 27
TERMS = 28
PAIRS = TERMS // 2
BLOCK = 128
BF = jnp.bfloat16
F32 = jnp.float32


def call(kernel, name, outs, kinds, scratch=(), flops=0, size=0, limit=48 << 20):
    space = {"s": pltpu.SMEM, "v": pltpu.VMEM, "a": pl.ANY}
    many = isinstance(outs, (list, tuple))
    spec = pl.BlockSpec(memory_space=pltpu.VMEM)
    return pl.pallas_call(
        kernel,
        name=name,
        out_shape=outs,
        in_specs=[pl.BlockSpec(memory_space=space[k]) for k in kinds],
        out_specs=[spec] * len(outs) if many else spec,
        scratch_shapes=list(scratch),
        compiler_params=pltpu.CompilerParams(vmem_limit_bytes=limit),
        cost_estimate=pl.CostEstimate(flops=flops, bytes_accessed=size, transcendentals=0),
    )


def mean_matrix():
    row = lax.broadcasted_iota(jnp.int32, (BLOCK, BLOCK), 0) // 8
    column = lax.broadcasted_iota(jnp.int32, (BLOCK, BLOCK), 1) // 8
    return jnp.where(row == column, 0.125, 0.0).astype(BF)


def columns(index):
    return pl.ds(pl.multiple_of(index * BLOCK, BLOCK), BLOCK)


def pack_kernel(send_block, send_count, features, after, outgoing):
    del after
    for peer in range(outgoing.shape[0]):
        block = features[:, columns(send_block[0, peer])]
        outgoing[peer] = block * send_count[0, peer].astype(F32).astype(BF)


def split_kernel(place, conv_weight, coarse_weight, pieces):
    quarter = conv_weight.shape[1]
    for pair in range(PAIRS):
        first = conv_weight[2 * pair]
        second = conv_weight[2 * pair + 1] if 2 * pair + 1 < OFFSETS else coarse_weight[...]
        cuts = [slice(t * quarter, (t + 1) * quarter) for t in range(4)]
        tiles = [jnp.concatenate([first[:, c], second[:, c]], axis=1) for c in cuts]
        for step in range(4):
            target = lax.rem(place[0] + step, 4)
            low = jnp.where(target == 0, tiles[0], tiles[1])
            high = jnp.where(target == 2, tiles[2], tiles[3])
            pieces[step * PAIRS + pair] = jnp.where(target < 2, low, high)


def join_kernel(piece0, piece1, piece2, piece3, weight, flipped):
    for pair in range(PAIRS):
        tile = jnp.concatenate([p[pair] for p in (piece0, piece1, piece2, piece3)], axis=0)
        weight[:, pair * BLOCK : (pair + 1) * BLOCK] = tile
        flipped[pair * BLOCK : (pair + 1) * BLOCK, :] = tile.T


def fill_table(features, incoming, table, nblocks):
    for block in range(nblocks):
        table[block] = features[:, block * BLOCK : (block + 1) * BLOCK]
    table[nblocks : nblocks + incoming.shape[0]] = incoming[...]
    table[nblocks + incoming.shape[0]] = jnp.zeros(table.shape[1:], BF)


def slot(neighbour, offset, block, extent):
    named = neighbour[offset, block]
    return jnp.where(named < 0, extent, named)


def fill_gathered(neighbour, table, gathered, first, extent):
    quarter = table.shape[1]
    nblocks = gathered.shape[1] // BLOCK

    def step(offset, carry):
        rows = pl.ds(pl.multiple_of(offset * quarter, quarter), quarter)
        for block in range(nblocks):
            picked = table[slot(neighbour, offset, first + block, extent)]
            gathered[rows, block * BLOCK : (block + 1) * BLOCK] = picked
        return carry

    lax.fori_loop(0, OFFSETS, step, 0, unroll=27)
    mean = mean_matrix()
    for block in range(nblocks):
        pooled = jnp.dot(table[first + block], mean, preferred_element_type=F32).astype(BF)
        gathered[OFFSETS * quarter :, block * BLOCK : (block + 1) * BLOCK] = pooled


def forward_kernel(
    half, neighbour, features, incoming, weight, out0, out1, out2, out3, table, gathered
):
    quarter, row_count = features.shape
    nblocks = row_count // BLOCK
    extent = nblocks + incoming.shape[0]
    fill_table(features, incoming, table, nblocks)
    fill_gathered(neighbour, table, gathered, half * nblocks // 2, extent)
    for tile in range(row_count // 512):
        cut = slice(tile * 256, (tile + 1) * 256)
        total = jnp.dot(weight[...], gathered[:, cut], preferred_element_type=F32)
        for step, out in enumerate((out0, out1, out2, out3)):
            out[:, cut] = total[step * quarter : (step + 1) * quarter].astype(out.dtype)


def activate(own, part1, part2, part3, out_grad):
    pre = (own[...] + part1[...].astype(F32)) + (part2[...].astype(F32) + part3[...].astype(F32))
    sigma = 1.0 / (1.0 + jnp.exp(-pre))
    grad = out_grad.astype(F32) * sigma * (1.0 + pre * (1.0 - sigma))
    return (pre * sigma).astype(BF), grad.astype(BF)


def activation_kernel(own, part1, part2, part3, out_grad, output, grad):
    middle = own.shape[1]
    output[...], grad[...] = activate(own, part1, part2, part3, out_grad[:, :middle])


def activation_end_kernel(own, part1, part2, part3, out_grad, before, output, grad):
    middle = own.shape[1]
    output[:, :middle] = before[...]
    output[:, middle:], grad[...] = activate(own, part1, part2, part3, out_grad[:, middle:])


def prepare_weight(half, neighbour, features, incoming, grads, table, gathered, flipped):
    nblocks = features.shape[1] // BLOCK
    extent = nblocks + incoming.shape[0]
    fill_table(features, incoming, table, nblocks)
    fill_gathered(neighbour, table, gathered, half * nblocks // 2, extent)
    for block in range(nblocks // 2):
        cut = slice(block * BLOCK, (block + 1) * BLOCK)
        tall = jnp.concatenate([g[:, cut] for g in grads], axis=0)
        flipped[cut, :] = tall.T


def weight_first_kernel(
    neighbour, features, incoming, grad0, grad1, grad2, grad3, held, table, gathered, flipped
):
    grads = (grad0, grad1, grad2, grad3)
    prepare_weight(0, neighbour, features, incoming, grads, table, gathered, flipped)
    held[...] = jnp.dot(gathered[...], flipped[...], preferred_element_type=F32)


def weight_second_kernel(
    place, neighbour, features, incoming, grad0, grad1, grad2, grad3, held, parts, table, gathered, flipped
):
    quarter = features.shape[0]
    grads = (grad0, grad1, grad2, grad3)
    prepare_weight(1, neighbour, features, incoming, grads, table, gathered, flipped)
    half = quarter // 2
    for pair in range(PAIRS):
        rows = slice(pair * BLOCK, (pair + 1) * BLOCK)
        product = jnp.dot(gathered[rows, :], flipped[...], preferred_element_type=F32)
        upright = (product + held[rows, :]).T.astype(BF)
        for step in range(4):
            target = lax.rem(place[0] - step + 4, 4)
            for side in range(2):
                start = step * quarter + side * half
                parts[2 * pair + side, target] = upright[start : start + half]
    for spare in range(2 * PAIRS, parts.shape[0]):
        parts[spare] = jnp.zeros(parts.shape[1:], BF)


def table_kernel(
    neighbour, weight_t, g00, g01, g02, g03, g10, g11, g12, g13, local, returned, total, spread
):
    quarter, row_count = local.shape
    nblocks = row_count // BLOCK
    extent = nblocks + returned.shape[0]
    total[...] = jnp.zeros_like(total)
    mean = mean_matrix()
    for tile in range(nblocks // 2):
        grads = (g00, g01, g02, g03) if tile < nblocks // 4 else (g10, g11, g12, g13)
        start = tile % (nblocks // 4) * 256
        tall = jnp.concatenate([g[:, start : start + 256] for g in grads], axis=0)
        product = jnp.dot(weight_t[...], tall, preferred_element_type=F32)
        spread[...] = product[: OFFSETS * quarter]

        def step(offset, carry, tile=tile):
            rows = pl.ds(pl.multiple_of(offset * quarter, quarter), quarter)
            for side in range(2):
                place = slot(neighbour, offset, 2 * tile + side, extent)
                total[place] += spread[rows, side * BLOCK : (side + 1) * BLOCK]
            return carry

        lax.fori_loop(0, OFFSETS, step, 0, unroll=27)
        coarse = product[OFFSETS * quarter :]
        for side in range(2):
            value = coarse[:, side * BLOCK : (side + 1) * BLOCK]
            high = value.astype(BF)
            low = (value - high.astype(F32)).astype(BF)
            total[2 * tile + side] += jnp.dot(high, mean, preferred_element_type=F32) + jnp.dot(
                low, mean, preferred_element_type=F32
            )
    for block in range(nblocks):
        local[:, block * BLOCK : (block + 1) * BLOCK] = total[block]
    returned[...] = total[nblocks:extent].astype(BF)


def return_kernel(send_block, send_count, local, returned, input_grad):
    input_grad[...] = local[...]
    for peer in range(returned.shape[0]):
        factor = send_count[0, peer].astype(F32)
        input_grad[:, columns(send_block[0, peer])] += returned[peer].astype(F32) * factor


def sum_kernel(scale, parts, after, chunk):
    del after
    quarter = 64
    total = parts[0].astype(F32)
    for source in range(1, parts.shape[0]):
        total = total + parts[source].astype(F32)
    total = total * scale
    for side in range(2):
        cut = slice(side * quarter, (side + 1) * quarter)
        chunk[side] = jnp.concatenate([total[c, :, cut] for c in range(4)], axis=1).astype(BF)


def unpack_kernel(core, mine, other, conv_grad, coarse_grad):
    half = mine.shape[2]
    for chunks, side in ((mine, core[0]), (other, 1 - core[0])):
        rows = pl.ds(pl.multiple_of(side * half, half), half)
        for offset in range(TERMS):
            value = chunks[offset // 2, offset % 2].astype(F32)
            if offset < OFFSETS:
                conv_grad[offset, rows, :] = value
            else:
                coarse_grad[rows, :] = value


def shift(value, axis, step):
    size = lax.axis_size(axis)
    return lax.ppermute(value, axis, [(i, (i + step) % size) for i in range(size)])


def local_step(features, conv_weight, coarse_weight, out_grad, send_block, send_count, neighbour):
    n_morton = lax.axis_size("morton")
    quarter, row_count = features.shape
    channels = conv_weight.shape[2]
    nblocks = row_count // BLOCK
    extent = nblocks + n_morton
    depth = TERMS * quarter
    flops = 2 * depth * channels * row_count
    place = lax.axis_index("chan").astype(jnp.int32).reshape(1)
    shape = jax.ShapeDtypeStruct

    pieces = call(
        split_kernel, "split", shape((4 * PAIRS, quarter, BLOCK), BF), "svv", size=2 << 20
    )(place, conv_weight, coarse_weight)
    outgoing = call(
        pack_kernel, "pack", shape((n_morton, quarter, BLOCK), BF), "ssva", size=64 << 20
    )(send_block, send_count, features, pieces)
    incoming = lax.all_to_all(outgoing, "morton", 0, 0, tiled=True)

    pieces = pieces.reshape(4, PAIRS, quarter, BLOCK)
    weights = [pieces[0]] + [shift(pieces[s], "chan", s) for s in (1, 2, 3)]
    weight, weight_t = call(
        join_kernel,
        "join",
        [shape((channels, depth), BF), shape((depth, channels), BF)],
        "vvvv",
        size=3 << 20,
    )(*weights)

    middle = row_count // 2
    big = [pltpu.VMEM((extent + 1, quarter, BLOCK), BF), pltpu.VMEM((depth, middle), BF)]
    turned = [pltpu.VMEM((middle, channels), BF)]
    wide, part = (quarter, row_count), (quarter, middle)
    grads = []
    output = ()
    for half in range(2):
        partial = call(
            functools.partial(forward_kernel, half),
            f"forward{half}",
            [shape(part, F32)] + [shape(part, BF)] * 3,
            "svvv",
            big,
            flops // 2,
            3 << 20,
        )(neighbour, features, incoming, weight)
        arrived = [shift(partial[s], "chan", -s) for s in (1, 2, 3)]
        output, grad = call(
            activation_end_kernel if half else activation_kernel,
            f"activation{half}",
            [shape(wide if half else part, BF), shape(part, BF)],
            "vvvvvv" if half else "vvvvv",
            size=1 << 20,
        )(partial[0], *arrived, out_grad, *((output,) if half else ()))
        grads.append([grad] + [shift(grad, "chan", s) for s in (1, 2, 3)])

    held = call(
        weight_first_kernel,
        "weight_grad0",
        shape((depth, channels), F32),
        "svvvvvv",
        big + turned,
        flops // 2,
        4 << 20,
    )(neighbour, features, incoming, *grads[0])
    parts = call(
        weight_second_kernel,
        "weight_grad1",
        shape((n_morton, 4, quarter // 2, BLOCK), BF),
        "ssvvvvvvv",
        big + turned,
        flops // 2,
        4 << 20,
    )(place, neighbour, features, incoming, *grads[1], held)
    received = lax.all_to_all(
        parts.reshape(n_morton * 4, quarter // 2, BLOCK), ("morton", "chan"), 0, 0, tiled=True
    ).reshape(parts.shape)

    local, outward = call(
        table_kernel,
        "table_grad",
        [shape(wide, F32), shape((n_morton, quarter, BLOCK), BF)],
        "s" + "v" * 9,
        [
            pltpu.VMEM((extent + 1, quarter, BLOCK), F32),
            pltpu.VMEM((OFFSETS * quarter, 256), F32),
        ],
        flops,
        4 << 20,
    )(neighbour, weight_t, *grads[0], *grads[1])
    returned = lax.all_to_all(outward, "morton", 0, 0, tiled=True)
    input_grad = call(return_kernel, "return_add", shape(wide, F32), "ssvv", size=2 << 20)(
        send_block, send_count, local, returned
    )

    scale = float(row_count * n_morton) ** (-0.5)
    chunk = call(
        functools.partial(sum_kernel, scale),
        "sum_parts",
        shape((2, quarter // 2, channels), BF),
        "va",
        size=1 << 20,
    )(received, outward)
    chips = n_morton // 2
    same_core = [[2 * chip + core for chip in range(chips)] for core in range(2)]
    mine = lax.all_to_all(
        jnp.broadcast_to(chunk, (chips,) + chunk.shape),
        "morton",
        0,
        0,
        axis_index_groups=same_core,
        tiled=True,
    )
    other = lax.ppermute(mine, "morton", [(i, i ^ 1) for i in range(n_morton)])
    core = lax.rem(lax.axis_index("morton"), 2).astype(jnp.int32).reshape(1)
    conv_grad, coarse_grad = call(
        unpack_kernel,
        "unpack",
        [shape((OFFSETS, quarter, channels), F32), shape((quarter, channels), F32)],
        "svv",
        size=3 << 20,
    )(core, mine, other)
    return output, input_grad, conv_grad, coarse_grad


def solution(mesh):
    placed = (
        P("chan", "morton"),
        P(None, "chan", None),
        P("chan", None),
        P("chan", "morton"),
        P("morton", None),
        P("morton", None),
        P(None, "morton"),
    )
    return jax.shard_map(
        local_step,
        mesh=mesh,
        in_specs=placed,
        out_specs=(
            P("chan", "morton"),
            P("chan", "morton"),
            P(None, "chan", None),
            P("chan", None),
        ),
        check_vma=False,
    )
```

```python
import functools

import jax
import jax.numpy as jnp
from jax import lax
from jax.experimental import pallas as pl
from jax.experimental.pallas import tpu as pltpu
from jax.sharding import PartitionSpec as P

OFFSETS = 27
TERMS = 28
PAIRS = TERMS // 2
BLOCK = 128
BF = jnp.bfloat16
F32 = jnp.float32


def call(kernel, name, outs, kinds, scratch=(), flops=0, size=0, limit=24 << 20):
    space = {"s": pltpu.SMEM, "v": pltpu.VMEM, "a": pl.ANY}
    many = isinstance(outs, (list, tuple))
    spec = pl.BlockSpec(memory_space=pltpu.VMEM)
    return pl.pallas_call(
        kernel,
        name=name,
        out_shape=outs,
        in_specs=[pl.BlockSpec(memory_space=space[k]) for k in kinds],
        out_specs=[spec] * len(outs) if many else spec,
        scratch_shapes=list(scratch),
        compiler_params=pltpu.CompilerParams(vmem_limit_bytes=limit),
        cost_estimate=pl.CostEstimate(flops=flops, bytes_accessed=size, transcendentals=0),
    )


def mean_matrix():
    row = lax.broadcasted_iota(jnp.int32, (BLOCK, BLOCK), 0) // 8
    column = lax.broadcasted_iota(jnp.int32, (BLOCK, BLOCK), 1) // 8
    return jnp.where(row == column, 0.125, 0.0).astype(BF)


def columns(index):
    return pl.ds(pl.multiple_of(index * BLOCK, BLOCK), BLOCK)


def pack_kernel(send_block, send_count, features, outgoing):
    for peer in range(outgoing.shape[0]):
        block = features[:, columns(send_block[0, peer])]
        outgoing[peer] = block * send_count[0, peer].astype(F32).astype(BF)


def split_kernel(place, conv_weight, coarse_weight, pieces):
    quarter = conv_weight.shape[1]
    for pair in range(PAIRS):
        first = conv_weight[2 * pair]
        second = conv_weight[2 * pair + 1] if 2 * pair + 1 < OFFSETS else coarse_weight[...]
        cuts = [slice(t * quarter, (t + 1) * quarter) for t in range(4)]
        tiles = [jnp.concatenate([first[:, c], second[:, c]], axis=1) for c in cuts]
        for step in range(4):
            target = lax.rem(place[0] + step, 4)
            low = jnp.where(target == 0, tiles[0], tiles[1])
            high = jnp.where(target == 2, tiles[2], tiles[3])
            pieces[step * PAIRS + pair] = jnp.where(target < 2, low, high)


def join_kernel(piece0, piece1, piece2, piece3, weight, flipped):
    for pair in range(PAIRS):
        tile = jnp.concatenate([p[pair] for p in (piece0, piece1, piece2, piece3)], axis=0)
        weight[:, pair * BLOCK : (pair + 1) * BLOCK] = tile
        flipped[pair * BLOCK : (pair + 1) * BLOCK, :] = tile.T


def fill_table(features, incoming, table, nblocks):
    for block in range(nblocks):
        table[block] = features[:, block * BLOCK : (block + 1) * BLOCK]
    table[nblocks : nblocks + incoming.shape[0]] = incoming[...]
    table[nblocks + incoming.shape[0]] = jnp.zeros(table.shape[1:], BF)


def slot(neighbour, offset, block, extent):
    named = neighbour[offset, block]
    return jnp.where(named < 0, extent, named)


def fill_gathered(neighbour, table, gathered, first, extent):
    quarter = table.shape[1]
    nblocks = gathered.shape[1] // BLOCK

    def step(offset, carry):
        rows = pl.ds(pl.multiple_of(offset * quarter, quarter), quarter)
        for block in range(nblocks):
            picked = table[slot(neighbour, offset, first + block, extent)]
            gathered[rows, block * BLOCK : (block + 1) * BLOCK] = picked
        return carry

    lax.fori_loop(0, OFFSETS, step, 0, unroll=27)
    mean = mean_matrix()
    for block in range(nblocks):
        pooled = jnp.dot(table[first + block], mean, preferred_element_type=F32).astype(BF)
        gathered[OFFSETS * quarter :, block * BLOCK : (block + 1) * BLOCK] = pooled


def forward_kernel(
    half, neighbour, features, incoming, weight, out0, out1, out2, out3, table, gathered
):
    quarter, row_count = features.shape
    nblocks = row_count // BLOCK
    extent = nblocks + incoming.shape[0]
    fill_table(features, incoming, table, nblocks)
    fill_gathered(neighbour, table, gathered, half * nblocks // 2, extent)
    for tile in range(row_count // 512):
        cut = slice(tile * 256, (tile + 1) * 256)
        total = jnp.dot(weight[...], gathered[:, cut], preferred_element_type=F32)
        for step, out in enumerate((out0, out1, out2, out3)):
            out[:, cut] = total[step * quarter : (step + 1) * quarter].astype(out.dtype)


def activate(own, part1, part2, part3, out_grad):
    pre = (own[...] + part1[...].astype(F32)) + (part2[...].astype(F32) + part3[...].astype(F32))
    sigma = 1.0 / (1.0 + jnp.exp(-pre))
    grad = out_grad.astype(F32) * sigma * (1.0 + pre * (1.0 - sigma))
    return (pre * sigma).astype(BF), grad.astype(BF)


def activation_kernel(own, part1, part2, part3, out_grad, output, grad):
    middle = own.shape[1]
    output[...], grad[...] = activate(own, part1, part2, part3, out_grad[:, :middle])


def activation_end_kernel(own, part1, part2, part3, out_grad, before, output, grad):
    middle = own.shape[1]
    output[:, :middle] = before[...]
    output[:, middle:], grad[...] = activate(own, part1, part2, part3, out_grad[:, middle:])


def prepare_weight(half, neighbour, features, incoming, grads, table, gathered, flipped):
    nblocks = features.shape[1] // BLOCK
    extent = nblocks + incoming.shape[0]
    fill_table(features, incoming, table, nblocks)
    fill_gathered(neighbour, table, gathered, half * nblocks // 2, extent)
    for block in range(nblocks // 2):
        cut = slice(block * BLOCK, (block + 1) * BLOCK)
        tall = jnp.concatenate([g[:, cut] for g in grads], axis=0)
        flipped[cut, :] = tall.T


def weight_first_kernel(
    neighbour, features, incoming, grad0, grad1, grad2, grad3, held, table, gathered, flipped
):
    grads = (grad0, grad1, grad2, grad3)
    prepare_weight(0, neighbour, features, incoming, grads, table, gathered, flipped)
    held[...] = jnp.dot(gathered[...], flipped[...], preferred_element_type=F32)


def weight_second_kernel(
    core, neighbour, features, incoming, grad0, grad1, grad2, grad3, held, keep, give, table, gathered, flipped
):
    quarter = features.shape[0]
    grads = (grad0, grad1, grad2, grad3)
    prepare_weight(1, neighbour, features, incoming, grads, table, gathered, flipped)
    half = quarter // 2
    for pair in range(PAIRS):
        rows = slice(pair * BLOCK, (pair + 1) * BLOCK)
        product = jnp.dot(gathered[rows, :], flipped[...], preferred_element_type=F32)
        upright = (product + held[rows, :]).T
        for step in range(4):
            low = upright[step * quarter : step * quarter + half]
            high = upright[step * quarter + half : (step + 1) * quarter]
            keep[pair, step] = jnp.where(core[0] == 0, low, high)
            give[pair, step] = jnp.where(core[0] == 0, high, low).astype(BF)


def pair_kernel(keep, arrived, parts):
    parts[:PAIRS] = (keep[...] + arrived[...].astype(F32)).astype(BF)
    parts[PAIRS:] = jnp.zeros((parts.shape[0] - PAIRS,) + parts.shape[1:], BF)


def table_kernel(
    neighbour, weight_t, g00, g01, g02, g03, g10, g11, g12, g13, after, local, returned, total, spread
):
    del after
    quarter, row_count = local.shape
    nblocks = row_count // BLOCK
    extent = nblocks + returned.shape[0]
    total[...] = jnp.zeros_like(total)
    mean = mean_matrix()
    for tile in range(nblocks // 2):
        grads = (g00, g01, g02, g03) if tile < nblocks // 4 else (g10, g11, g12, g13)
        start = tile % (nblocks // 4) * 256
        tall = jnp.concatenate([g[:, start : start + 256] for g in grads], axis=0)
        product = jnp.dot(weight_t[...], tall, preferred_element_type=F32)
        spread[...] = product[: OFFSETS * quarter]

        def step(offset, carry, tile=tile):
            rows = pl.ds(pl.multiple_of(offset * quarter, quarter), quarter)
            for side in range(2):
                place = slot(neighbour, offset, 2 * tile + side, extent)
                total[place] += spread[rows, side * BLOCK : (side + 1) * BLOCK]
            return carry

        lax.fori_loop(0, OFFSETS, step, 0, unroll=27)
        coarse = product[OFFSETS * quarter :]
        for side in range(2):
            value = coarse[:, side * BLOCK : (side + 1) * BLOCK]
            high = value.astype(BF)
            low = (value - high.astype(F32)).astype(BF)
            total[2 * tile + side] += jnp.dot(high, mean, preferred_element_type=F32) + jnp.dot(
                low, mean, preferred_element_type=F32
            )
    for block in range(nblocks):
        local[:, block * BLOCK : (block + 1) * BLOCK] = total[block]
    returned[...] = total[nblocks:extent].astype(BF)


def return_kernel(send_block, send_count, local, returned, input_grad):
    input_grad[...] = local[...]
    for peer in range(returned.shape[0]):
        factor = send_count[0, peer].astype(F32)
        input_grad[:, columns(send_block[0, peer])] += returned[peer].astype(F32) * factor


def sum_kernel(scale, parts, after, own, sent1, sent2, sent3):
    del after
    total = parts[0].astype(F32)
    for source in range(1, parts.shape[0]):
        total = total + parts[source].astype(F32)
    total = total * scale
    own[...] = total[0]
    sent1[...] = total[1].astype(BF)
    sent2[...] = total[2].astype(BF)
    sent3[...] = total[3].astype(BF)


def assemble_kernel(place, own, part1, part2, part3, chunk):
    quarter = own.shape[1] // 2
    pieces = (own[...], part1[...].astype(F32), part2[...].astype(F32), part3[...].astype(F32))
    for side in range(2):
        cut = slice(side * quarter, (side + 1) * quarter)
        columns_of = []
        for source in range(4):
            step = lax.rem(source - place[0] + 4, 4)
            low = jnp.where(step == 0, pieces[0][:, cut], pieces[1][:, cut])
            high = jnp.where(step == 2, pieces[2][:, cut], pieces[3][:, cut])
            columns_of.append(jnp.where(step < 2, low, high))
        chunk[side] = jnp.concatenate(columns_of, axis=1).astype(BF)


def unpack_kernel(chip, *refs):
    conv_grad, coarse_grad = refs[-2:]
    half = refs[0].shape[2]
    core = chip[2]
    for index, ref in enumerate(refs[:-2]):
        side = core if index < 4 else 1 - core
        rows = pl.ds(pl.multiple_of(side * half, half), half)
        for step in range(4):
            source_y = lax.rem(chip[0] - step + 4, 4)
            source_x = lax.rem(chip[1] - index % 4 + 4, 4)
            pair = source_y * 4 + source_x

            @pl.when(pair < PAIRS)
            def _(ref=ref, step=step, pair=pair, rows=rows):
                conv_grad[2 * pair, rows, :] = ref[step, 0].astype(F32)

            @pl.when(pair < PAIRS - 1)
            def _(ref=ref, step=step, pair=pair, rows=rows):
                conv_grad[2 * pair + 1, rows, :] = ref[step, 1].astype(F32)

            @pl.when(pair == PAIRS - 1)
            def _(ref=ref, step=step, rows=rows):
                coarse_grad[rows, :] = ref[step, 1].astype(F32)


def shift(value, axis, step):
    size = lax.axis_size(axis)
    return lax.ppermute(value, axis, [(i, (i + step) % size) for i in range(size)])


def move(value, step_y, step_x, flip):
    moves = []
    for y in range(4):
        for x in range(4):
            for core in range(2):
                target = ((y + step_y) % 4 * 4 + (x + step_x) % 4) * 2 + (core ^ flip)
                moves.append(((y * 4 + x) * 2 + core, target))
    return lax.ppermute(value, "morton", moves)


def local_step(features, conv_weight, coarse_weight, out_grad, send_block, send_count, neighbour):
    n_morton = lax.axis_size("morton")
    quarter, row_count = features.shape
    channels = conv_weight.shape[2]
    nblocks = row_count // BLOCK
    extent = nblocks + n_morton
    depth = TERMS * quarter
    flops = 2 * depth * channels * row_count
    place = lax.axis_index("chan").astype(jnp.int32).reshape(1)
    spot = lax.axis_index("morton").astype(jnp.int32)
    chip = jnp.stack([spot // 8, spot // 2 % 4, spot % 2])
    core = (spot % 2).reshape(1)
    shape = jax.ShapeDtypeStruct

    pieces = call(
        split_kernel, "split", shape((4 * PAIRS, quarter, BLOCK), BF), "svv", size=2 << 20
    )(place, conv_weight, coarse_weight)
    outgoing = call(
        pack_kernel, "pack", shape((n_morton, quarter, BLOCK), BF), "ssv", size=1 << 20
    )(send_block, send_count, features)
    incoming = lax.all_to_all(outgoing, "morton", 0, 0, tiled=True)

    pieces = pieces.reshape(4, PAIRS, quarter, BLOCK)
    weights = [pieces[0]] + [shift(pieces[s], "chan", s) for s in (1, 2, 3)]
    weight, weight_t = call(
        join_kernel,
        "join",
        [shape((channels, depth), BF), shape((depth, channels), BF)],
        "vvvv",
        size=3 << 20,
    )(*weights)

    middle = row_count // 2
    big = [pltpu.VMEM((extent + 1, quarter, BLOCK), BF), pltpu.VMEM((depth, middle), BF)]
    turned = [pltpu.VMEM((middle, channels), BF)]
    wide, part = (quarter, row_count), (quarter, middle)
    grads = []
    output = ()
    for half in range(2):
        partial = call(
            functools.partial(forward_kernel, half),
            f"forward{half}",
            [shape(part, F32)] + [shape(part, BF)] * 3,
            "svvv",
            big,
            flops // 2,
            3 << 20,
        )(neighbour, features, incoming, weight)
        arrived = [shift(partial[s], "chan", -s) for s in (1, 2, 3)]
        output, grad = call(
            activation_end_kernel if half else activation_kernel,
            f"activation{half}",
            [shape(wide if half else part, BF), shape(part, BF)],
            "vvvvvv" if half else "vvvvv",
            size=1 << 20,
        )(partial[0], *arrived, out_grad, *((output,) if half else ()))
        grads.append([grad] + [shift(grad, "chan", s) for s in (1, 2, 3)])

    held = call(
        weight_first_kernel,
        "weight_grad0",
        shape((depth, channels), F32),
        "svvvvvv",
        big + turned,
        flops // 2,
        4 << 20,
    )(neighbour, features, incoming, *grads[0])
    piece = (4, quarter // 2, BLOCK)
    keep, give = call(
        weight_second_kernel,
        "weight_grad1",
        [shape((PAIRS,) + piece, F32), shape((PAIRS,) + piece, BF)],
        "ssvvvvvvv",
        big + turned,
        flops // 2,
        4 << 20,
    )(core, neighbour, features, incoming, *grads[1], held)
    chips = n_morton // 2
    parts = call(pair_kernel, "pair_sum", shape((chips,) + piece, BF), "vv", size=3 << 20)(
        keep, move(give, 0, 0, 1)
    )
    same_core = [[2 * c + side for c in range(chips)] for side in range(2)]
    received = lax.all_to_all(
        parts, "morton", 0, 0, axis_index_groups=same_core, tiled=True
    )

    local, outward = call(
        table_kernel,
        "table_grad",
        [shape(wide, F32), shape((n_morton, quarter, BLOCK), BF)],
        "s" + "v" * 9 + "a",
        [
            pltpu.VMEM((extent + 1, quarter, BLOCK), F32),
            pltpu.VMEM((OFFSETS * quarter, 256), F32),
        ],
        flops,
        4 << 20,
    )(neighbour, weight_t, *grads[0], *grads[1], parts)
    returned = lax.all_to_all(outward, "morton", 0, 0, tiled=True)
    input_grad = call(return_kernel, "return_add", shape(wide, F32), "ssvv", size=2 << 20)(
        send_block, send_count, local, returned
    )

    scale = float(row_count * n_morton) ** (-0.5)
    small = piece[1:]
    own, *sent = call(
        functools.partial(sum_kernel, scale),
        "sum_parts",
        [shape(small, F32)] + [shape(small, BF)] * 3,
        "va",
        size=1 << 20,
    )(received, outward)
    sent = [shift(value, "chan", -step) for step, value in zip((1, 2, 3), sent)]
    chunk = call(
        assemble_kernel, "assemble", shape((2, quarter // 2, channels), BF), "svvvv", size=1 << 17
    )(place, own, *sent)
    column = jnp.stack([chunk] + [move(chunk, step, 0, 0) for step in (1, 2, 3)])
    mine = [column] + [move(column, 0, step, 0) for step in (1, 2, 3)]
    other = [move(value, 0, 0, 1) for value in mine]
    conv_grad, coarse_grad = call(
        unpack_kernel,
        "unpack",
        [shape((OFFSETS, quarter, channels), F32), shape((quarter, channels), F32)],
        "s" + "v" * 8,
        size=3 << 20,
    )(chip, *mine, *other)
    return output, input_grad, conv_grad, coarse_grad


def solution(mesh):
    placed = (
        P("chan", "morton"),
        P(None, "chan", None),
        P("chan", None),
        P("chan", "morton"),
        P("morton", None),
        P("morton", None),
        P(None, "morton"),
    )
    return jax.shard_map(
        local_step,
        mesh=mesh,
        in_specs=placed,
        out_specs=(
            P("chan", "morton"),
            P("chan", "morton"),
            P(None, "chan", None),
            P("chan", None),
        ),
        check_vma=False,
    )
```

```python
import functools

import jax
import jax.numpy as jnp
from jax import lax
from jax.experimental import pallas as pl
from jax.experimental.pallas import tpu as pltpu
from jax.sharding import PartitionSpec as P

OFFSETS = 27
TERMS = 28
PAIRS = TERMS // 2
BLOCK = 128
BF = jnp.bfloat16
F32 = jnp.float32


def call(kernel, name, outs, kinds, scratch=(), flops=0, size=0, limit=24 << 20):
    space = {"s": pltpu.SMEM, "v": pltpu.VMEM, "a": pl.ANY}
    many = isinstance(outs, (list, tuple))
    spec = pl.BlockSpec(memory_space=pltpu.VMEM)
    return pl.pallas_call(
        kernel,
        name=name,
        out_shape=outs,
        in_specs=[pl.BlockSpec(memory_space=space[k]) for k in kinds],
        out_specs=[spec] * len(outs) if many else spec,
        scratch_shapes=list(scratch),
        compiler_params=pltpu.CompilerParams(vmem_limit_bytes=limit),
        cost_estimate=pl.CostEstimate(flops=flops, bytes_accessed=size, transcendentals=0),
    )


def mean_matrix():
    row = lax.broadcasted_iota(jnp.int32, (BLOCK, BLOCK), 0) // 8
    column = lax.broadcasted_iota(jnp.int32, (BLOCK, BLOCK), 1) // 8
    return jnp.where(row == column, 0.125, 0.0).astype(BF)


def columns(index):
    return pl.ds(pl.multiple_of(index * BLOCK, BLOCK), BLOCK)


def pack_kernel(send_block, send_count, features, outgoing):
    for peer in range(outgoing.shape[0]):
        block = features[:, columns(send_block[0, peer])]
        outgoing[peer] = block * send_count[0, peer].astype(F32).astype(BF)


def split_kernel(place, conv_weight, coarse_weight, pieces):
    quarter = conv_weight.shape[1]
    for pair in range(PAIRS):
        first = conv_weight[2 * pair]
        second = conv_weight[2 * pair + 1] if 2 * pair + 1 < OFFSETS else coarse_weight[...]
        cuts = [slice(t * quarter, (t + 1) * quarter) for t in range(4)]
        tiles = [jnp.concatenate([first[:, c], second[:, c]], axis=1) for c in cuts]
        for step in range(4):
            target = lax.rem(place[0] + step, 4)
            low = jnp.where(target == 0, tiles[0], tiles[1])
            high = jnp.where(target == 2, tiles[2], tiles[3])
            pieces[step * PAIRS + pair] = jnp.where(target < 2, low, high)


def join_kernel(piece0, piece1, piece2, piece3, after, flipped):
    del after
    for pair in range(PAIRS):
        tile = jnp.concatenate([p[pair] for p in (piece0, piece1, piece2, piece3)], axis=0)
        flipped[pair * BLOCK : (pair + 1) * BLOCK, :] = tile.T


def fill_table(features, incoming, table, nblocks):
    for block in range(nblocks):
        table[block] = features[:, block * BLOCK : (block + 1) * BLOCK]
    table[nblocks : nblocks + incoming.shape[0]] = incoming[...]
    table[nblocks + incoming.shape[0]] = jnp.zeros(table.shape[1:], BF)


def slot(neighbour, offset, block, extent):
    named = neighbour[offset, block]
    return jnp.where(named < 0, extent, named)


def fill_gathered(neighbour, table, gathered, first, extent):
    quarter = table.shape[1]
    nblocks = gathered.shape[1] // BLOCK

    def step(offset, carry):
        rows = pl.ds(pl.multiple_of(offset * quarter, quarter), quarter)
        for block in range(nblocks):
            picked = table[slot(neighbour, offset, first + block, extent)]
            gathered[rows, block * BLOCK : (block + 1) * BLOCK] = picked
        return carry

    lax.fori_loop(0, OFFSETS, step, 0, unroll=27)
    mean = mean_matrix()
    for block in range(nblocks):
        pooled = jnp.dot(table[first + block], mean, preferred_element_type=F32).astype(BF)
        gathered[OFFSETS * quarter :, block * BLOCK : (block + 1) * BLOCK] = pooled


def forward_kernel(half, neighbour, features, incoming, *refs):
    pieces, outs, (weight, table, gathered) = refs[:4], refs[4:8], refs[8:]
    quarter, row_count = features.shape
    nblocks = row_count // BLOCK
    extent = nblocks + incoming.shape[0]
    for step, piece in enumerate(pieces):
        for pair in range(PAIRS):
            rows = slice(step * quarter, (step + 1) * quarter)
            weight[rows, pair * BLOCK : (pair + 1) * BLOCK] = piece[pair]
    fill_table(features, incoming, table, nblocks)
    fill_gathered(neighbour, table, gathered, half * nblocks // 2, extent)
    for tile in range(row_count // 512):
        cut = slice(tile * 256, (tile + 1) * 256)
        total = jnp.dot(weight[...], gathered[:, cut], preferred_element_type=F32)
        for step, out in enumerate(outs):
            out[:, cut] = total[step * quarter : (step + 1) * quarter].astype(out.dtype)


def activate(own, part1, part2, part3, out_grad):
    pre = (own[...] + part1[...].astype(F32)) + (part2[...].astype(F32) + part3[...].astype(F32))
    sigma = 1.0 / (1.0 + jnp.exp(-pre))
    grad = out_grad.astype(F32) * sigma * (1.0 + pre * (1.0 - sigma))
    return (pre * sigma).astype(BF), grad.astype(BF)


def activation_kernel(own, part1, part2, part3, out_grad, output, grad):
    middle = own.shape[1]
    output[...], grad[...] = activate(own, part1, part2, part3, out_grad[:, :middle])


def activation_end_kernel(own, part1, part2, part3, out_grad, before, output, grad):
    middle = own.shape[1]
    output[:, :middle] = before[...]
    output[:, middle:], grad[...] = activate(own, part1, part2, part3, out_grad[:, middle:])


def prepare_weight(half, neighbour, features, incoming, grads, table, gathered, flipped):
    nblocks = features.shape[1] // BLOCK
    extent = nblocks + incoming.shape[0]
    fill_table(features, incoming, table, nblocks)
    fill_gathered(neighbour, table, gathered, half * nblocks // 2, extent)
    for block in range(nblocks // 2):
        cut = slice(block * BLOCK, (block + 1) * BLOCK)
        tall = jnp.concatenate([g[:, cut] for g in grads], axis=0)
        flipped[cut, :] = tall.T


def weight_first_kernel(
    neighbour, features, incoming, grad0, grad1, grad2, grad3, held, table, gathered, flipped
):
    grads = (grad0, grad1, grad2, grad3)
    prepare_weight(0, neighbour, features, incoming, grads, table, gathered, flipped)
    held[...] = jnp.dot(gathered[...], flipped[...], preferred_element_type=F32)


def weight_second_kernel(
    core, neighbour, features, incoming, grad0, grad1, grad2, grad3, held, keep, give, table, gathered, flipped
):
    quarter = features.shape[0]
    grads = (grad0, grad1, grad2, grad3)
    prepare_weight(1, neighbour, features, incoming, grads, table, gathered, flipped)
    half = quarter // 2
    for pair in range(PAIRS):
        rows = slice(pair * BLOCK, (pair + 1) * BLOCK)
        product = jnp.dot(gathered[rows, :], flipped[...], preferred_element_type=F32)
        upright = (product + held[rows, :]).T
        for step in range(4):
            low = upright[step * quarter : step * quarter + half]
            high = upright[step * quarter + half : (step + 1) * quarter]
            keep[pair, step] = jnp.where(core[0] == 0, low, high)
            give[pair, step] = jnp.where(core[0] == 0, high, low).astype(BF)


def pair_kernel(place, keep, arrived, parts):
    for step in range(4):
        target = lax.rem(place[0] - step + 4, 4)
        for pair in range(PAIRS):
            parts[pair, target] = (keep[pair, step] + arrived[pair, step].astype(F32)).astype(BF)
    for spare in range(PAIRS, parts.shape[0]):
        parts[spare] = jnp.zeros(parts.shape[1:], BF)


def peer_at(chip, step_y, step_x, flip):
    y = lax.rem(chip[0] + step_y + 4, 4)
    x = lax.rem(chip[1] + step_x + 4, 4)
    return (y * 4 + x) * 2 + (1 - chip[2] if flip else chip[2])


def table_kernel(
    chip, neighbour, weight_t, g00, g01, g02, g03, g10, g11, g12, g13, after, local, home, away, total, spread
):
    del after
    quarter, row_count = local.shape
    nblocks = row_count // BLOCK
    extent = total.shape[0] - 1
    total[...] = jnp.zeros_like(total)
    mean = mean_matrix()
    for tile in range(nblocks // 2):
        grads = (g00, g01, g02, g03) if tile < nblocks // 4 else (g10, g11, g12, g13)
        start = tile % (nblocks // 4) * 256
        tall = jnp.concatenate([g[:, start : start + 256] for g in grads], axis=0)
        product = jnp.dot(weight_t[...], tall, preferred_element_type=F32)
        spread[...] = product[: OFFSETS * quarter]

        def step(offset, carry, tile=tile):
            rows = pl.ds(pl.multiple_of(offset * quarter, quarter), quarter)
            for side in range(2):
                place = slot(neighbour, offset, 2 * tile + side, extent)
                total[place] += spread[rows, side * BLOCK : (side + 1) * BLOCK]
            return carry

        lax.fori_loop(0, OFFSETS, step, 0, unroll=27)
        coarse = product[OFFSETS * quarter :]
        for side in range(2):
            value = coarse[:, side * BLOCK : (side + 1) * BLOCK]
            high = value.astype(BF)
            low = (value - high.astype(F32)).astype(BF)
            total[2 * tile + side] += jnp.dot(high, mean, preferred_element_type=F32) + jnp.dot(
                low, mean, preferred_element_type=F32
            )
    for block in range(nblocks):
        local[:, block * BLOCK : (block + 1) * BLOCK] = total[block]
    for flip, out in enumerate((home, away)):
        for x in range(4):
            for y in range(4):
                out[x, y] = total[nblocks + peer_at(chip, y, x, flip)].astype(BF)


def by_x_kernel(home, away, *outs):
    for x, out in enumerate(outs):
        for y in range(4):
            out[y, 0] = home[x, y]
            out[y, 1] = away[x, y]


def by_y_kernel(*refs):
    for y, out in enumerate(refs[4:]):
        for x, ref in enumerate(refs[:4]):
            out[x] = ref[y]


def return_kernel(chip, send_block, send_count, local, from0, from1, from2, from3, input_grad):
    input_grad[...] = local[...]
    for y, ref in enumerate((from0, from1, from2, from3)):
        for x in range(4):
            for flip in range(2):
                peer = peer_at(chip, -y, -x, flip)
                factor = send_count[0, peer].astype(F32)
                input_grad[:, columns(send_block[0, peer])] += ref[x, flip].astype(F32) * factor


def sum_kernel(scale, parts, after, chunks):
    del after
    half = parts.shape[3] // 2
    total = parts[0].astype(F32)
    for source in range(1, parts.shape[0]):
        total = total + parts[source].astype(F32)
    total = total * scale
    for side in range(2):
        cut = slice(side * half, (side + 1) * half)
        value = jnp.concatenate([total[c, :, cut] for c in range(4)], axis=1).astype(BF)
        for target in range(chunks.shape[0]):
            chunks[target, side] = value


def unpack_kernel(core, mine, other, conv_grad, coarse_grad):
    half = mine.shape[2]
    for chunks, side in ((mine, core[0]), (other, 1 - core[0])):
        rows = pl.ds(pl.multiple_of(side * half, half), half)
        for offset in range(TERMS):
            value = chunks[offset // 2, offset % 2].astype(F32)
            if offset < OFFSETS:
                conv_grad[offset, rows, :] = value
            else:
                coarse_grad[rows, :] = value


def shift(value, axis, step):
    size = lax.axis_size(axis)
    return lax.ppermute(value, axis, [(i, (i + step) % size) for i in range(size)])


def move(value, step_y, step_x, flip):
    moves = []
    for y in range(4):
        for x in range(4):
            for core in range(2):
                target = ((y + step_y) % 4 * 4 + (x + step_x) % 4) * 2 + (core ^ flip)
                moves.append(((y * 4 + x) * 2 + core, target))
    return lax.ppermute(value, "morton", moves)


def local_step(features, conv_weight, coarse_weight, out_grad, send_block, send_count, neighbour):
    n_morton = lax.axis_size("morton")
    quarter, row_count = features.shape
    channels = conv_weight.shape[2]
    nblocks = row_count // BLOCK
    extent = nblocks + n_morton
    depth = TERMS * quarter
    flops = 2 * depth * channels * row_count
    place = lax.axis_index("chan").astype(jnp.int32).reshape(1)
    spot = lax.axis_index("morton").astype(jnp.int32)
    chip = jnp.stack([spot // 8, spot // 2 % 4, spot % 2])
    core = (spot % 2).reshape(1)
    shape = jax.ShapeDtypeStruct

    pieces = call(
        split_kernel, "split", shape((4 * PAIRS, quarter, BLOCK), BF), "svv", size=2 << 20
    )(place, conv_weight, coarse_weight)
    outgoing = call(
        pack_kernel, "pack", shape((n_morton, quarter, BLOCK), BF), "ssv", size=1 << 20
    )(send_block, send_count, features)
    incoming = lax.all_to_all(outgoing, "morton", 0, 0, tiled=True)

    pieces = pieces.reshape(4, PAIRS, quarter, BLOCK)
    weights = [pieces[0]] + [shift(pieces[s], "chan", s) for s in (1, 2, 3)]
    middle = row_count // 2
    big = [pltpu.VMEM((extent + 1, quarter, BLOCK), BF), pltpu.VMEM((depth, middle), BF)]
    turned = [pltpu.VMEM((middle, channels), BF)]
    wide, part = (quarter, row_count), (quarter, middle)
    grads = []
    output = ()
    for half in range(2):
        partial = call(
            functools.partial(forward_kernel, half),
            f"forward{half}",
            [shape(part, F32)] + [shape(part, BF)] * 3,
            "svvvvvv",
            [pltpu.VMEM((channels, depth), BF)] + big,
            flops // 2,
            3 << 20,
        )(neighbour, features, incoming, *weights)
        arrived = [shift(partial[s], "chan", -s) for s in (1, 2, 3)]
        output, grad = call(
            activation_end_kernel if half else activation_kernel,
            f"activation{half}",
            [shape(wide if half else part, BF), shape(part, BF)],
            "vvvvvv" if half else "vvvvv",
            size=1 << 20,
        )(partial[0], *arrived, out_grad, *((output,) if half else ()))
        grads.append([grad] + [shift(grad, "chan", s) for s in (1, 2, 3)])

    weight_t = call(join_kernel, "join", shape((depth, channels), BF), "vvvva", size=3 << 20)(
        *weights, grads[0][0]
    )
    held = call(
        weight_first_kernel,
        "weight_grad0",
        shape((depth, channels), F32),
        "svvvvvv",
        big + turned,
        flops // 2,
        4 << 20,
    )(neighbour, features, incoming, *grads[0])
    piece = (4, quarter // 2, BLOCK)
    keep, give = call(
        weight_second_kernel,
        "weight_grad1",
        [shape((PAIRS,) + piece, F32), shape((PAIRS,) + piece, BF)],
        "ssvvvvvvv",
        big + turned,
        flops // 2,
        4 << 20,
    )(core, neighbour, features, incoming, *grads[1], held)
    chips = n_morton // 2
    parts = call(pair_kernel, "pair_sum", shape((chips,) + piece, BF), "svv", size=3 << 20)(
        place, keep, move(give, 0, 0, 1)
    )
    same_core = [[2 * c + side for c in range(chips)] for side in range(2)]
    same_core_all = [[device * 4 + z for device in group for z in range(4)] for group in same_core]
    received = lax.all_to_all(
        parts.reshape((4 * chips,) + piece[1:]),
        ("morton", "chan"),
        0,
        0,
        axis_index_groups=same_core_all,
        tiled=True,
    ).reshape(parts.shape)

    blocks = (4, 4, quarter, BLOCK)
    local, home, away = call(
        table_kernel,
        "table_grad",
        [shape(wide, F32), shape(blocks, BF), shape(blocks, BF)],
        "ss" + "v" * 9 + "a",
        [
            pltpu.VMEM((extent + 1, quarter, BLOCK), F32),
            pltpu.VMEM((OFFSETS * quarter, 256), F32),
        ],
        flops,
        4 << 20,
    )(chip, neighbour, weight_t, *grads[0], *grads[1], parts)
    bundle = [shape((4, 2, quarter, BLOCK), BF)] * 4
    along_x = call(by_x_kernel, "by_x", bundle, "vv", size=1 << 20)(home, move(away, 0, 0, 1))
    along_x = [along_x[0]] + [move(along_x[step], 0, step, 0) for step in (1, 2, 3)]
    along_y = call(by_y_kernel, "by_y", bundle, "vvvv", size=1 << 20)(*along_x)
    along_y = [along_y[0]] + [move(along_y[step], step, 0, 0) for step in (1, 2, 3)]
    input_grad = call(return_kernel, "return_add", shape(wide, F32), "sssvvvvv", size=2 << 20)(
        chip, send_block, send_count, local, *along_y
    )

    scale = float(row_count * n_morton) ** (-0.5)
    chunks = call(
        functools.partial(sum_kernel, scale),
        "sum_parts",
        shape((chips, 2, quarter // 2, channels), BF),
        "va",
        size=1 << 20,
    )(received, home)
    mine = lax.all_to_all(chunks, "morton", 0, 0, axis_index_groups=same_core, tiled=True)
    conv_grad, coarse_grad = call(
        unpack_kernel,
        "unpack",
        [shape((OFFSETS, quarter, channels), F32), shape((quarter, channels), F32)],
        "svv",
        size=3 << 20,
    )(core, mine, move(mine, 0, 0, 1))
    return output, input_grad, conv_grad, coarse_grad


def solution(mesh):
    placed = (
        P("chan", "morton"),
        P(None, "chan", None),
        P("chan", None),
        P("chan", "morton"),
        P("morton", None),
        P("morton", None),
        P(None, "morton"),
    )
    return jax.shard_map(
        local_step,
        mesh=mesh,
        in_specs=placed,
        out_specs=(
            P("chan", "morton"),
            P("chan", "morton"),
            P(None, "chan", None),
            P("chan", None),
        ),
        check_vma=False,
    )
```

```python
import functools

import jax
import jax.numpy as jnp
from jax import lax
from jax.experimental import pallas as pl
from jax.experimental.pallas import tpu as pltpu
from jax.sharding import PartitionSpec as P

OFFSETS = 27
TERMS = 28
PAIRS = TERMS // 2
BLOCK = 128
BF = jnp.bfloat16
F32 = jnp.float32


def call(kernel, name, outs, kinds, scratch=(), flops=0, size=0, limit=24 << 20):
    space = {"s": pltpu.SMEM, "v": pltpu.VMEM, "a": pl.ANY}
    many = isinstance(outs, (list, tuple))
    spec = pl.BlockSpec(memory_space=pltpu.VMEM)
    return pl.pallas_call(
        kernel,
        name=name,
        out_shape=outs,
        in_specs=[pl.BlockSpec(memory_space=space[k]) for k in kinds],
        out_specs=[spec] * len(outs) if many else spec,
        scratch_shapes=list(scratch),
        compiler_params=pltpu.CompilerParams(vmem_limit_bytes=limit),
        cost_estimate=pl.CostEstimate(flops=flops, bytes_accessed=size, transcendentals=0),
    )


def mean_matrix():
    row = lax.broadcasted_iota(jnp.int32, (BLOCK, BLOCK), 0) // 8
    column = lax.broadcasted_iota(jnp.int32, (BLOCK, BLOCK), 1) // 8
    return jnp.where(row == column, 0.125, 0.0).astype(BF)


def columns(index):
    return pl.ds(pl.multiple_of(index * BLOCK, BLOCK), BLOCK)


def pack_kernel(send_block, send_count, features, outgoing):
    for peer in range(outgoing.shape[0]):
        block = features[:, columns(send_block[0, peer])]
        outgoing[peer] = block * send_count[0, peer].astype(F32).astype(BF)


def split_kernel(place, conv_weight, coarse_weight, pieces):
    quarter = conv_weight.shape[1]
    for pair in range(PAIRS):
        first = conv_weight[2 * pair]
        second = conv_weight[2 * pair + 1] if 2 * pair + 1 < OFFSETS else coarse_weight[...]
        cuts = [slice(t * quarter, (t + 1) * quarter) for t in range(4)]
        tiles = [jnp.concatenate([first[:, c], second[:, c]], axis=1) for c in cuts]
        for step in range(4):
            target = lax.rem(place[0] + step, 4)
            low = jnp.where(target == 0, tiles[0], tiles[1])
            high = jnp.where(target == 2, tiles[2], tiles[3])
            pieces[step * PAIRS + pair] = jnp.where(target < 2, low, high)


def join_kernel(piece0, piece1, piece2, piece3, after, flipped):
    del after
    for pair in range(PAIRS):
        tile = jnp.concatenate([p[pair] for p in (piece0, piece1, piece2, piece3)], axis=0)
        flipped[pair * BLOCK : (pair + 1) * BLOCK, :] = tile.T


def fill_table(features, incoming, table, nblocks):
    for block in range(nblocks):
        table[block] = features[:, block * BLOCK : (block + 1) * BLOCK]
    table[nblocks : nblocks + incoming.shape[0]] = incoming[...]
    table[nblocks + incoming.shape[0]] = jnp.zeros(table.shape[1:], BF)


def slot(neighbour, offset, block, extent):
    named = neighbour[offset, block]
    return jnp.where(named < 0, extent, named)


def fill_gathered(neighbour, table, gathered, first, extent):
    quarter = table.shape[1]
    nblocks = gathered.shape[1] // BLOCK

    def step(offset, carry):
        rows = pl.ds(pl.multiple_of(offset * quarter, quarter), quarter)
        for block in range(nblocks):
            picked = table[slot(neighbour, offset, first + block, extent)]
            gathered[rows, block * BLOCK : (block + 1) * BLOCK] = picked
        return carry

    lax.fori_loop(0, OFFSETS, step, 0, unroll=27)
    mean = mean_matrix()
    for block in range(nblocks):
        pooled = jnp.dot(table[first + block], mean, preferred_element_type=F32).astype(BF)
        gathered[OFFSETS * quarter :, block * BLOCK : (block + 1) * BLOCK] = pooled


def forward_kernel(half, neighbour, features, incoming, *refs):
    pieces, outs, (weight, table, gathered) = refs[:4], refs[4:8], refs[8:]
    quarter, row_count = features.shape
    nblocks = row_count // BLOCK
    extent = nblocks + incoming.shape[0]
    for step, piece in enumerate(pieces):
        for pair in range(PAIRS):
            rows = slice(step * quarter, (step + 1) * quarter)
            weight[rows, pair * BLOCK : (pair + 1) * BLOCK] = piece[pair]
    fill_table(features, incoming, table, nblocks)
    fill_gathered(neighbour, table, gathered, half * nblocks // 2, extent)
    for tile in range(row_count // 512):
        cut = slice(tile * 256, (tile + 1) * 256)
        total = jnp.dot(weight[...], gathered[:, cut], preferred_element_type=F32)
        for step, out in enumerate(outs):
            out[:, cut] = total[step * quarter : (step + 1) * quarter].astype(out.dtype)


def activate(own, part1, part2, part3, out_grad):
    pre = (own[...] + part1[...].astype(F32)) + (part2[...].astype(F32) + part3[...].astype(F32))
    sigma = 1.0 / (1.0 + jnp.exp(-pre))
    grad = out_grad.astype(F32) * sigma * (1.0 + pre * (1.0 - sigma))
    return (pre * sigma).astype(BF), grad.astype(BF)


def activation_kernel(own, part1, part2, part3, out_grad, output, grad):
    middle = own.shape[1]
    output[...], grad[...] = activate(own, part1, part2, part3, out_grad[:, :middle])


def activation_end_kernel(own, part1, part2, part3, out_grad, before, output, grad):
    middle = own.shape[1]
    output[:, :middle] = before[...]
    output[:, middle:], grad[...] = activate(own, part1, part2, part3, out_grad[:, middle:])


def prepare_weight(half, neighbour, features, incoming, grads, table, gathered, flipped):
    nblocks = features.shape[1] // BLOCK
    extent = nblocks + incoming.shape[0]
    fill_table(features, incoming, table, nblocks)
    fill_gathered(neighbour, table, gathered, half * nblocks // 2, extent)
    for block in range(nblocks // 2):
        cut = slice(block * BLOCK, (block + 1) * BLOCK)
        tall = jnp.concatenate([g[:, cut] for g in grads], axis=0)
        flipped[cut, :] = tall.T


def weight_first_kernel(
    neighbour, features, incoming, grad0, grad1, grad2, grad3, held, table, gathered, flipped
):
    grads = (grad0, grad1, grad2, grad3)
    prepare_weight(0, neighbour, features, incoming, grads, table, gathered, flipped)
    held[...] = jnp.dot(gathered[...], flipped[...], preferred_element_type=F32)


def weight_second_kernel(
    core, neighbour, features, incoming, grad0, grad1, grad2, grad3, held, keep, give, table, gathered, flipped
):
    quarter = features.shape[0]
    grads = (grad0, grad1, grad2, grad3)
    prepare_weight(1, neighbour, features, incoming, grads, table, gathered, flipped)
    half = quarter // 2
    for pair in range(PAIRS):
        rows = slice(pair * BLOCK, (pair + 1) * BLOCK)
        product = jnp.dot(gathered[rows, :], flipped[...], preferred_element_type=F32)
        upright = (product + held[rows, :]).T
        for step in range(4):
            low = upright[step * quarter : step * quarter + half]
            high = upright[step * quarter + half : (step + 1) * quarter]
            keep[pair, step] = jnp.where(core[0] == 0, low, high)
            give[pair, step] = jnp.where(core[0] == 0, high, low).astype(BF)


def pair_kernel(place, keep, arrived, parts):
    for step in range(4):
        target = lax.rem(place[0] - step + 4, 4)
        for pair in range(PAIRS):
            parts[pair, target] = (keep[pair, step] + arrived[pair, step].astype(F32)).astype(BF)
    for spare in range(PAIRS, parts.shape[0]):
        parts[spare] = jnp.zeros(parts.shape[1:], BF)


def table_kernel(
    core, neighbour, weight_t, g00, g01, g02, g03, g10, g11, g12, g13, after, local, home, away, total, spread
):
    del after
    quarter, row_count = local.shape
    nblocks = row_count // BLOCK
    extent = total.shape[0] - 1
    total[...] = jnp.zeros_like(total)
    mean = mean_matrix()
    for tile in range(nblocks // 2):
        grads = (g00, g01, g02, g03) if tile < nblocks // 4 else (g10, g11, g12, g13)
        start = tile % (nblocks // 4) * 256
        tall = jnp.concatenate([g[:, start : start + 256] for g in grads], axis=0)
        product = jnp.dot(weight_t[...], tall, preferred_element_type=F32)
        spread[...] = product[: OFFSETS * quarter]

        def step(offset, carry, tile=tile):
            rows = pl.ds(pl.multiple_of(offset * quarter, quarter), quarter)
            for side in range(2):
                place = slot(neighbour, offset, 2 * tile + side, extent)
                total[place] += spread[rows, side * BLOCK : (side + 1) * BLOCK]
            return carry

        lax.fori_loop(0, OFFSETS, step, 0, unroll=27)
        coarse = product[OFFSETS * quarter :]
        for side in range(2):
            value = coarse[:, side * BLOCK : (side + 1) * BLOCK]
            high = value.astype(BF)
            low = (value - high.astype(F32)).astype(BF)
            total[2 * tile + side] += jnp.dot(high, mean, preferred_element_type=F32) + jnp.dot(
                low, mean, preferred_element_type=F32
            )
    for block in range(nblocks):
        local[:, block * BLOCK : (block + 1) * BLOCK] = total[block]
    for chip in range(home.shape[0]):
        home[chip] = total[nblocks + 2 * chip + core[0]].astype(BF)
        away[chip] = total[nblocks + 2 * chip + 1 - core[0]].astype(BF)


def return_kernel(core, send_block, send_count, local, mixed, input_grad):
    input_grad[...] = local[...]
    for chip in range(mixed.shape[0]):
        for flip in range(2):
            peer = 2 * chip + (1 - core[0] if flip else core[0])
            value = jnp.concatenate([mixed[chip, 4 + 2 * flip], mixed[chip, 5 + 2 * flip]], axis=0)
            factor = send_count[0, peer].astype(F32)
            input_grad[:, columns(send_block[0, peer])] += value.astype(F32) * factor


def sum_kernel(scale, parts, home, away, mixed):
    half = parts.shape[3] // 2
    rows = parts.shape[2]
    total = parts[0].astype(F32)
    for source in range(1, parts.shape[0]):
        total = total + parts[source].astype(F32)
    total = total * scale
    for side in range(2):
        cut = slice(side * half, (side + 1) * half)
        for pair in range(2):
            value = jnp.concatenate([total[2 * pair + c, :, cut] for c in range(2)], axis=1)
            for target in range(mixed.shape[0]):
                mixed[target, 2 * side + pair] = value.astype(BF)
    for target in range(mixed.shape[0]):
        for flip, blocks in enumerate((home, away)):
            for part in range(2):
                mixed[target, 4 + 2 * flip + part] = blocks[target, part * rows : (part + 1) * rows]


def unpack_kernel(core, mine, other, conv_grad, coarse_grad):
    half = mine.shape[2]
    for mixed, side in ((mine, core[0]), (other, 1 - core[0])):
        rows = pl.ds(pl.multiple_of(side * half, half), half)
        for offset in range(TERMS):
            for pair in range(2):
                value = mixed[offset // 2, 2 * (offset % 2) + pair].astype(F32)
                cut = slice(pair * BLOCK, (pair + 1) * BLOCK)
                if offset < OFFSETS:
                    conv_grad[offset, rows, cut] = value
                else:
                    coarse_grad[rows, cut] = value


def shift(value, axis, step):
    size = lax.axis_size(axis)
    return lax.ppermute(value, axis, [(i, (i + step) % size) for i in range(size)])


def swap_cores(value):
    size = lax.axis_size("morton")
    return lax.ppermute(value, "morton", [(i, i ^ 1) for i in range(size)])


def local_step(features, conv_weight, coarse_weight, out_grad, send_block, send_count, neighbour):
    n_morton = lax.axis_size("morton")
    quarter, row_count = features.shape
    channels = conv_weight.shape[2]
    nblocks = row_count // BLOCK
    extent = nblocks + n_morton
    depth = TERMS * quarter
    flops = 2 * depth * channels * row_count
    place = lax.axis_index("chan").astype(jnp.int32).reshape(1)
    core = (lax.axis_index("morton") % 2).astype(jnp.int32).reshape(1)
    shape = jax.ShapeDtypeStruct

    pieces = call(
        split_kernel, "split", shape((4 * PAIRS, quarter, BLOCK), BF), "svv", size=2 << 20
    )(place, conv_weight, coarse_weight)
    outgoing = call(
        pack_kernel, "pack", shape((n_morton, quarter, BLOCK), BF), "ssv", size=1 << 20
    )(send_block, send_count, features)
    incoming = lax.all_to_all(outgoing, "morton", 0, 0, tiled=True)

    pieces = pieces.reshape(4, PAIRS, quarter, BLOCK)
    weights = [pieces[0]] + [shift(pieces[s], "chan", s) for s in (1, 2, 3)]
    middle = row_count // 2
    big = [pltpu.VMEM((extent + 1, quarter, BLOCK), BF), pltpu.VMEM((depth, middle), BF)]
    turned = [pltpu.VMEM((middle, channels), BF)]
    wide, part = (quarter, row_count), (quarter, middle)
    grads = []
    output = ()
    for half in range(2):
        partial = call(
            functools.partial(forward_kernel, half),
            f"forward{half}",
            [shape(part, F32)] + [shape(part, BF)] * 3,
            "svvvvvv",
            [pltpu.VMEM((channels, depth), BF)] + big,
            flops // 2,
            3 << 20,
        )(neighbour, features, incoming, *weights)
        arrived = [shift(partial[s], "chan", -s) for s in (1, 2, 3)]
        output, grad = call(
            activation_end_kernel if half else activation_kernel,
            f"activation{half}",
            [shape(wide if half else part, BF), shape(part, BF)],
            "vvvvvv" if half else "vvvvv",
            size=1 << 20,
        )(partial[0], *arrived, out_grad, *((output,) if half else ()))
        grads.append([grad] + [shift(grad, "chan", s) for s in (1, 2, 3)])

    weight_t = call(join_kernel, "join", shape((depth, channels), BF), "vvvva", size=3 << 20)(
        *weights, grads[0][0]
    )
    held = call(
        weight_first_kernel,
        "weight_grad0",
        shape((depth, channels), F32),
        "svvvvvv",
        big + turned,
        flops // 2,
        4 << 20,
    )(neighbour, features, incoming, *grads[0])
    piece = (4, quarter // 2, BLOCK)
    keep, give = call(
        weight_second_kernel,
        "weight_grad1",
        [shape((PAIRS,) + piece, F32), shape((PAIRS,) + piece, BF)],
        "ssvvvvvvv",
        big + turned,
        flops // 2,
        4 << 20,
    )(core, neighbour, features, incoming, *grads[1], held)
    chips = n_morton // 2
    parts = call(pair_kernel, "pair_sum", shape((chips,) + piece, BF), "svv", size=3 << 20)(
        place, keep, swap_cores(give)
    )
    same_core = [[2 * c + side for c in range(chips)] for side in range(2)]
    same_core_all = [[device * 4 + z for device in group for z in range(4)] for group in same_core]
    received = lax.all_to_all(
        parts.reshape((4 * chips,) + piece[1:]),
        ("morton", "chan"),
        0,
        0,
        axis_index_groups=same_core_all,
        tiled=True,
    ).reshape(parts.shape)

    blocks = (chips, quarter, BLOCK)
    local, home, away = call(
        table_kernel,
        "table_grad",
        [shape(wide, F32), shape(blocks, BF), shape(blocks, BF)],
        "ss" + "v" * 9 + "a",
        [
            pltpu.VMEM((extent + 1, quarter, BLOCK), F32),
            pltpu.VMEM((OFFSETS * quarter, 256), F32),
        ],
        flops,
        4 << 20,
    )(core, neighbour, weight_t, *grads[0], *grads[1], parts)
    scale = float(row_count * n_morton) ** (-0.5)
    mixed = call(
        functools.partial(sum_kernel, scale),
        "sum_parts",
        shape((chips, 8, quarter // 2, BLOCK), BF),
        "vvv",
        size=1 << 20,
    )(received, home, swap_cores(away))
    mine = lax.all_to_all(mixed, "morton", 0, 0, axis_index_groups=same_core, tiled=True)
    input_grad = call(return_kernel, "return_add", shape(wide, F32), "sssvv", size=2 << 20)(
        core, send_block, send_count, local, mine
    )
    conv_grad, coarse_grad = call(
        unpack_kernel,
        "unpack",
        [shape((OFFSETS, quarter, channels), F32), shape((quarter, channels), F32)],
        "svv",
        size=3 << 20,
    )(core, mine, swap_cores(mine))
    return output, input_grad, conv_grad, coarse_grad


def solution(mesh):
    placed = (
        P("chan", "morton"),
        P(None, "chan", None),
        P("chan", None),
        P("chan", "morton"),
        P("morton", None),
        P("morton", None),
        P(None, "morton"),
    )
    return jax.shard_map(
        local_step,
        mesh=mesh,
        in_specs=placed,
        out_specs=(
            P("chan", "morton"),
            P("chan", "morton"),
            P(None, "chan", None),
            P("chan", None),
        ),
        check_vma=False,
    )
```

```python
import functools

import jax
import jax.numpy as jnp
from jax import lax
from jax.experimental import pallas as pl
from jax.experimental.pallas import tpu as pltpu
from jax.sharding import PartitionSpec as P

OFFSETS = 27
TERMS = 28
PAIRS = TERMS // 2
BLOCK = 128
BF = jnp.bfloat16
F32 = jnp.float32


def call(kernel, name, outs, kinds, scratch=(), flops=0, size=0, limit=24 << 20):
    space = {"s": pltpu.SMEM, "v": pltpu.VMEM, "a": pl.ANY}
    many = isinstance(outs, (list, tuple))
    spec = pl.BlockSpec(memory_space=pltpu.VMEM)
    return pl.pallas_call(
        kernel,
        name=name,
        out_shape=outs,
        in_specs=[pl.BlockSpec(memory_space=space[k]) for k in kinds],
        out_specs=[spec] * len(outs) if many else spec,
        scratch_shapes=list(scratch),
        compiler_params=pltpu.CompilerParams(vmem_limit_bytes=limit),
        cost_estimate=pl.CostEstimate(flops=flops, bytes_accessed=size, transcendentals=0),
    )


def mean_matrix():
    row = lax.broadcasted_iota(jnp.int32, (BLOCK, BLOCK), 0) // 8
    column = lax.broadcasted_iota(jnp.int32, (BLOCK, BLOCK), 1) // 8
    return jnp.where(row == column, 0.125, 0.0).astype(BF)


def columns(index):
    return pl.ds(pl.multiple_of(index * BLOCK, BLOCK), BLOCK)


def pack_kernel(send_block, send_count, features, outgoing):
    for peer in range(outgoing.shape[0]):
        block = features[:, columns(send_block[0, peer])]
        outgoing[peer] = block * send_count[0, peer].astype(F32).astype(BF)


def split_kernel(place, conv_weight, coarse_weight, pieces):
    quarter = conv_weight.shape[1]
    for pair in range(PAIRS):
        first = conv_weight[2 * pair]
        second = conv_weight[2 * pair + 1] if 2 * pair + 1 < OFFSETS else coarse_weight[...]
        cuts = [slice(t * quarter, (t + 1) * quarter) for t in range(4)]
        tiles = [jnp.concatenate([first[:, c], second[:, c]], axis=1) for c in cuts]
        for step in range(4):
            target = place[0] ^ step
            low = jnp.where(target == 0, tiles[0], tiles[1])
            high = jnp.where(target == 2, tiles[2], tiles[3])
            pieces[step * PAIRS + pair] = jnp.where(target < 2, low, high)


def join_kernel(piece0, piece1, piece2, piece3, after, flipped):
    del after
    for pair in range(PAIRS):
        tile = jnp.concatenate([p[pair] for p in (piece0, piece1, piece2, piece3)], axis=0)
        flipped[pair * BLOCK : (pair + 1) * BLOCK, :] = tile.T


def fill_table(features, incoming, table, nblocks):
    for block in range(nblocks):
        table[block] = features[:, block * BLOCK : (block + 1) * BLOCK]
    table[nblocks : nblocks + incoming.shape[0]] = incoming[...]
    table[nblocks + incoming.shape[0]] = jnp.zeros(table.shape[1:], BF)


def slot(neighbour, offset, block, extent):
    named = neighbour[offset, block]
    return jnp.where(named < 0, extent, named)


def fill_gathered(neighbour, table, gathered, first, extent):
    quarter = table.shape[1]
    nblocks = gathered.shape[1] // BLOCK

    def step(offset, carry):
        rows = pl.ds(pl.multiple_of(offset * quarter, quarter), quarter)
        for block in range(nblocks):
            picked = table[slot(neighbour, offset, first + block, extent)]
            gathered[rows, block * BLOCK : (block + 1) * BLOCK] = picked
        return carry

    lax.fori_loop(0, OFFSETS, step, 0, unroll=27)
    mean = mean_matrix()
    for block in range(nblocks):
        pooled = jnp.dot(table[first + block], mean, preferred_element_type=F32).astype(BF)
        gathered[OFFSETS * quarter :, block * BLOCK : (block + 1) * BLOCK] = pooled


def forward_kernel(half, neighbour, features, incoming, *refs):
    pieces, outs, (weight, table, gathered) = refs[:4], refs[4:8], refs[8:]
    quarter, row_count = features.shape
    nblocks = row_count // BLOCK
    extent = nblocks + incoming.shape[0]
    for step, piece in enumerate(pieces):
        for pair in range(PAIRS):
            rows = slice(step * quarter, (step + 1) * quarter)
            weight[rows, pair * BLOCK : (pair + 1) * BLOCK] = piece[pair]
    fill_table(features, incoming, table, nblocks)
    fill_gathered(neighbour, table, gathered, half * nblocks // 2, extent)
    for tile in range(row_count // 512):
        cut = slice(tile * 256, (tile + 1) * 256)
        total = jnp.dot(weight[...], gathered[:, cut], preferred_element_type=F32)
        for step, out in enumerate(outs):
            out[:, cut] = total[step * quarter : (step + 1) * quarter].astype(out.dtype)


def activate(own, part1, part2, part3, out_grad):
    pre = (own[...] + part1[...].astype(F32)) + (part2[...].astype(F32) + part3[...].astype(F32))
    sigma = 1.0 / (1.0 + jnp.exp(-pre))
    grad = out_grad.astype(F32) * sigma * (1.0 + pre * (1.0 - sigma))
    return (pre * sigma).astype(BF), grad.astype(BF)


def activation_kernel(own, part1, part2, part3, out_grad, output, grad):
    middle = own.shape[1]
    output[...], grad[...] = activate(own, part1, part2, part3, out_grad[:, :middle])


def activation_end_kernel(own, part1, part2, part3, out_grad, before, output, grad):
    middle = own.shape[1]
    output[:, :middle] = before[...]
    output[:, middle:], grad[...] = activate(own, part1, part2, part3, out_grad[:, middle:])


def prepare_weight(half, neighbour, features, incoming, grads, table, gathered, flipped):
    nblocks = features.shape[1] // BLOCK
    extent = nblocks + incoming.shape[0]
    fill_table(features, incoming, table, nblocks)
    fill_gathered(neighbour, table, gathered, half * nblocks // 2, extent)
    for block in range(nblocks // 2):
        cut = slice(block * BLOCK, (block + 1) * BLOCK)
        tall = jnp.concatenate([g[:, cut] for g in grads], axis=0)
        flipped[cut, :] = tall.T


def weight_first_kernel(
    neighbour, features, incoming, grad0, grad1, grad2, grad3, held, table, gathered, flipped
):
    grads = (grad0, grad1, grad2, grad3)
    prepare_weight(0, neighbour, features, incoming, grads, table, gathered, flipped)
    held[...] = jnp.dot(gathered[...], flipped[...], preferred_element_type=F32)


def weight_second_kernel(
    core, neighbour, features, incoming, grad0, grad1, grad2, grad3, held, keep, give, table, gathered, flipped
):
    quarter = features.shape[0]
    grads = (grad0, grad1, grad2, grad3)
    prepare_weight(1, neighbour, features, incoming, grads, table, gathered, flipped)
    half = quarter // 2
    for pair in range(PAIRS):
        rows = slice(pair * BLOCK, (pair + 1) * BLOCK)
        product = jnp.dot(gathered[rows, :], flipped[...], preferred_element_type=F32)
        upright = (product + held[rows, :]).T
        for step in range(4):
            low = upright[step * quarter : step * quarter + half]
            high = upright[step * quarter + half : (step + 1) * quarter]
            keep[pair, step] = jnp.where(core[0] == 0, low, high)
            give[pair, step] = jnp.where(core[0] == 0, high, low).astype(BF)


def pair_kernel(place, keep, arrived, parts):
    for step in range(4):
        target = place[0] ^ step
        for pair in range(PAIRS):
            parts[pair, target] = (keep[pair, step] + arrived[pair, step].astype(F32)).astype(BF)
    for spare in range(PAIRS, parts.shape[0]):
        parts[spare] = jnp.zeros(parts.shape[1:], BF)


def table_kernel(
    core, neighbour, weight_t, g00, g01, g02, g03, g10, g11, g12, g13, after, local, home, away, total, spread
):
    del after
    quarter, row_count = local.shape
    nblocks = row_count // BLOCK
    extent = total.shape[0] - 1
    total[...] = jnp.zeros_like(total)
    mean = mean_matrix()
    for tile in range(nblocks // 2):
        grads = (g00, g01, g02, g03) if tile < nblocks // 4 else (g10, g11, g12, g13)
        start = tile % (nblocks // 4) * 256
        tall = jnp.concatenate([g[:, start : start + 256] for g in grads], axis=0)
        product = jnp.dot(weight_t[...], tall, preferred_element_type=F32)
        spread[...] = product[: OFFSETS * quarter]

        def step(offset, carry, tile=tile):
            rows = pl.ds(pl.multiple_of(offset * quarter, quarter), quarter)
            for side in range(2):
                place = slot(neighbour, offset, 2 * tile + side, extent)
                total[place] += spread[rows, side * BLOCK : (side + 1) * BLOCK]
            return carry

        lax.fori_loop(0, OFFSETS, step, 0, unroll=27)
        coarse = product[OFFSETS * quarter :]
        for side in range(2):
            value = coarse[:, side * BLOCK : (side + 1) * BLOCK]
            high = value.astype(BF)
            low = (value - high.astype(F32)).astype(BF)
            total[2 * tile + side] += jnp.dot(high, mean, preferred_element_type=F32) + jnp.dot(
                low, mean, preferred_element_type=F32
            )
    for block in range(nblocks):
        local[:, block * BLOCK : (block + 1) * BLOCK] = total[block]
    for chip in range(home.shape[0]):
        home[chip] = total[nblocks + 2 * chip + core[0]].astype(BF)
        away[chip] = total[nblocks + 2 * chip + 1 - core[0]].astype(BF)


def return_kernel(core, send_block, send_count, local, mixed, input_grad):
    input_grad[...] = local[...]
    for chip in range(mixed.shape[0]):
        for flip in range(2):
            peer = 2 * chip + (1 - core[0] if flip else core[0])
            value = jnp.concatenate([mixed[chip, 4 + 2 * flip], mixed[chip, 5 + 2 * flip]], axis=0)
            factor = send_count[0, peer].astype(F32)
            input_grad[:, columns(send_block[0, peer])] += value.astype(F32) * factor


def sum_kernel(scale, parts, home, away, mixed):
    half = parts.shape[3] // 2
    rows = parts.shape[2]
    total = parts[0].astype(F32)
    for source in range(1, parts.shape[0]):
        total = total + parts[source].astype(F32)
    total = total * scale
    for side in range(2):
        cut = slice(side * half, (side + 1) * half)
        for pair in range(2):
            value = jnp.concatenate([total[2 * pair + c, :, cut] for c in range(2)], axis=1)
            for target in range(mixed.shape[0]):
                mixed[target, 2 * side + pair] = value.astype(BF)
    for target in range(mixed.shape[0]):
        for flip, blocks in enumerate((home, away)):
            for part in range(2):
                mixed[target, 4 + 2 * flip + part] = blocks[target, part * rows : (part + 1) * rows]


def unpack_kernel(core, mine, other, conv_grad, coarse_grad):
    half = mine.shape[2]
    for mixed, side in ((mine, core[0]), (other, 1 - core[0])):
        rows = pl.ds(pl.multiple_of(side * half, half), half)
        for offset in range(TERMS):
            for pair in range(2):
                value = mixed[offset // 2, 2 * (offset % 2) + pair].astype(F32)
                cut = slice(pair * BLOCK, (pair + 1) * BLOCK)
                if offset < OFFSETS:
                    conv_grad[offset, rows, cut] = value
                else:
                    coarse_grad[rows, cut] = value


def exchange(value, step):
    size = lax.axis_size("chan")
    return lax.ppermute(value, "chan", [(i, i ^ step) for i in range(size)])


def swap_cores(value):
    size = lax.axis_size("morton")
    return lax.ppermute(value, "morton", [(i, i ^ 1) for i in range(size)])


def local_step(features, conv_weight, coarse_weight, out_grad, send_block, send_count, neighbour):
    n_morton = lax.axis_size("morton")
    quarter, row_count = features.shape
    channels = conv_weight.shape[2]
    nblocks = row_count // BLOCK
    extent = nblocks + n_morton
    depth = TERMS * quarter
    flops = 2 * depth * channels * row_count
    place = lax.axis_index("chan").astype(jnp.int32).reshape(1)
    core = (lax.axis_index("morton") % 2).astype(jnp.int32).reshape(1)
    shape = jax.ShapeDtypeStruct

    pieces = call(
        split_kernel, "split", shape((4 * PAIRS, quarter, BLOCK), BF), "svv", size=2 << 20
    )(place, conv_weight, coarse_weight)
    outgoing = call(
        pack_kernel, "pack", shape((n_morton, quarter, BLOCK), BF), "ssv", size=1 << 20
    )(send_block, send_count, features)
    incoming = lax.all_to_all(outgoing, "morton", 0, 0, tiled=True)

    pieces = pieces.reshape(4, PAIRS, quarter, BLOCK)
    weights = [pieces[0]] + [exchange(pieces[s], s) for s in (1, 2, 3)]
    middle = row_count // 2
    big = [pltpu.VMEM((extent + 1, quarter, BLOCK), BF), pltpu.VMEM((depth, middle), BF)]
    turned = [pltpu.VMEM((middle, channels), BF)]
    wide, part = (quarter, row_count), (quarter, middle)
    grads = []
    output = ()
    for half in range(2):
        partial = call(
            functools.partial(forward_kernel, half),
            f"forward{half}",
            [shape(part, F32)] + [shape(part, BF)] * 3,
            "svvvvvv",
            [pltpu.VMEM((channels, depth), BF)] + big,
            flops // 2,
            3 << 20,
        )(neighbour, features, incoming, *weights)
        arrived = [exchange(partial[s], s) for s in (1, 2, 3)]
        output, grad = call(
            activation_end_kernel if half else activation_kernel,
            f"activation{half}",
            [shape(wide if half else part, BF), shape(part, BF)],
            "vvvvvv" if half else "vvvvv",
            size=1 << 20,
        )(partial[0], *arrived, out_grad, *((output,) if half else ()))
        grads.append([grad] + [exchange(grad, s) for s in (1, 2, 3)])

    weight_t = call(join_kernel, "join", shape((depth, channels), BF), "vvvva", size=3 << 20)(
        *weights, grads[0][0]
    )
    held = call(
        weight_first_kernel,
        "weight_grad0",
        shape((depth, channels), F32),
        "svvvvvv",
        big + turned,
        flops // 2,
        4 << 20,
    )(neighbour, features, incoming, *grads[0])
    piece = (4, quarter // 2, BLOCK)
    keep, give = call(
        weight_second_kernel,
        "weight_grad1",
        [shape((PAIRS,) + piece, F32), shape((PAIRS,) + piece, BF)],
        "ssvvvvvvv",
        big + turned,
        flops // 2,
        4 << 20,
    )(core, neighbour, features, incoming, *grads[1], held)
    chips = n_morton // 2
    parts = call(pair_kernel, "pair_sum", shape((chips,) + piece, BF), "svv", size=3 << 20)(
        place, keep, swap_cores(give)
    )
    same_core = [[2 * c + side for c in range(chips)] for side in range(2)]
    same_core_all = [[device * 4 + z for device in group for z in range(4)] for group in same_core]
    received = lax.all_to_all(
        parts.reshape((4 * chips,) + piece[1:]),
        ("morton", "chan"),
        0,
        0,
        axis_index_groups=same_core_all,
        tiled=True,
    ).reshape(parts.shape)

    blocks = (chips, quarter, BLOCK)
    local, home, away = call(
        table_kernel,
        "table_grad",
        [shape(wide, F32), shape(blocks, BF), shape(blocks, BF)],
        "ss" + "v" * 9 + "a",
        [
            pltpu.VMEM((extent + 1, quarter, BLOCK), F32),
            pltpu.VMEM((OFFSETS * quarter, 256), F32),
        ],
        flops,
        4 << 20,
    )(core, neighbour, weight_t, *grads[0], *grads[1], parts)
    scale = float(row_count * n_morton) ** (-0.5)
    mixed = call(
        functools.partial(sum_kernel, scale),
        "sum_parts",
        shape((chips, 8, quarter // 2, BLOCK), BF),
        "vvv",
        size=1 << 20,
    )(received, home, swap_cores(away))
    mine = lax.all_to_all(mixed, "morton", 0, 0, axis_index_groups=same_core, tiled=True)
    input_grad = call(return_kernel, "return_add", shape(wide, F32), "sssvv", size=2 << 20)(
        core, send_block, send_count, local, mine
    )
    conv_grad, coarse_grad = call(
        unpack_kernel,
        "unpack",
        [shape((OFFSETS, quarter, channels), F32), shape((quarter, channels), F32)],
        "svv",
        size=3 << 20,
    )(core, mine, swap_cores(mine))
    return output, input_grad, conv_grad, coarse_grad


def solution(mesh):
    placed = (
        P("chan", "morton"),
        P(None, "chan", None),
        P("chan", None),
        P("chan", "morton"),
        P("morton", None),
        P("morton", None),
        P(None, "morton"),
    )
    return jax.shard_map(
        local_step,
        mesh=mesh,
        in_specs=placed,
        out_specs=(
            P("chan", "morton"),
            P("chan", "morton"),
            P(None, "chan", None),
            P("chan", None),
        ),
        check_vma=False,
    )
```

```python
import functools

import jax
import jax.numpy as jnp
from jax import lax
from jax.experimental import pallas as pl
from jax.experimental.pallas import tpu as pltpu
from jax.sharding import PartitionSpec as P

OFFSETS = 27
TERMS = 28
PAIRS = TERMS // 2
BLOCK = 128
CUTS = (0, 8, 16)
BF = jnp.bfloat16
F32 = jnp.float32


def call(kernel, name, outs, kinds, scratch=(), flops=0, size=0, limit=24 << 20):
    space = {"s": pltpu.SMEM, "v": pltpu.VMEM, "a": pl.ANY, "h": pltpu.HBM}
    many = isinstance(outs, (list, tuple))
    spec = pl.BlockSpec(memory_space=pltpu.VMEM)
    return pl.pallas_call(
        kernel,
        name=name,
        out_shape=outs,
        in_specs=[pl.BlockSpec(memory_space=space[k]) for k in kinds],
        out_specs=[spec] * len(outs) if many else spec,
        scratch_shapes=list(scratch),
        compiler_params=pltpu.CompilerParams(vmem_limit_bytes=limit),
        cost_estimate=pl.CostEstimate(flops=flops, bytes_accessed=size, transcendentals=0),
    )


def mean_matrix():
    row = lax.broadcasted_iota(jnp.int32, (BLOCK, BLOCK), 0) // 8
    column = lax.broadcasted_iota(jnp.int32, (BLOCK, BLOCK), 1) // 8
    return jnp.where(row == column, 0.125, 0.0).astype(BF)


def columns(index):
    return pl.ds(pl.multiple_of(index * BLOCK, BLOCK), BLOCK)


def pack_kernel(block_hbm, count_hbm, features_hbm, outgoing, send_block, send_count, features, sems):
    copies = [
        pltpu.make_async_copy(block_hbm, send_block, sems.at[0]),
        pltpu.make_async_copy(count_hbm, send_count, sems.at[1]),
        pltpu.make_async_copy(features_hbm, features, sems.at[2]),
    ]
    for copy in copies:
        copy.start()
    for copy in copies:
        copy.wait()
    for peer in range(outgoing.shape[0]):
        block = features[:, columns(send_block[0, peer])]
        outgoing[peer] = block * send_count[0, peer].astype(F32).astype(BF)


def split_kernel(place, core, conv_weight, coarse_weight, own, sent1, sent2, sent3):
    quarter = conv_weight.shape[1]
    cuts = [slice(t * quarter, (t + 1) * quarter) for t in range(4)]

    def tiles_of(pair):
        first = conv_weight[2 * pair]
        second = conv_weight[2 * pair + 1] if 2 * pair + 1 < OFFSETS else coarse_weight[...]
        return [jnp.concatenate([first[:, c], second[:, c]], axis=1) for c in cuts]

    def pick(tiles, target):
        low = jnp.where(target == 0, tiles[0], tiles[1])
        high = jnp.where(target == 2, tiles[2], tiles[3])
        return jnp.where(target < 2, low, high)

    half = PAIRS // 2
    for pair in range(half):
        low, high = tiles_of(pair), tiles_of(pair + half)
        own[pair] = pick(low, place[0])
        own[pair + half] = pick(high, place[0])
        mine = [jnp.where(core[0] == 0, a, b) for a, b in zip(low, high)]
        for step, sent in enumerate((sent1, sent2, sent3)):
            sent[pair] = pick(mine, place[0] ^ (step + 1))


def weight_tiles(place, core, pieces, pair):
    half = PAIRS // 2
    local = core[0] == pair // half
    own = pieces[0][pair]
    first, second, third = (
        jnp.where(local, pieces[s][pair % half], pieces[s + 3][pair % half]) for s in (1, 2, 3)
    )
    odd = place[0] % 2 == 1
    return own, jnp.where(odd, first, third), second, jnp.where(odd, third, first)


def join_kernel(place, core, *refs):
    flipped = refs[-1]
    for pair in range(PAIRS):
        tile = jnp.concatenate(weight_tiles(place, core, refs[:7], pair), axis=0)
        flipped[pair * BLOCK : (pair + 1) * BLOCK, :] = tile.T


def fill_table(features, incoming, table, nblocks):
    for block in range(nblocks):
        table[block] = features[:, block * BLOCK : (block + 1) * BLOCK]
    table[nblocks : nblocks + incoming.shape[0]] = incoming[...]
    table[nblocks + incoming.shape[0]] = jnp.zeros(table.shape[1:], BF)


def slot(neighbour, offset, block, extent):
    named = neighbour[offset, block]
    return jnp.where(named < 0, extent, named)


def fill_gathered(neighbour, table, gathered, first, extent):
    quarter = table.shape[1]
    nblocks = gathered.shape[1] // BLOCK

    def step(offset, carry):
        rows = pl.ds(pl.multiple_of(offset * quarter, quarter), quarter)
        for block in range(nblocks):
            picked = table[slot(neighbour, offset, first + block, extent)]
            gathered[rows, block * BLOCK : (block + 1) * BLOCK] = picked
        return carry

    lax.fori_loop(0, OFFSETS, step, 0, unroll=27)
    mean = mean_matrix()
    for block in range(nblocks):
        pooled = jnp.dot(table[first + block], mean, preferred_element_type=F32).astype(BF)
        gathered[OFFSETS * quarter :, block * BLOCK : (block + 1) * BLOCK] = pooled


def forward_kernel(first, place, core, neighbour, features, incoming, *refs):
    pieces, outs, (weight, table, gathered) = refs[:7], refs[7:11], refs[11:]
    quarter, row_count = features.shape
    nblocks = row_count // BLOCK
    extent = nblocks + incoming.shape[0]
    for pair in range(PAIRS):
        for step, tile in enumerate(weight_tiles(place, core, pieces, pair)):
            rows = slice(step * quarter, (step + 1) * quarter)
            weight[rows, pair * BLOCK : (pair + 1) * BLOCK] = tile
    fill_table(features, incoming, table, nblocks)
    fill_gathered(neighbour, table, gathered, first, extent)
    for tile in range(gathered.shape[1] // 256):
        cut = slice(tile * 256, (tile + 1) * 256)
        total = jnp.dot(weight[...], gathered[:, cut], preferred_element_type=F32)
        for step, out in enumerate(outs):
            out[:, cut] = total[step * quarter : (step + 1) * quarter].astype(out.dtype)


def activate(own, part1, part2, part3, out_grad):
    pre = (own[...] + part1[...].astype(F32)) + (part2[...].astype(F32) + part3[...].astype(F32))
    sigma = 1.0 / (1.0 + jnp.exp(-pre))
    grad = out_grad.astype(F32) * sigma * (1.0 + pre * (1.0 - sigma))
    return (pre * sigma).astype(BF), grad.astype(BF)


def activation_kernel(first, own, part1, part2, part3, out_grad, output, grad):
    cut = slice(first * BLOCK, first * BLOCK + own.shape[1])
    output[...], grad[...] = activate(own, part1, part2, part3, out_grad[:, cut])


def activation_end_kernel(first, own, part1, part2, part3, out_grad, *refs):
    output, grad = refs[-2:]
    start = 0
    for before in refs[:-2]:
        output[:, start : start + before.shape[1]] = before[...]
        start += before.shape[1]
    cut = slice(first * BLOCK, first * BLOCK + own.shape[1])
    output[:, cut], grad[...] = activate(own, part1, part2, part3, out_grad[:, cut])


def prepare_weight(first, neighbour, features, incoming, grads, table, gathered, flipped):
    nblocks = features.shape[1] // BLOCK
    extent = nblocks + incoming.shape[0]
    fill_table(features, incoming, table, nblocks)
    fill_gathered(neighbour, table, gathered, first, extent)
    for block in range(gathered.shape[1] // BLOCK):
        cut = slice(block * BLOCK, (block + 1) * BLOCK)
        tall = jnp.concatenate([g[:, cut] for g in grads], axis=0)
        flipped[cut, :] = tall.T


def weight_first_kernel(
    first, neighbour, features, incoming, grad0, grad1, grad2, grad3, held, table, gathered, flipped
):
    grads = (grad0, grad1, grad2, grad3)
    prepare_weight(first, neighbour, features, incoming, grads, table, gathered, flipped)
    held[...] = jnp.dot(gathered[...], flipped[...], preferred_element_type=F32)


def weight_more_kernel(
    first, neighbour, features, incoming, grad0, grad1, grad2, grad3, held, more, table, gathered, flipped
):
    grads = (grad0, grad1, grad2, grad3)
    prepare_weight(first, neighbour, features, incoming, grads, table, gathered, flipped)
    more[...] = held[...] + jnp.dot(gathered[...], flipped[...], preferred_element_type=F32)


def weight_last_kernel(
    first, core, neighbour, features, incoming, grad0, grad1, grad2, grad3, held, keep, give, table, gathered, flipped
):
    quarter = features.shape[0]
    grads = (grad0, grad1, grad2, grad3)
    prepare_weight(first, neighbour, features, incoming, grads, table, gathered, flipped)
    half = quarter // 2
    for pair in range(PAIRS):
        rows = slice(pair * BLOCK, (pair + 1) * BLOCK)
        product = jnp.dot(gathered[rows, :], flipped[...], preferred_element_type=F32)
        upright = (product + held[rows, :]).T
        for step in range(4):
            low = upright[step * quarter : step * quarter + half]
            high = upright[step * quarter + half : (step + 1) * quarter]
            keep[pair, step] = jnp.where(core[0] == 0, low, high)
            give[pair, step] = jnp.where(core[0] == 0, high, low).astype(BF)


def pair_kernel(place, keep, arrived, parts):
    for step in range(4):
        target = lax.rem(place[0] - step + 4, 4)
        for pair in range(PAIRS):
            parts[pair, target] = (keep[pair, step] + arrived[pair, step].astype(F32)).astype(BF)
    for spare in range(PAIRS, parts.shape[0]):
        parts[spare] = jnp.zeros(parts.shape[1:], BF)


def table_kernel(core, neighbour, weight_t, *refs):
    local, home, away, total, spread = refs[-5:]
    grads = refs[: 4 * (len(CUTS) - 1)]
    quarter, row_count = local.shape
    nblocks = row_count // BLOCK
    extent = total.shape[0] - 1
    total[...] = jnp.zeros_like(total)
    mean = mean_matrix()
    for tile in range(nblocks // 2):
        part = sum(2 * tile >= cut for cut in CUTS[1:])
        start = (2 * tile - CUTS[part]) * BLOCK
        tall = jnp.concatenate(
            [g[:, start : start + 256] for g in grads[4 * part : 4 * part + 4]], axis=0
        )
        product = jnp.dot(weight_t[...], tall, preferred_element_type=F32)
        spread[...] = product[: OFFSETS * quarter]

        def step(offset, carry, tile=tile):
            rows = pl.ds(pl.multiple_of(offset * quarter, quarter), quarter)
            for side in range(2):
                place = slot(neighbour, offset, 2 * tile + side, extent)
                total[place] += spread[rows, side * BLOCK : (side + 1) * BLOCK]
            return carry

        lax.fori_loop(0, OFFSETS, step, 0, unroll=27)
        coarse = product[OFFSETS * quarter :]
        for side in range(2):
            value = coarse[:, side * BLOCK : (side + 1) * BLOCK]
            high = value.astype(BF)
            low = (value - high.astype(F32)).astype(BF)
            total[2 * tile + side] += jnp.dot(high, mean, preferred_element_type=F32) + jnp.dot(
                low, mean, preferred_element_type=F32
            )
    for block in range(nblocks):
        local[:, block * BLOCK : (block + 1) * BLOCK] = total[block]
    for chip in range(home.shape[0]):
        home[chip] = total[nblocks + 2 * chip + core[0]].astype(BF)
        away[chip] = total[nblocks + 2 * chip + 1 - core[0]].astype(BF)


def return_kernel(core, send_block, send_count, local, mixed, input_grad):
    input_grad[...] = local[...]
    for chip in range(mixed.shape[0]):
        for flip in range(2):
            peer = 2 * chip + (1 - core[0] if flip else core[0])
            value = jnp.concatenate([mixed[chip, 4 + 2 * flip], mixed[chip, 5 + 2 * flip]], axis=0)
            factor = send_count[0, peer].astype(F32)
            input_grad[:, columns(send_block[0, peer])] += value.astype(F32) * factor


def sum_kernel(scale, parts, home, away, mixed):
    half = parts.shape[3] // 2
    rows = parts.shape[2]
    total = parts[0].astype(F32)
    for source in range(1, parts.shape[0]):
        total = total + parts[source].astype(F32)
    total = total * scale
    for side in range(2):
        cut = slice(side * half, (side + 1) * half)
        for pair in range(2):
            value = jnp.concatenate([total[2 * pair + c, :, cut] for c in range(2)], axis=1)
            for target in range(mixed.shape[0]):
                mixed[target, 2 * side + pair] = value.astype(BF)
    for target in range(mixed.shape[0]):
        for flip, blocks in enumerate((home, away)):
            for part in range(2):
                mixed[target, 4 + 2 * flip + part] = blocks[target, part * rows : (part + 1) * rows]


def unpack_kernel(core, mine, other, conv_grad, coarse_grad):
    half = mine.shape[2]
    for mixed, side in ((mine, core[0]), (other, 1 - core[0])):
        rows = pl.ds(pl.multiple_of(side * half, half), half)
        for offset in range(TERMS):
            for pair in range(2):
                value = mixed[offset // 2, 2 * (offset % 2) + pair].astype(F32)
                cut = slice(pair * BLOCK, (pair + 1) * BLOCK)
                if offset < OFFSETS:
                    conv_grad[offset, rows, cut] = value
                else:
                    coarse_grad[rows, cut] = value


def shift(value, step):
    size = lax.axis_size("chan")
    return lax.ppermute(value, "chan", [(i, (i + step) % size) for i in range(size)])


def exchange(value, step):
    size = lax.axis_size("chan")
    return lax.ppermute(value, "chan", [(i, i ^ step) for i in range(size)])


def swap_cores(value):
    size = lax.axis_size("morton")
    return lax.ppermute(value, "morton", [(i, i ^ 1) for i in range(size)])


def local_step(features, conv_weight, coarse_weight, out_grad, send_block, send_count, neighbour):
    n_morton = lax.axis_size("morton")
    quarter, row_count = features.shape
    channels = conv_weight.shape[2]
    nblocks = row_count // BLOCK
    extent = nblocks + n_morton
    depth = TERMS * quarter
    flops = 2 * depth * channels * row_count
    place = lax.axis_index("chan").astype(jnp.int32).reshape(1)
    core = (lax.axis_index("morton") % 2).astype(jnp.int32).reshape(1)
    shape = jax.ShapeDtypeStruct

    outgoing = call(
        pack_kernel, "pack", shape((n_morton, quarter, BLOCK), BF), "hhh",
        [
            pltpu.SMEM((1, n_morton), jnp.int32),
            pltpu.SMEM((1, n_morton), jnp.int32),
            pltpu.VMEM((quarter, row_count), BF),
            pltpu.SemaphoreType.DMA((3,)),
        ],
        size=1 << 20,
        limit=60 << 20,
    )(send_block, send_count, features)
    incoming = lax.all_to_all(outgoing, "morton", 0, 0, tiled=True)

    half_piece = shape((PAIRS // 2, quarter, BLOCK), BF)
    own_piece, *sent = call(
        split_kernel,
        "split",
        [shape((PAIRS, quarter, BLOCK), BF)] + [half_piece] * 3,
        "ssvv",
        size=2 << 20,
    )(place, core, conv_weight, coarse_weight)
    came = [exchange(value, step) for step, value in zip((1, 2, 3), sent)]
    weights = [own_piece] + came + [swap_cores(value) for value in came]

    table = pltpu.VMEM((extent + 1, quarter, BLOCK), BF)
    wide, piece = (quarter, row_count), (4, quarter // 2, BLOCK)
    grads, outputs = [], []
    for first, end in zip(CUTS, CUTS[1:]):
        width = (end - first) * BLOCK
        part = (quarter, width)
        partial = call(
            functools.partial(forward_kernel, first),
            f"forward{first}",
            [shape(part, F32)] + [shape(part, BF)] * 3,
            "sss" + "v" * 9,
            [pltpu.VMEM((channels, depth), BF), table, pltpu.VMEM((depth, width), BF)],
            flops * width // row_count,
            3 << 20,
        )(place, core, neighbour, features, incoming, *weights)
        arrived = [shift(partial[s], -s) for s in (1, 2, 3)]
        last = end == CUTS[-1]
        output, grad = call(
            functools.partial(activation_end_kernel if last else activation_kernel, first),
            f"activation{first}",
            [shape(wide if last else part, BF), shape(part, BF)],
            "vvvvv" + "v" * (len(outputs) if last else 0),
            size=1 << 20,
        )(partial[0], *arrived, out_grad, *(outputs if last else ()))
        outputs.append(output)
        grads.append([grad] + [shift(grad, s) for s in (1, 2, 3)])

    weight_t = call(join_kernel, "join", shape((depth, channels), BF), "ss" + "v" * 7 + "a", size=3 << 20)(
        place, core, *weights, grads[0][0]
    )
    held = ()
    for (first, end), given in zip(zip(CUTS, CUTS[1:]), grads):
        width = (end - first) * BLOCK
        last = end == CUTS[-1]
        kernel = weight_last_kernel if last else weight_more_kernel if held else weight_first_kernel
        sums = [shape((PAIRS,) + piece, F32), shape((PAIRS,) + piece, BF)]
        result = call(
            functools.partial(kernel, first),
            f"weight_grad{first}",
            sums if last else shape((depth, channels), F32),
            "s" * (1 + last) + "v" * (6 + len(held)),
            [table, pltpu.VMEM((depth, width), BF), pltpu.VMEM((width, channels), BF)],
            flops * width // row_count,
            4 << 20,
        )(*((core,) if last else ()), neighbour, features, incoming, *given, *held)
        held = (result,)
    keep, give = result
    output = outputs[-1]
    chips = n_morton // 2
    parts = call(pair_kernel, "pair_sum", shape((chips,) + piece, BF), "svv", size=3 << 20)(
        place, keep, swap_cores(give)
    )
    same_core = [[2 * c + side for c in range(chips)] for side in range(2)]
    same_core_all = [[device * 4 + z for device in group for z in range(4)] for group in same_core]
    received = lax.all_to_all(
        parts.reshape((4 * chips,) + piece[1:]),
        ("morton", "chan"),
        0,
        0,
        axis_index_groups=same_core_all,
        tiled=True,
    ).reshape(parts.shape)

    blocks = (chips, quarter, BLOCK)
    local, home, away = call(
        table_kernel,
        "table_grad",
        [shape(wide, F32), shape(blocks, BF), shape(blocks, BF)],
        "ssv" + "v" * 4 * len(grads) + "a",
        [
            pltpu.VMEM((extent + 1, quarter, BLOCK), F32),
            pltpu.VMEM((OFFSETS * quarter, 256), F32),
        ],
        flops,
        4 << 20,
    )(core, neighbour, weight_t, *(g for given in grads for g in given), parts)
    scale = float(row_count * n_morton) ** (-0.5)
    mixed = call(
        functools.partial(sum_kernel, scale),
        "sum_parts",
        shape((chips, 8, quarter // 2, BLOCK), BF),
        "vvv",
        size=1 << 20,
    )(received, home, swap_cores(away))
    mine = lax.all_to_all(mixed, "morton", 0, 0, axis_index_groups=same_core, tiled=True)
    input_grad = call(return_kernel, "return_add", shape(wide, F32), "sssvv", size=2 << 20)(
        core, send_block, send_count, local, mine
    )
    conv_grad, coarse_grad = call(
        unpack_kernel,
        "unpack",
        [shape((OFFSETS, quarter, channels), F32), shape((quarter, channels), F32)],
        "svv",
        size=3 << 20,
    )(core, mine, swap_cores(mine))
    return output, input_grad, conv_grad, coarse_grad


def solution(mesh):
    placed = (
        P("chan", "morton"),
        P(None, "chan", None),
        P("chan", None),
        P("chan", "morton"),
        P("morton", None),
        P("morton", None),
        P(None, "morton"),
    )
    return jax.shard_map(
        local_step,
        mesh=mesh,
        in_specs=placed,
        out_specs=(
            P("chan", "morton"),
            P("chan", "morton"),
            P(None, "chan", None),
            P("chan", None),
        ),
        check_vma=False,
    )
```

```python
import functools

import jax
import jax.numpy as jnp
from jax import lax
from jax.experimental import pallas as pl
from jax.experimental.pallas import tpu as pltpu
from jax.sharding import PartitionSpec as P

OFFSETS = 27
TERMS = 28
PAIRS = TERMS // 2
BLOCK = 128
CUTS = (0, 8, 16)
BF = jnp.bfloat16
F32 = jnp.float32


def call(kernel, name, outs, kinds, scratch=(), flops=0, size=0, limit=24 << 20):
    space = {"s": pltpu.SMEM, "v": pltpu.VMEM, "a": pl.ANY, "h": pltpu.HBM}
    many = isinstance(outs, (list, tuple))
    spec = pl.BlockSpec(memory_space=pltpu.VMEM)
    return pl.pallas_call(
        kernel,
        name=name,
        out_shape=outs,
        in_specs=[pl.BlockSpec(memory_space=space[k]) for k in kinds],
        out_specs=[spec] * len(outs) if many else spec,
        scratch_shapes=list(scratch),
        compiler_params=pltpu.CompilerParams(vmem_limit_bytes=limit),
        cost_estimate=pl.CostEstimate(flops=flops, bytes_accessed=size, transcendentals=0),
    )


def mean_matrix():
    row = lax.broadcasted_iota(jnp.int32, (BLOCK, BLOCK), 0) // 8
    column = lax.broadcasted_iota(jnp.int32, (BLOCK, BLOCK), 1) // 8
    return jnp.where(row == column, 0.125, 0.0).astype(BF)


def columns(index):
    return pl.ds(pl.multiple_of(index * BLOCK, BLOCK), BLOCK)


def pack_kernel(block_hbm, count_hbm, features_hbm, outgoing, send_block, send_count, features, sems):
    copies = [
        pltpu.make_async_copy(block_hbm, send_block, sems.at[0]),
        pltpu.make_async_copy(count_hbm, send_count, sems.at[1]),
        pltpu.make_async_copy(features_hbm, features, sems.at[2]),
    ]
    for copy in copies:
        copy.start()
    for copy in copies:
        copy.wait()
    for peer in range(outgoing.shape[0]):
        block = features[:, columns(send_block[0, peer])]
        outgoing[peer] = block * send_count[0, peer].astype(F32).astype(BF)


def split_kernel(place, core, conv_weight, coarse_weight, own, sent1, sent2, sent3):
    quarter = conv_weight.shape[1]
    cuts = [slice(t * quarter, (t + 1) * quarter) for t in range(4)]

    def tiles_of(pair):
        first = conv_weight[2 * pair]
        second = conv_weight[2 * pair + 1] if 2 * pair + 1 < OFFSETS else coarse_weight[...]
        return [jnp.concatenate([first[:, c], second[:, c]], axis=1) for c in cuts]

    def pick(tiles, target):
        low = jnp.where(target == 0, tiles[0], tiles[1])
        high = jnp.where(target == 2, tiles[2], tiles[3])
        return jnp.where(target < 2, low, high)

    half = PAIRS // 2
    for pair in range(half):
        low, high = tiles_of(pair), tiles_of(pair + half)
        own[pair] = pick(low, place[0])
        own[pair + half] = pick(high, place[0])
        mine = [jnp.where(core[0] == 0, a, b) for a, b in zip(low, high)]
        for step, sent in enumerate((sent1, sent2, sent3)):
            sent[pair] = pick(mine, place[0] ^ (step + 1))


def weight_tiles(place, core, pieces, pair):
    half = PAIRS // 2
    local = core[0] == pair // half
    own = pieces[0][pair]
    first, second, third = (
        jnp.where(local, pieces[s][pair % half], pieces[s + 3][pair % half]) for s in (1, 2, 3)
    )
    odd = place[0] % 2 == 1
    return own, jnp.where(odd, first, third), second, jnp.where(odd, third, first)


def join_kernel(place, core, *refs):
    flipped = refs[-1]
    for pair in range(PAIRS):
        tile = jnp.concatenate(weight_tiles(place, core, refs[:7], pair), axis=0)
        flipped[pair * BLOCK : (pair + 1) * BLOCK, :] = tile.T


def fill_table(features, incoming, table, nblocks):
    for block in range(nblocks):
        table[block] = features[:, block * BLOCK : (block + 1) * BLOCK]
    table[nblocks : nblocks + incoming.shape[0]] = incoming[...]
    table[nblocks + incoming.shape[0]] = jnp.zeros(table.shape[1:], BF)


def slot(neighbour, offset, block, extent):
    named = neighbour[offset, block]
    return jnp.where(named < 0, extent, named)


def fill_gathered(neighbour, table, gathered, first, extent):
    quarter = table.shape[1]
    nblocks = gathered.shape[1] // BLOCK

    def step(offset, carry):
        rows = pl.ds(pl.multiple_of(offset * quarter, quarter), quarter)
        for block in range(nblocks):
            picked = table[slot(neighbour, offset, first + block, extent)]
            gathered[rows, block * BLOCK : (block + 1) * BLOCK] = picked
        return carry

    lax.fori_loop(0, OFFSETS, step, 0, unroll=27)
    mean = mean_matrix()
    for block in range(nblocks):
        pooled = jnp.dot(table[first + block], mean, preferred_element_type=F32).astype(BF)
        gathered[OFFSETS * quarter :, block * BLOCK : (block + 1) * BLOCK] = pooled


def forward_kernel(place, core, neighbour, features, incoming, *refs):
    pieces, outs, (weight, table, gathered) = refs[:7], refs[7:-3], refs[-3:]
    quarter, row_count = features.shape
    nblocks = row_count // BLOCK
    extent = nblocks + incoming.shape[0]
    for pair in range(PAIRS):
        for step, tile in enumerate(weight_tiles(place, core, pieces, pair)):
            rows = slice(step * quarter, (step + 1) * quarter)
            weight[rows, pair * BLOCK : (pair + 1) * BLOCK] = tile
    fill_table(features, incoming, table, nblocks)
    for part, first in enumerate(CUTS[:-1]):
        width = outs[4 * part].shape[1]
        fill_gathered(neighbour, table, gathered.at[:, :width], first, extent)
        for tile in range(width // 256):
            cut = slice(tile * 256, (tile + 1) * 256)
            total = jnp.dot(weight[...], gathered[:, cut], preferred_element_type=F32)
            for step, out in enumerate(outs[4 * part : 4 * part + 4]):
                out[:, cut] = total[step * quarter : (step + 1) * quarter].astype(out.dtype)


def activate(own, part1, part2, part3, out_grad):
    pre = (own[...] + part1[...].astype(F32)) + (part2[...].astype(F32) + part3[...].astype(F32))
    sigma = 1.0 / (1.0 + jnp.exp(-pre))
    grad = out_grad.astype(F32) * sigma * (1.0 + pre * (1.0 - sigma))
    return (pre * sigma).astype(BF), grad.astype(BF)


def activation_kernel(first, own, part1, part2, part3, out_grad, output, grad):
    cut = slice(first * BLOCK, first * BLOCK + own.shape[1])
    output[...], grad[...] = activate(own, part1, part2, part3, out_grad[:, cut])


def activation_end_kernel(first, own, part1, part2, part3, out_grad, *refs):
    output, grad = refs[-2:]
    start = 0
    for before in refs[:-2]:
        output[:, start : start + before.shape[1]] = before[...]
        start += before.shape[1]
    cut = slice(first * BLOCK, first * BLOCK + own.shape[1])
    output[:, cut], grad[...] = activate(own, part1, part2, part3, out_grad[:, cut])


def prepare_weight(first, neighbour, features, incoming, grads, table, gathered, flipped):
    nblocks = features.shape[1] // BLOCK
    extent = nblocks + incoming.shape[0]
    fill_table(features, incoming, table, nblocks)
    fill_gathered(neighbour, table, gathered, first, extent)
    for block in range(gathered.shape[1] // BLOCK):
        cut = slice(block * BLOCK, (block + 1) * BLOCK)
        tall = jnp.concatenate([g[:, cut] for g in grads], axis=0)
        flipped[cut, :] = tall.T


def weight_first_kernel(
    first, neighbour, features, incoming, grad0, grad1, grad2, grad3, held, table, gathered, flipped
):
    grads = (grad0, grad1, grad2, grad3)
    prepare_weight(first, neighbour, features, incoming, grads, table, gathered, flipped)
    held[...] = jnp.dot(gathered[...], flipped[...], preferred_element_type=F32)


def weight_more_kernel(
    first, neighbour, features, incoming, grad0, grad1, grad2, grad3, held, more, table, gathered, flipped
):
    grads = (grad0, grad1, grad2, grad3)
    prepare_weight(first, neighbour, features, incoming, grads, table, gathered, flipped)
    more[...] = held[...] + jnp.dot(gathered[...], flipped[...], preferred_element_type=F32)


def weight_last_kernel(
    first, core, neighbour, features, incoming, grad0, grad1, grad2, grad3, held, keep, give, table, gathered, flipped
):
    quarter = features.shape[0]
    grads = (grad0, grad1, grad2, grad3)
    prepare_weight(first, neighbour, features, incoming, grads, table, gathered, flipped)
    half = quarter // 2
    for pair in range(PAIRS):
        rows = slice(pair * BLOCK, (pair + 1) * BLOCK)
        product = jnp.dot(gathered[rows, :], flipped[...], preferred_element_type=F32)
        upright = (product + held[rows, :]).T
        for step in range(4):
            low = upright[step * quarter : step * quarter + half]
            high = upright[step * quarter + half : (step + 1) * quarter]
            keep[pair, step] = jnp.where(core[0] == 0, low, high)
            give[pair, step] = jnp.where(core[0] == 0, high, low).astype(BF)


def pair_kernel(place, keep, arrived, parts):
    for step in range(4):
        target = lax.rem(place[0] - step + 4, 4)
        for pair in range(PAIRS):
            parts[pair, target] = (keep[pair, step] + arrived[pair, step].astype(F32)).astype(BF)
    for spare in range(PAIRS, parts.shape[0]):
        parts[spare] = jnp.zeros(parts.shape[1:], BF)


def table_kernel(core, neighbour, weight_t, *refs):
    local, home, away, total, spread = refs[-5:]
    grads = refs[: 4 * (len(CUTS) - 1)]
    quarter, row_count = local.shape
    nblocks = row_count // BLOCK
    extent = total.shape[0] - 1
    total[...] = jnp.zeros_like(total)
    mean = mean_matrix()
    for tile in range(nblocks // 2):
        part = sum(2 * tile >= cut for cut in CUTS[1:])
        start = (2 * tile - CUTS[part]) * BLOCK
        tall = jnp.concatenate(
            [g[:, start : start + 256] for g in grads[4 * part : 4 * part + 4]], axis=0
        )
        product = jnp.dot(weight_t[...], tall, preferred_element_type=F32)
        spread[...] = product[: OFFSETS * quarter]

        def step(offset, carry, tile=tile):
            rows = pl.ds(pl.multiple_of(offset * quarter, quarter), quarter)
            for side in range(2):
                place = slot(neighbour, offset, 2 * tile + side, extent)
                total[place] += spread[rows, side * BLOCK : (side + 1) * BLOCK]
            return carry

        lax.fori_loop(0, OFFSETS, step, 0, unroll=27)
        coarse = product[OFFSETS * quarter :]
        for side in range(2):
            value = coarse[:, side * BLOCK : (side + 1) * BLOCK]
            high = value.astype(BF)
            low = (value - high.astype(F32)).astype(BF)
            total[2 * tile + side] += jnp.dot(high, mean, preferred_element_type=F32) + jnp.dot(
                low, mean, preferred_element_type=F32
            )
    for block in range(nblocks):
        local[:, block * BLOCK : (block + 1) * BLOCK] = total[block]
    for chip in range(home.shape[0]):
        home[chip] = total[nblocks + 2 * chip + core[0]].astype(BF)
        away[chip] = total[nblocks + 2 * chip + 1 - core[0]].astype(BF)


def return_kernel(core, send_block, send_count, local, mixed, input_grad):
    input_grad[...] = local[...]
    for chip in range(mixed.shape[0]):
        for flip in range(2):
            peer = 2 * chip + (1 - core[0] if flip else core[0])
            value = jnp.concatenate([mixed[chip, 4 + 2 * flip], mixed[chip, 5 + 2 * flip]], axis=0)
            factor = send_count[0, peer].astype(F32)
            input_grad[:, columns(send_block[0, peer])] += value.astype(F32) * factor


def sum_kernel(scale, parts, home, away, mixed):
    half = parts.shape[3] // 2
    rows = parts.shape[2]
    total = parts[0].astype(F32)
    for source in range(1, parts.shape[0]):
        total = total + parts[source].astype(F32)
    total = total * scale
    for side in range(2):
        cut = slice(side * half, (side + 1) * half)
        for pair in range(2):
            value = jnp.concatenate([total[2 * pair + c, :, cut] for c in range(2)], axis=1)
            for target in range(mixed.shape[0]):
                mixed[target, 2 * side + pair] = value.astype(BF)
    for target in range(mixed.shape[0]):
        for flip, blocks in enumerate((home, away)):
            for part in range(2):
                mixed[target, 4 + 2 * flip + part] = blocks[target, part * rows : (part + 1) * rows]


def unpack_kernel(core, mine, other, conv_grad, coarse_grad):
    half = mine.shape[2]
    for mixed, side in ((mine, core[0]), (other, 1 - core[0])):
        rows = pl.ds(pl.multiple_of(side * half, half), half)
        for offset in range(TERMS):
            for pair in range(2):
                value = mixed[offset // 2, 2 * (offset % 2) + pair].astype(F32)
                cut = slice(pair * BLOCK, (pair + 1) * BLOCK)
                if offset < OFFSETS:
                    conv_grad[offset, rows, cut] = value
                else:
                    coarse_grad[rows, cut] = value


def shift(value, step):
    size = lax.axis_size("chan")
    return lax.ppermute(value, "chan", [(i, (i + step) % size) for i in range(size)])


def exchange(value, step):
    size = lax.axis_size("chan")
    return lax.ppermute(value, "chan", [(i, i ^ step) for i in range(size)])


def swap_cores(value):
    size = lax.axis_size("morton")
    return lax.ppermute(value, "morton", [(i, i ^ 1) for i in range(size)])


def local_step(features, conv_weight, coarse_weight, out_grad, send_block, send_count, neighbour):
    n_morton = lax.axis_size("morton")
    quarter, row_count = features.shape
    channels = conv_weight.shape[2]
    nblocks = row_count // BLOCK
    extent = nblocks + n_morton
    depth = TERMS * quarter
    flops = 2 * depth * channels * row_count
    place = lax.axis_index("chan").astype(jnp.int32).reshape(1)
    core = (lax.axis_index("morton") % 2).astype(jnp.int32).reshape(1)
    shape = jax.ShapeDtypeStruct

    outgoing = call(
        pack_kernel, "pack", shape((n_morton, quarter, BLOCK), BF), "hhh",
        [
            pltpu.SMEM((1, n_morton), jnp.int32),
            pltpu.SMEM((1, n_morton), jnp.int32),
            pltpu.VMEM((quarter, row_count), BF),
            pltpu.SemaphoreType.DMA((3,)),
        ],
        size=1 << 20,
        limit=60 << 20,
    )(send_block, send_count, features)
    incoming = lax.all_to_all(outgoing, "morton", 0, 0, tiled=True)

    half_piece = shape((PAIRS // 2, quarter, BLOCK), BF)
    own_piece, *sent = call(
        split_kernel,
        "split",
        [shape((PAIRS, quarter, BLOCK), BF)] + [half_piece] * 3,
        "ssvv",
        size=2 << 20,
    )(place, core, conv_weight, coarse_weight)
    came = [exchange(value, step) for step, value in zip((1, 2, 3), sent)]
    weights = [own_piece] + came + [swap_cores(value) for value in came]

    table = pltpu.VMEM((extent + 1, quarter, BLOCK), BF)
    wide, piece = (quarter, row_count), (4, quarter // 2, BLOCK)
    grads, outputs = [], []
    widths = [(end - first) * BLOCK for first, end in zip(CUTS, CUTS[1:])]
    partials = call(
        forward_kernel,
        "forward",
        [shape((quarter, w), BF if s else F32) for w in widths for s in range(4)],
        "sss" + "v" * 9,
        [pltpu.VMEM((channels, depth), BF), table, pltpu.VMEM((depth, max(widths)), BF)],
        flops,
        3 << 20,
    )(place, core, neighbour, features, incoming, *weights)
    for index, (first, end) in enumerate(zip(CUTS, CUTS[1:])):
        part = (quarter, widths[index])
        partial = partials[4 * index : 4 * index + 4]
        arrived = [shift(partial[s], -s) for s in (1, 2, 3)]
        last = end == CUTS[-1]
        output, grad = call(
            functools.partial(activation_end_kernel if last else activation_kernel, first),
            f"activation{first}",
            [shape(wide if last else part, BF), shape(part, BF)],
            "vvvvv" + "v" * (len(outputs) if last else 0),
            size=1 << 20,
        )(partial[0], *arrived, out_grad, *(outputs if last else ()))
        outputs.append(output)
        grads.append([grad] + [shift(grad, s) for s in (1, 2, 3)])

    weight_t = call(join_kernel, "join", shape((depth, channels), BF), "ss" + "v" * 7 + "a", size=3 << 20)(
        place, core, *weights, grads[0][0]
    )
    held = ()
    for (first, end), given in zip(zip(CUTS, CUTS[1:]), grads):
        width = (end - first) * BLOCK
        last = end == CUTS[-1]
        kernel = weight_last_kernel if last else weight_more_kernel if held else weight_first_kernel
        sums = [shape((PAIRS,) + piece, F32), shape((PAIRS,) + piece, BF)]
        result = call(
            functools.partial(kernel, first),
            f"weight_grad{first}",
            sums if last else shape((depth, channels), F32),
            "s" * (1 + last) + "v" * (6 + len(held)),
            [table, pltpu.VMEM((depth, width), BF), pltpu.VMEM((width, channels), BF)],
            flops * width // row_count,
            4 << 20,
        )(*((core,) if last else ()), neighbour, features, incoming, *given, *held)
        held = (result,)
    keep, give = result
    output = outputs[-1]
    chips = n_morton // 2
    parts = call(pair_kernel, "pair_sum", shape((chips,) + piece, BF), "svv", size=3 << 20)(
        place, keep, swap_cores(give)
    )
    same_core = [[2 * c + side for c in range(chips)] for side in range(2)]
    same_core_all = [[device * 4 + z for device in group for z in range(4)] for group in same_core]
    received = lax.all_to_all(
        parts.reshape((4 * chips,) + piece[1:]),
        ("morton", "chan"),
        0,
        0,
        axis_index_groups=same_core_all,
        tiled=True,
    ).reshape(parts.shape)

    blocks = (chips, quarter, BLOCK)
    local, home, away = call(
        table_kernel,
        "table_grad",
        [shape(wide, F32), shape(blocks, BF), shape(blocks, BF)],
        "ssv" + "v" * 4 * len(grads) + "a",
        [
            pltpu.VMEM((extent + 1, quarter, BLOCK), F32),
            pltpu.VMEM((OFFSETS * quarter, 256), F32),
        ],
        flops,
        4 << 20,
    )(core, neighbour, weight_t, *(g for given in grads for g in given), parts)
    scale = float(row_count * n_morton) ** (-0.5)
    mixed = call(
        functools.partial(sum_kernel, scale),
        "sum_parts",
        shape((chips, 8, quarter // 2, BLOCK), BF),
        "vvv",
        size=1 << 20,
    )(received, home, swap_cores(away))
    mine = lax.all_to_all(mixed, "morton", 0, 0, axis_index_groups=same_core, tiled=True)
    input_grad = call(return_kernel, "return_add", shape(wide, F32), "sssvv", size=2 << 20)(
        core, send_block, send_count, local, mine
    )
    conv_grad, coarse_grad = call(
        unpack_kernel,
        "unpack",
        [shape((OFFSETS, quarter, channels), F32), shape((quarter, channels), F32)],
        "svv",
        size=3 << 20,
    )(core, mine, swap_cores(mine))
    return output, input_grad, conv_grad, coarse_grad


def solution(mesh):
    placed = (
        P("chan", "morton"),
        P(None, "chan", None),
        P("chan", None),
        P("chan", "morton"),
        P("morton", None),
        P("morton", None),
        P(None, "morton"),
    )
    return jax.shard_map(
        local_step,
        mesh=mesh,
        in_specs=placed,
        out_specs=(
            P("chan", "morton"),
            P("chan", "morton"),
            P(None, "chan", None),
            P("chan", None),
        ),
        check_vma=False,
    )
```

```python
import functools

import jax
import jax.numpy as jnp
from jax import lax
from jax.experimental import pallas as pl
from jax.experimental.pallas import tpu as pltpu
from jax.sharding import PartitionSpec as P

OFFSETS = 27
TERMS = 28
PAIRS = TERMS // 2
BLOCK = 128
CUTS = (0, 8, 16)
BF = jnp.bfloat16
F32 = jnp.float32


def call(kernel, name, outs, kinds, scratch=(), flops=0, size=0, limit=24 << 20):
    space = {"s": pltpu.SMEM, "v": pltpu.VMEM, "a": pl.ANY, "h": pltpu.HBM}
    many = isinstance(outs, (list, tuple))
    spec = pl.BlockSpec(memory_space=pltpu.VMEM)
    return pl.pallas_call(
        kernel,
        name=name,
        out_shape=outs,
        in_specs=[pl.BlockSpec(memory_space=space[k]) for k in kinds],
        out_specs=[spec] * len(outs) if many else spec,
        scratch_shapes=list(scratch),
        compiler_params=pltpu.CompilerParams(vmem_limit_bytes=limit),
        cost_estimate=pl.CostEstimate(flops=flops, bytes_accessed=size, transcendentals=0),
    )


def mean_matrix():
    row = lax.broadcasted_iota(jnp.int32, (BLOCK, BLOCK), 0) // 8
    column = lax.broadcasted_iota(jnp.int32, (BLOCK, BLOCK), 1) // 8
    return jnp.where(row == column, 0.125, 0.0).astype(BF)


def columns(index):
    return pl.ds(pl.multiple_of(index * BLOCK, BLOCK), BLOCK)


def pack_kernel(block_hbm, count_hbm, features_hbm, outgoing, send_block, send_count, features, sems):
    copies = [
        pltpu.make_async_copy(block_hbm, send_block, sems.at[0]),
        pltpu.make_async_copy(count_hbm, send_count, sems.at[1]),
        pltpu.make_async_copy(features_hbm, features, sems.at[2]),
    ]
    for copy in copies:
        copy.start()
    for copy in copies:
        copy.wait()
    for peer in range(outgoing.shape[0]):
        block = features[:, columns(send_block[0, peer])]
        outgoing[peer] = block * send_count[0, peer].astype(F32).astype(BF)


def split_kernel(place, core, conv_weight, coarse_weight, own, sent1, sent2, sent3):
    quarter = conv_weight.shape[1]
    cuts = [slice(t * quarter, (t + 1) * quarter) for t in range(4)]

    def tiles_of(pair):
        first = conv_weight[2 * pair]
        second = conv_weight[2 * pair + 1] if 2 * pair + 1 < OFFSETS else coarse_weight[...]
        return [jnp.concatenate([first[:, c], second[:, c]], axis=1) for c in cuts]

    def pick(tiles, target):
        low = jnp.where(target == 0, tiles[0], tiles[1])
        high = jnp.where(target == 2, tiles[2], tiles[3])
        return jnp.where(target < 2, low, high)

    half = PAIRS // 2
    for pair in range(half):
        low, high = tiles_of(pair), tiles_of(pair + half)
        own[pair] = pick(low, place[0])
        own[pair + half] = pick(high, place[0])
        mine = [jnp.where(core[0] == 0, a, b) for a, b in zip(low, high)]
        for step, sent in enumerate((sent1, sent2, sent3)):
            sent[pair] = pick(mine, place[0] ^ (step + 1))


def weight_tiles(place, core, pieces, pair):
    half = PAIRS // 2
    local = core[0] == pair // half
    own = pieces[0][pair]
    first, second, third = (
        jnp.where(local, pieces[s][pair % half], pieces[s + 3][pair % half]) for s in (1, 2, 3)
    )
    odd = place[0] % 2 == 1
    return own, jnp.where(odd, first, third), second, jnp.where(odd, third, first)


def join_kernel(place, core, *refs):
    flipped = refs[-1]
    for pair in range(PAIRS):
        tile = jnp.concatenate(weight_tiles(place, core, refs[:7], pair), axis=0)
        flipped[pair * BLOCK : (pair + 1) * BLOCK, :] = tile.T


def fill_table(features, incoming, table, nblocks):
    for block in range(nblocks):
        table[block] = features[:, block * BLOCK : (block + 1) * BLOCK]
    table[nblocks : nblocks + incoming.shape[0]] = incoming[...]
    table[nblocks + incoming.shape[0]] = jnp.zeros(table.shape[1:], BF)


def slot(neighbour, offset, block, extent):
    named = neighbour[offset, block]
    return jnp.where(named < 0, extent, named)


def gather(neighbour, table, gathered, first, blocks, offsets):
    quarter = table.shape[1]
    extent = table.shape[0] - 1
    for offset in offsets:
        rows = slice(offset * quarter, (offset + 1) * quarter)
        for block in blocks:
            cut = slice(block * BLOCK, (block + 1) * BLOCK)
            if offset < OFFSETS:
                gathered[rows, cut] = table[slot(neighbour, offset, first + block, extent)]
            else:
                pooled = jnp.dot(table[first + block], mean_matrix(), preferred_element_type=F32)
                gathered[rows, cut] = pooled.astype(BF)


def forward_kernel(place, core, neighbour, features, incoming, *refs):
    pieces, outs, (weight, table, gathered) = refs[:7], refs[7:-3], refs[-3:]
    quarter, row_count = features.shape
    nblocks = row_count // BLOCK
    for pair in range(PAIRS):
        for step, tile in enumerate(weight_tiles(place, core, pieces, pair)):
            rows = slice(step * quarter, (step + 1) * quarter)
            weight[rows, pair * BLOCK : (pair + 1) * BLOCK] = tile
    fill_table(features, incoming, table, nblocks)
    for tile in range(nblocks // 2):
        if tile == 0:
            gather(neighbour, table, gathered, 0, range(2), range(TERMS))
        if tile < nblocks // 2 - 1:
            ahead = range(2 * tile + 2, 2 * tile + 4)
            gather(neighbour, table, gathered, 0, ahead, range(TERMS))
        read = slice(tile * 256, (tile + 1) * 256)
        total = jnp.dot(weight[...], gathered[:, read], preferred_element_type=F32)
        part = sum(2 * tile >= cut for cut in CUTS[1:])
        start = (2 * tile - CUTS[part]) * BLOCK
        for step, out in enumerate(outs[4 * part : 4 * part + 4]):
            value = total[step * quarter : (step + 1) * quarter]
            out[:, start : start + 256] = value.astype(out.dtype)


def activate(own, part1, part2, part3, out_grad):
    pre = (own[...] + part1[...].astype(F32)) + (part2[...].astype(F32) + part3[...].astype(F32))
    sigma = 1.0 / (1.0 + jnp.exp(-pre))
    grad = out_grad.astype(F32) * sigma * (1.0 + pre * (1.0 - sigma))
    return (pre * sigma).astype(BF), grad.astype(BF)


def activation_kernel(first, own, part1, part2, part3, out_grad, output, grad):
    cut = slice(first * BLOCK, first * BLOCK + own.shape[1])
    output[...], grad[...] = activate(own, part1, part2, part3, out_grad[:, cut])


def activation_end_kernel(first, own, part1, part2, part3, out_grad, *refs):
    output, grad = refs[-2:]
    start = 0
    for before in refs[:-2]:
        output[:, start : start + before.shape[1]] = before[...]
        start += before.shape[1]
    cut = slice(first * BLOCK, first * BLOCK + own.shape[1])
    output[:, cut], grad[...] = activate(own, part1, part2, part3, out_grad[:, cut])


def weight_products(first, neighbour, features, incoming, grads, table, gathered, flipped):
    nblocks = features.shape[1] // BLOCK
    blocks = range(gathered.shape[1] // BLOCK)
    fill_table(features, incoming, table, nblocks)
    for block in blocks:
        cut = slice(block * BLOCK, (block + 1) * BLOCK)
        tall = jnp.concatenate([g[:, cut] for g in grads], axis=0)
        flipped[cut, :] = tall.T
    for pair in range(PAIRS):
        if pair == 0:
            gather(neighbour, table, gathered, first, blocks, range(2))
        if pair < PAIRS - 1:
            gather(neighbour, table, gathered, first, blocks, range(2 * pair + 2, 2 * pair + 4))
        rows = slice(pair * BLOCK, (pair + 1) * BLOCK)
        yield pair, rows, jnp.dot(gathered[rows, :], flipped[...], preferred_element_type=F32)


def weight_first_kernel(
    first, neighbour, features, incoming, grad0, grad1, grad2, grad3, held, table, gathered, flipped
):
    grads = (grad0, grad1, grad2, grad3)
    for _, rows, product in weight_products(
        first, neighbour, features, incoming, grads, table, gathered, flipped
    ):
        held[rows, :] = product


def weight_last_kernel(
    first, core, neighbour, features, incoming, grad0, grad1, grad2, grad3, held, keep, give, table, gathered, flipped
):
    quarter = features.shape[0]
    half = quarter // 2
    grads = (grad0, grad1, grad2, grad3)
    for pair, rows, product in weight_products(
        first, neighbour, features, incoming, grads, table, gathered, flipped
    ):
        upright = (product + held[rows, :]).T
        for step in range(4):
            low = upright[step * quarter : step * quarter + half]
            high = upright[step * quarter + half : (step + 1) * quarter]
            keep[pair, step] = jnp.where(core[0] == 0, low, high)
            give[pair, step] = jnp.where(core[0] == 0, high, low).astype(BF)


def pair_kernel(place, keep, arrived, parts):
    for step in range(4):
        target = lax.rem(place[0] - step + 4, 4)
        for pair in range(PAIRS):
            parts[pair, target] = (keep[pair, step] + arrived[pair, step].astype(F32)).astype(BF)
    for spare in range(PAIRS, parts.shape[0]):
        parts[spare] = jnp.zeros(parts.shape[1:], BF)


def table_kernel(core, neighbour, weight_t, *refs):
    local, home, away, total, spread = refs[-5:]
    grads = refs[: 4 * (len(CUTS) - 1)]
    quarter, row_count = local.shape
    nblocks = row_count // BLOCK
    extent = total.shape[0] - 1
    total[...] = jnp.zeros_like(total)
    mean = mean_matrix()
    for tile in range(nblocks // 2):
        part = sum(2 * tile >= cut for cut in CUTS[1:])
        start = (2 * tile - CUTS[part]) * BLOCK
        tall = jnp.concatenate(
            [g[:, start : start + 256] for g in grads[4 * part : 4 * part + 4]], axis=0
        )
        product = jnp.dot(weight_t[...], tall, preferred_element_type=F32)
        spread[...] = product[: OFFSETS * quarter]

        def step(offset, carry, tile=tile):
            rows = pl.ds(pl.multiple_of(offset * quarter, quarter), quarter)
            for side in range(2):
                place = slot(neighbour, offset, 2 * tile + side, extent)
                total[place] += spread[rows, side * BLOCK : (side + 1) * BLOCK]
            return carry

        lax.fori_loop(0, OFFSETS, step, 0, unroll=27)
        coarse = product[OFFSETS * quarter :]
        for side in range(2):
            value = coarse[:, side * BLOCK : (side + 1) * BLOCK]
            high = value.astype(BF)
            low = (value - high.astype(F32)).astype(BF)
            total[2 * tile + side] += jnp.dot(high, mean, preferred_element_type=F32) + jnp.dot(
                low, mean, preferred_element_type=F32
            )
    for block in range(nblocks):
        local[:, block * BLOCK : (block + 1) * BLOCK] = total[block]
    for chip in range(home.shape[0]):
        home[chip] = total[nblocks + 2 * chip + core[0]].astype(BF)
        away[chip] = total[nblocks + 2 * chip + 1 - core[0]].astype(BF)


def return_kernel(core, send_block, send_count, local, mixed, input_grad):
    input_grad[...] = local[...]
    for chip in range(mixed.shape[0]):
        for flip in range(2):
            peer = 2 * chip + (1 - core[0] if flip else core[0])
            value = jnp.concatenate([mixed[chip, 4 + 2 * flip], mixed[chip, 5 + 2 * flip]], axis=0)
            factor = send_count[0, peer].astype(F32)
            input_grad[:, columns(send_block[0, peer])] += value.astype(F32) * factor


def sum_kernel(scale, parts, home, away, mixed):
    half = parts.shape[3] // 2
    rows = parts.shape[2]
    total = parts[0].astype(F32)
    for source in range(1, parts.shape[0]):
        total = total + parts[source].astype(F32)
    total = total * scale
    for side in range(2):
        cut = slice(side * half, (side + 1) * half)
        for pair in range(2):
            value = jnp.concatenate([total[2 * pair + c, :, cut] for c in range(2)], axis=1)
            for target in range(mixed.shape[0]):
                mixed[target, 2 * side + pair] = value.astype(BF)
    for target in range(mixed.shape[0]):
        for flip, blocks in enumerate((home, away)):
            for part in range(2):
                mixed[target, 4 + 2 * flip + part] = blocks[target, part * rows : (part + 1) * rows]


def unpack_kernel(core, mine, other, conv_grad, coarse_grad):
    half = mine.shape[2]
    for mixed, side in ((mine, core[0]), (other, 1 - core[0])):
        rows = pl.ds(pl.multiple_of(side * half, half), half)
        for offset in range(TERMS):
            for pair in range(2):
                value = mixed[offset // 2, 2 * (offset % 2) + pair].astype(F32)
                cut = slice(pair * BLOCK, (pair + 1) * BLOCK)
                if offset < OFFSETS:
                    conv_grad[offset, rows, cut] = value
                else:
                    coarse_grad[rows, cut] = value


def shift(value, step):
    size = lax.axis_size("chan")
    return lax.ppermute(value, "chan", [(i, (i + step) % size) for i in range(size)])


def exchange(value, step):
    size = lax.axis_size("chan")
    return lax.ppermute(value, "chan", [(i, i ^ step) for i in range(size)])


def swap_cores(value):
    size = lax.axis_size("morton")
    return lax.ppermute(value, "morton", [(i, i ^ 1) for i in range(size)])


def local_step(features, conv_weight, coarse_weight, out_grad, send_block, send_count, neighbour):
    n_morton = lax.axis_size("morton")
    quarter, row_count = features.shape
    channels = conv_weight.shape[2]
    nblocks = row_count // BLOCK
    extent = nblocks + n_morton
    depth = TERMS * quarter
    flops = 2 * depth * channels * row_count
    place = lax.axis_index("chan").astype(jnp.int32).reshape(1)
    core = (lax.axis_index("morton") % 2).astype(jnp.int32).reshape(1)
    shape = jax.ShapeDtypeStruct

    outgoing = call(
        pack_kernel, "pack", shape((n_morton, quarter, BLOCK), BF), "hhh",
        [
            pltpu.SMEM((1, n_morton), jnp.int32),
            pltpu.SMEM((1, n_morton), jnp.int32),
            pltpu.VMEM((quarter, row_count), BF),
            pltpu.SemaphoreType.DMA((3,)),
        ],
        size=1 << 20,
        limit=60 << 20,
    )(send_block, send_count, features)
    incoming = lax.all_to_all(outgoing, "morton", 0, 0, tiled=True)

    half_piece = shape((PAIRS // 2, quarter, BLOCK), BF)
    own_piece, *sent = call(
        split_kernel,
        "split",
        [shape((PAIRS, quarter, BLOCK), BF)] + [half_piece] * 3,
        "ssvv",
        size=2 << 20,
    )(place, core, conv_weight, coarse_weight)
    came = [exchange(value, step) for step, value in zip((1, 2, 3), sent)]
    weights = [own_piece] + came + [swap_cores(value) for value in came]

    table = pltpu.VMEM((extent + 1, quarter, BLOCK), BF)
    wide, piece = (quarter, row_count), (4, quarter // 2, BLOCK)
    grads, outputs = [], []
    widths = [(end - first) * BLOCK for first, end in zip(CUTS, CUTS[1:])]
    partials = call(
        forward_kernel,
        "forward",
        [shape((quarter, w), BF if s else F32) for w in widths for s in range(4)],
        "sss" + "v" * 9,
        [pltpu.VMEM((channels, depth), BF), table, pltpu.VMEM((depth, row_count), BF)],
        flops,
        3 << 20,
    )(place, core, neighbour, features, incoming, *weights)
    for index, (first, end) in enumerate(zip(CUTS, CUTS[1:])):
        part = (quarter, widths[index])
        partial = partials[4 * index : 4 * index + 4]
        arrived = [shift(partial[s], -s) for s in (1, 2, 3)]
        last = end == CUTS[-1]
        output, grad = call(
            functools.partial(activation_end_kernel if last else activation_kernel, first),
            f"activation{first}",
            [shape(wide if last else part, BF), shape(part, BF)],
            "vvvvv" + "v" * (len(outputs) if last else 0),
            size=1 << 20,
        )(partial[0], *arrived, out_grad, *(outputs if last else ()))
        outputs.append(output)
        grads.append([grad] + [shift(grad, s) for s in (1, 2, 3)])

    weight_t = call(join_kernel, "join", shape((depth, channels), BF), "ss" + "v" * 7 + "a", size=3 << 20)(
        place, core, *weights, grads[0][0]
    )
    held = ()
    for (first, end), given in zip(zip(CUTS, CUTS[1:]), grads):
        width = (end - first) * BLOCK
        last = end == CUTS[-1]
        kernel = weight_last_kernel if last else weight_first_kernel
        sums = [shape((PAIRS,) + piece, F32), shape((PAIRS,) + piece, BF)]
        result = call(
            functools.partial(kernel, first),
            f"weight_grad{first}",
            sums if last else shape((depth, channels), F32),
            "s" * (1 + last) + "v" * (6 + len(held)),
            [table, pltpu.VMEM((depth, width), BF), pltpu.VMEM((width, channels), BF)],
            flops * width // row_count,
            4 << 20,
        )(*((core,) if last else ()), neighbour, features, incoming, *given, *held)
        held = (result,)
    keep, give = result
    output = outputs[-1]
    chips = n_morton // 2
    parts = call(pair_kernel, "pair_sum", shape((chips,) + piece, BF), "svv", size=3 << 20)(
        place, keep, swap_cores(give)
    )
    same_core = [[2 * c + side for c in range(chips)] for side in range(2)]
    same_core_all = [[device * 4 + z for device in group for z in range(4)] for group in same_core]
    received = lax.all_to_all(
        parts.reshape((4 * chips,) + piece[1:]),
        ("morton", "chan"),
        0,
        0,
        axis_index_groups=same_core_all,
        tiled=True,
    ).reshape(parts.shape)

    blocks = (chips, quarter, BLOCK)
    local, home, away = call(
        table_kernel,
        "table_grad",
        [shape(wide, F32), shape(blocks, BF), shape(blocks, BF)],
        "ssv" + "v" * 4 * len(grads) + "a",
        [
            pltpu.VMEM((extent + 1, quarter, BLOCK), F32),
            pltpu.VMEM((OFFSETS * quarter, 256), F32),
        ],
        flops,
        4 << 20,
    )(core, neighbour, weight_t, *(g for given in grads for g in given), parts)
    scale = float(row_count * n_morton) ** (-0.5)
    mixed = call(
        functools.partial(sum_kernel, scale),
        "sum_parts",
        shape((chips, 8, quarter // 2, BLOCK), BF),
        "vvv",
        size=1 << 20,
    )(received, home, swap_cores(away))
    mine = lax.all_to_all(mixed, "morton", 0, 0, axis_index_groups=same_core, tiled=True)
    input_grad = call(return_kernel, "return_add", shape(wide, F32), "sssvv", size=2 << 20)(
        core, send_block, send_count, local, mine
    )
    conv_grad, coarse_grad = call(
        unpack_kernel,
        "unpack",
        [shape((OFFSETS, quarter, channels), F32), shape((quarter, channels), F32)],
        "svv",
        size=3 << 20,
    )(core, mine, swap_cores(mine))
    return output, input_grad, conv_grad, coarse_grad


def solution(mesh):
    placed = (
        P("chan", "morton"),
        P(None, "chan", None),
        P("chan", None),
        P("chan", "morton"),
        P("morton", None),
        P("morton", None),
        P(None, "morton"),
    )
    return jax.shard_map(
        local_step,
        mesh=mesh,
        in_specs=placed,
        out_specs=(
            P("chan", "morton"),
            P("chan", "morton"),
            P(None, "chan", None),
            P("chan", None),
        ),
        check_vma=False,
    )
```

```python
import functools

import jax
import jax.numpy as jnp
from jax import lax
from jax.experimental import pallas as pl
from jax.experimental.pallas import tpu as pltpu
from jax.sharding import PartitionSpec as P

OFFSETS = 27
TERMS = 28
PAIRS = TERMS // 2
BLOCK = 128
CUTS = (0, 8, 16)
BF = jnp.bfloat16
F32 = jnp.float32


def call(kernel, name, outs, kinds, scratch=(), flops=0, size=0, limit=24 << 20, space_out=pltpu.VMEM):
    space = {"s": pltpu.SMEM, "v": pltpu.VMEM, "a": pl.ANY, "h": pltpu.HBM}
    many = isinstance(outs, (list, tuple))
    spec = pl.BlockSpec(memory_space=space_out)
    return pl.pallas_call(
        kernel,
        name=name,
        out_shape=outs,
        in_specs=[pl.BlockSpec(memory_space=space[k]) for k in kinds],
        out_specs=[spec] * len(outs) if many else spec,
        scratch_shapes=list(scratch),
        compiler_params=pltpu.CompilerParams(vmem_limit_bytes=limit),
        cost_estimate=pl.CostEstimate(flops=flops, bytes_accessed=size, transcendentals=0),
    )


def mean_matrix():
    row = lax.broadcasted_iota(jnp.int32, (BLOCK, BLOCK), 0) // 8
    column = lax.broadcasted_iota(jnp.int32, (BLOCK, BLOCK), 1) // 8
    return jnp.where(row == column, 0.125, 0.0).astype(BF)


def columns(index):
    return pl.ds(pl.multiple_of(index * BLOCK, BLOCK), BLOCK)


def pack_kernel(block_hbm, count_hbm, features_hbm, out_hbm, send_block, send_count, features, outgoing, sems, out_sems):
    copies = [
        pltpu.make_async_copy(block_hbm, send_block, sems.at[0]),
        pltpu.make_async_copy(count_hbm, send_count, sems.at[1]),
        pltpu.make_async_copy(features_hbm, features, sems.at[2]),
    ]
    for copy in copies:
        copy.start()
    for copy in copies:
        copy.wait()
    groups = out_sems.shape[0]
    size = outgoing.shape[0] // groups
    sent = []
    for group in range(groups):
        for peer in range(group * size, (group + 1) * size):
            block = features[:, columns(send_block[0, peer])]
            outgoing[peer] = block * send_count[0, peer].astype(F32).astype(BF)
        part = pl.ds(group * size, size)
        sent.append(pltpu.make_async_copy(outgoing.at[part], out_hbm.at[part], out_sems.at[group]))
        sent[-1].start()
    for copy in sent:
        copy.wait()


def split_kernel(place, core, conv_weight, coarse_weight, own, sent1, sent2, sent3):
    quarter = conv_weight.shape[1]
    cuts = [slice(t * quarter, (t + 1) * quarter) for t in range(4)]

    def tiles_of(pair):
        first = conv_weight[2 * pair]
        second = conv_weight[2 * pair + 1] if 2 * pair + 1 < OFFSETS else coarse_weight[...]
        return [jnp.concatenate([first[:, c], second[:, c]], axis=1) for c in cuts]

    def pick(tiles, target):
        low = jnp.where(target == 0, tiles[0], tiles[1])
        high = jnp.where(target == 2, tiles[2], tiles[3])
        return jnp.where(target < 2, low, high)

    half = PAIRS // 2
    for pair in range(half):
        low, high = tiles_of(pair), tiles_of(pair + half)
        own[pair] = pick(low, place[0])
        own[pair + half] = pick(high, place[0])
        mine = [jnp.where(core[0] == 0, a, b) for a, b in zip(low, high)]
        for step, sent in enumerate((sent1, sent2, sent3)):
            sent[pair] = pick(mine, place[0] ^ (step + 1))


def weight_tiles(place, core, pieces, pair):
    half = PAIRS // 2
    local = core[0] == pair // half
    own = pieces[0][pair]
    first, second, third = (
        jnp.where(local, pieces[s][pair % half], pieces[s + 3][pair % half]) for s in (1, 2, 3)
    )
    odd = place[0] % 2 == 1
    return own, jnp.where(odd, first, third), second, jnp.where(odd, third, first)


def join_kernel(place, core, *refs):
    flipped = refs[-1]
    for pair in range(PAIRS):
        tile = jnp.concatenate(weight_tiles(place, core, refs[:7], pair), axis=0)
        flipped[pair * BLOCK : (pair + 1) * BLOCK, :] = tile.T


def fill_table(features, incoming, table, nblocks):
    for block in range(nblocks):
        table[block] = features[:, block * BLOCK : (block + 1) * BLOCK]
    table[nblocks : nblocks + incoming.shape[0]] = incoming[...]
    table[nblocks + incoming.shape[0]] = jnp.zeros(table.shape[1:], BF)


def slot(neighbour, offset, block, extent):
    named = neighbour[offset, block]
    return jnp.where(named < 0, extent, named)


def gather(neighbour, table, gathered, first, blocks, offsets):
    quarter = table.shape[1]
    extent = table.shape[0] - 1
    for offset in offsets:
        rows = slice(offset * quarter, (offset + 1) * quarter)
        for block in blocks:
            cut = slice(block * BLOCK, (block + 1) * BLOCK)
            if offset < OFFSETS:
                gathered[rows, cut] = table[slot(neighbour, offset, first + block, extent)]
            else:
                pooled = jnp.dot(table[first + block], mean_matrix(), preferred_element_type=F32)
                gathered[rows, cut] = pooled.astype(BF)


def forward_kernel(place, core, neighbour, features, incoming, *refs):
    pieces, outs, (weight, table, gathered) = refs[:7], refs[7:-3], refs[-3:]
    quarter, row_count = features.shape
    nblocks = row_count // BLOCK
    for pair in range(PAIRS):
        for step, tile in enumerate(weight_tiles(place, core, pieces, pair)):
            rows = slice(step * quarter, (step + 1) * quarter)
            weight[rows, pair * BLOCK : (pair + 1) * BLOCK] = tile
    fill_table(features, incoming, table, nblocks)
    for tile in range(nblocks // 2):
        if tile == 0:
            gather(neighbour, table, gathered, 0, range(2), range(TERMS))
        if tile < nblocks // 2 - 1:
            ahead = range(2 * tile + 2, 2 * tile + 4)
            gather(neighbour, table, gathered, 0, ahead, range(TERMS))
        read = slice(tile * 256, (tile + 1) * 256)
        total = jnp.dot(weight[...], gathered[:, read], preferred_element_type=F32)
        part = sum(2 * tile >= cut for cut in CUTS[1:])
        start = (2 * tile - CUTS[part]) * BLOCK
        for step, out in enumerate(outs[4 * part : 4 * part + 4]):
            value = total[step * quarter : (step + 1) * quarter]
            out[:, start : start + 256] = value.astype(out.dtype)


def activate(own, part1, part2, part3, out_grad):
    pre = (own[...] + part1[...].astype(F32)) + (part2[...].astype(F32) + part3[...].astype(F32))
    sigma = 1.0 / (1.0 + jnp.exp(-pre))
    grad = out_grad.astype(F32) * sigma * (1.0 + pre * (1.0 - sigma))
    return (pre * sigma).astype(BF), grad.astype(BF)


def activation_kernel(first, own, part1, part2, part3, out_grad, output, grad):
    cut = slice(first * BLOCK, first * BLOCK + own.shape[1])
    output[...], grad[...] = activate(own, part1, part2, part3, out_grad[:, cut])


def activation_end_kernel(first, own, part1, part2, part3, out_grad, *refs):
    output, grad = refs[-2:]
    start = 0
    for before in refs[:-2]:
        output[:, start : start + before.shape[1]] = before[...]
        start += before.shape[1]
    cut = slice(first * BLOCK, first * BLOCK + own.shape[1])
    output[:, cut], grad[...] = activate(own, part1, part2, part3, out_grad[:, cut])


def weight_products(first, neighbour, features, incoming, grads, table, gathered, flipped):
    nblocks = features.shape[1] // BLOCK
    blocks = range(gathered.shape[1] // BLOCK)
    fill_table(features, incoming, table, nblocks)
    for block in blocks:
        cut = slice(block * BLOCK, (block + 1) * BLOCK)
        tall = jnp.concatenate([g[:, cut] for g in grads], axis=0)
        flipped[cut, :] = tall.T
    for pair in range(PAIRS):
        if pair == 0:
            gather(neighbour, table, gathered, first, blocks, range(2))
        if pair < PAIRS - 1:
            gather(neighbour, table, gathered, first, blocks, range(2 * pair + 2, 2 * pair + 4))
        rows = slice(pair * BLOCK, (pair + 1) * BLOCK)
        yield pair, rows, jnp.dot(gathered[rows, :], flipped[...], preferred_element_type=F32)


def weight_first_kernel(
    first, neighbour, features, incoming, grad0, grad1, grad2, grad3, held, table, gathered, flipped
):
    grads = (grad0, grad1, grad2, grad3)
    for _, rows, product in weight_products(
        first, neighbour, features, incoming, grads, table, gathered, flipped
    ):
        held[rows, :] = product


def weight_last_kernel(
    first, core, neighbour, features, incoming, grad0, grad1, grad2, grad3, held, keep, give, table, gathered, flipped
):
    quarter = features.shape[0]
    half = quarter // 2
    grads = (grad0, grad1, grad2, grad3)
    for pair, rows, product in weight_products(
        first, neighbour, features, incoming, grads, table, gathered, flipped
    ):
        upright = (product + held[rows, :]).T
        for step in range(4):
            low = upright[step * quarter : step * quarter + half]
            high = upright[step * quarter + half : (step + 1) * quarter]
            keep[pair, step] = jnp.where(core[0] == 0, low, high)
            give[pair, step] = jnp.where(core[0] == 0, high, low).astype(BF)


def pair_kernel(place, keep, arrived, parts):
    for step in range(4):
        target = lax.rem(place[0] - step + 4, 4)
        for pair in range(PAIRS):
            parts[pair, target] = (keep[pair, step] + arrived[pair, step].astype(F32)).astype(BF)
    for spare in range(PAIRS, parts.shape[0]):
        parts[spare] = jnp.zeros(parts.shape[1:], BF)


def table_kernel(core, neighbour, weight_t, *refs):
    local, home, away, total, spread = refs[-5:]
    grads = refs[: 4 * (len(CUTS) - 1)]
    quarter, row_count = local.shape
    nblocks = row_count // BLOCK
    extent = total.shape[0] - 1
    total[...] = jnp.zeros_like(total)
    mean = mean_matrix()
    for tile in range(nblocks // 2):
        part = sum(2 * tile >= cut for cut in CUTS[1:])
        start = (2 * tile - CUTS[part]) * BLOCK
        tall = jnp.concatenate(
            [g[:, start : start + 256] for g in grads[4 * part : 4 * part + 4]], axis=0
        )
        product = jnp.dot(weight_t[...], tall, preferred_element_type=F32)
        spread[...] = product[: OFFSETS * quarter]

        def step(offset, carry, tile=tile):
            rows = pl.ds(pl.multiple_of(offset * quarter, quarter), quarter)
            for side in range(2):
                place = slot(neighbour, offset, 2 * tile + side, extent)
                total[place] += spread[rows, side * BLOCK : (side + 1) * BLOCK]
            return carry

        lax.fori_loop(0, OFFSETS, step, 0, unroll=27)
        coarse = product[OFFSETS * quarter :]
        for side in range(2):
            value = coarse[:, side * BLOCK : (side + 1) * BLOCK]
            high = value.astype(BF)
            low = (value - high.astype(F32)).astype(BF)
            total[2 * tile + side] += jnp.dot(high, mean, preferred_element_type=F32) + jnp.dot(
                low, mean, preferred_element_type=F32
            )
    for block in range(nblocks):
        local[:, block * BLOCK : (block + 1) * BLOCK] = total[block]
    for chip in range(home.shape[0]):
        home[chip] = total[nblocks + 2 * chip + core[0]].astype(BF)
        away[chip] = total[nblocks + 2 * chip + 1 - core[0]].astype(BF)


def return_kernel(core, send_block, send_count, local, mixed, input_grad):
    input_grad[...] = local[...]
    for chip in range(mixed.shape[0]):
        for flip in range(2):
            peer = 2 * chip + (1 - core[0] if flip else core[0])
            value = jnp.concatenate([mixed[chip, 4 + 2 * flip], mixed[chip, 5 + 2 * flip]], axis=0)
            factor = send_count[0, peer].astype(F32)
            input_grad[:, columns(send_block[0, peer])] += value.astype(F32) * factor


def sum_kernel(scale, parts, home, away, mixed):
    half = parts.shape[3] // 2
    rows = parts.shape[2]
    total = parts[0].astype(F32)
    for source in range(1, parts.shape[0]):
        total = total + parts[source].astype(F32)
    total = total * scale
    for side in range(2):
        cut = slice(side * half, (side + 1) * half)
        for pair in range(2):
            value = jnp.concatenate([total[2 * pair + c, :, cut] for c in range(2)], axis=1)
            for target in range(mixed.shape[0]):
                mixed[target, 2 * side + pair] = value.astype(BF)
    for target in range(mixed.shape[0]):
        for flip, blocks in enumerate((home, away)):
            for part in range(2):
                mixed[target, 4 + 2 * flip + part] = blocks[target, part * rows : (part + 1) * rows]


def unpack_kernel(core, mine, other, conv_grad, coarse_grad):
    half = mine.shape[2]
    for mixed, side in ((mine, core[0]), (other, 1 - core[0])):
        rows = pl.ds(pl.multiple_of(side * half, half), half)
        for offset in range(TERMS):
            for pair in range(2):
                value = mixed[offset // 2, 2 * (offset % 2) + pair].astype(F32)
                cut = slice(pair * BLOCK, (pair + 1) * BLOCK)
                if offset < OFFSETS:
                    conv_grad[offset, rows, cut] = value
                else:
                    coarse_grad[rows, cut] = value


def shift(value, step):
    size = lax.axis_size("chan")
    return lax.ppermute(value, "chan", [(i, (i + step) % size) for i in range(size)])


def exchange(value, step):
    size = lax.axis_size("chan")
    return lax.ppermute(value, "chan", [(i, i ^ step) for i in range(size)])


def swap_cores(value):
    size = lax.axis_size("morton")
    return lax.ppermute(value, "morton", [(i, i ^ 1) for i in range(size)])


def local_step(features, conv_weight, coarse_weight, out_grad, send_block, send_count, neighbour):
    n_morton = lax.axis_size("morton")
    quarter, row_count = features.shape
    channels = conv_weight.shape[2]
    nblocks = row_count // BLOCK
    extent = nblocks + n_morton
    depth = TERMS * quarter
    flops = 2 * depth * channels * row_count
    place = lax.axis_index("chan").astype(jnp.int32).reshape(1)
    core = (lax.axis_index("morton") % 2).astype(jnp.int32).reshape(1)
    shape = jax.ShapeDtypeStruct

    outgoing = call(
        pack_kernel, "pack", shape((n_morton, quarter, BLOCK), BF), "hhh",
        [
            pltpu.SMEM((1, n_morton), jnp.int32),
            pltpu.SMEM((1, n_morton), jnp.int32),
            pltpu.VMEM((quarter, row_count), BF),
            pltpu.VMEM((n_morton, quarter, BLOCK), BF),
            pltpu.SemaphoreType.DMA((3,)),
            pltpu.SemaphoreType.DMA((4,)),
        ],
        size=1 << 20,
        limit=60 << 20,
        space_out=pltpu.HBM,
    )(send_block, send_count, features)
    incoming = lax.all_to_all(outgoing, "morton", 0, 0, tiled=True)

    half_piece = shape((PAIRS // 2, quarter, BLOCK), BF)
    own_piece, *sent = call(
        split_kernel,
        "split",
        [shape((PAIRS, quarter, BLOCK), BF)] + [half_piece] * 3,
        "ssvv",
        size=2 << 20,
    )(place, core, conv_weight, coarse_weight)
    came = [exchange(value, step) for step, value in zip((1, 2, 3), sent)]
    weights = [own_piece] + came + [swap_cores(value) for value in came]

    table = pltpu.VMEM((extent + 1, quarter, BLOCK), BF)
    wide, piece = (quarter, row_count), (4, quarter // 2, BLOCK)
    grads, outputs = [], []
    widths = [(end - first) * BLOCK for first, end in zip(CUTS, CUTS[1:])]
    partials = call(
        forward_kernel,
        "forward",
        [shape((quarter, w), BF if s else F32) for w in widths for s in range(4)],
        "sss" + "v" * 9,
        [pltpu.VMEM((channels, depth), BF), table, pltpu.VMEM((depth, row_count), BF)],
        flops,
        3 << 20,
    )(place, core, neighbour, features, incoming, *weights)
    for index, (first, end) in enumerate(zip(CUTS, CUTS[1:])):
        part = (quarter, widths[index])
        partial = partials[4 * index : 4 * index + 4]
        arrived = [shift(partial[s], -s) for s in (1, 2, 3)]
        last = end == CUTS[-1]
        output, grad = call(
            functools.partial(activation_end_kernel if last else activation_kernel, first),
            f"activation{first}",
            [shape(wide if last else part, BF), shape(part, BF)],
            "vvvvv" + "v" * (len(outputs) if last else 0),
            size=1 << 20,
        )(partial[0], *arrived, out_grad, *(outputs if last else ()))
        outputs.append(output)
        grads.append([grad] + [shift(grad, s) for s in (1, 2, 3)])

    weight_t = call(join_kernel, "join", shape((depth, channels), BF), "ss" + "v" * 7 + "a", size=3 << 20)(
        place, core, *weights, grads[0][0]
    )
    held = ()
    for (first, end), given in zip(zip(CUTS, CUTS[1:]), grads):
        width = (end - first) * BLOCK
        last = end == CUTS[-1]
        kernel = weight_last_kernel if last else weight_first_kernel
        sums = [shape((PAIRS,) + piece, F32), shape((PAIRS,) + piece, BF)]
        result = call(
            functools.partial(kernel, first),
            f"weight_grad{first}",
            sums if last else shape((depth, channels), F32),
            "s" * (1 + last) + "v" * (6 + len(held)),
            [table, pltpu.VMEM((depth, width), BF), pltpu.VMEM((width, channels), BF)],
            flops * width // row_count,
            4 << 20,
        )(*((core,) if last else ()), neighbour, features, incoming, *given, *held)
        held = (result,)
    keep, give = result
    output = outputs[-1]
    chips = n_morton // 2
    parts = call(pair_kernel, "pair_sum", shape((chips,) + piece, BF), "svv", size=3 << 20)(
        place, keep, swap_cores(give)
    )
    same_core = [[2 * c + side for c in range(chips)] for side in range(2)]
    same_core_all = [[device * 4 + z for device in group for z in range(4)] for group in same_core]
    received = lax.all_to_all(
        parts.reshape((4 * chips,) + piece[1:]),
        ("morton", "chan"),
        0,
        0,
        axis_index_groups=same_core_all,
        tiled=True,
    ).reshape(parts.shape)

    blocks = (chips, quarter, BLOCK)
    local, home, away = call(
        table_kernel,
        "table_grad",
        [shape(wide, F32), shape(blocks, BF), shape(blocks, BF)],
        "ssv" + "v" * 4 * len(grads) + "a",
        [
            pltpu.VMEM((extent + 1, quarter, BLOCK), F32),
            pltpu.VMEM((OFFSETS * quarter, 256), F32),
        ],
        flops,
        4 << 20,
    )(core, neighbour, weight_t, *(g for given in grads for g in given), parts)
    scale = float(row_count * n_morton) ** (-0.5)
    mixed = call(
        functools.partial(sum_kernel, scale),
        "sum_parts",
        shape((chips, 8, quarter // 2, BLOCK), BF),
        "vvv",
        size=1 << 20,
    )(received, home, swap_cores(away))
    mine = lax.all_to_all(mixed, "morton", 0, 0, axis_index_groups=same_core, tiled=True)
    input_grad = call(return_kernel, "return_add", shape(wide, F32), "sssvv", size=2 << 20)(
        core, send_block, send_count, local, mine
    )
    conv_grad, coarse_grad = call(
        unpack_kernel,
        "unpack",
        [shape((OFFSETS, quarter, channels), F32), shape((quarter, channels), F32)],
        "svv",
        size=3 << 20,
    )(core, mine, swap_cores(mine[:, :4]))
    return output, input_grad, conv_grad, coarse_grad


def solution(mesh):
    placed = (
        P("chan", "morton"),
        P(None, "chan", None),
        P("chan", None),
        P("chan", "morton"),
        P("morton", None),
        P("morton", None),
        P(None, "morton"),
    )
    return jax.shard_map(
        local_step,
        mesh=mesh,
        in_specs=placed,
        out_specs=(
            P("chan", "morton"),
            P("chan", "morton"),
            P(None, "chan", None),
            P("chan", None),
        ),
        check_vma=False,
    )
```
